32 devices in a mesh: dp: 4 (over z), zero: 8 (over y, x, core).
Axes of the slice: x: 2, y: 2, z: 4, core: 2. Of those that a mesh axis runs over, the one named last changes fastest.
Arguments:
- tokens: bfloat16 [64, 1024, 256], P(('dp', 'zero')), may hold values from -6 to 6
- counts: int32 [64], P(('dp', 'zero')), may hold values from 256 to 1024, as said below
- key_mask: int32 [64, 1024], P(('dp', 'zero')), may hold values 0 or 1
- rotation: int32 [64], P(('dp', 'zero')), may hold values from 0 to 3
- token_order: int32 [64, 1024], P(('dp', 'zero')), may hold values from 0 to 1023, each once within a row
- query_weight: bfloat16 [256, 256], P('zero'), may hold values from -0.375 to 0.375
- key_weight: bfloat16 [256, 256], P('zero'), may hold values from -0.375 to 0.375
- value_weight: bfloat16 [256, 256], P('zero'), may hold values from -0.375 to 0.375
- out_weight: bfloat16 [256, 256], P('zero'), may hold values from -4 to 4
- up_weight: bfloat16 [256, 2048], P('zero'), may hold values from -0.375 to 0.375
- down_weight: bfloat16 [2048, 256], P('zero'), may hold values from -0.125 to 0.125
- query_bias: bfloat16 [256], P('zero'), may hold values from -3 to 3
- value_bias: bfloat16 [256], P('zero'), may hold values from -3 to 3
- out_bias: bfloat16 [256], P('zero'), may hold values from -3 to 3
- up_bias: bfloat16 [2048], P('zero'), may hold values from -3 to 3
- down_bias: bfloat16 [256], P('zero'), may hold values from -3 to 3
- first_gain: bfloat16 [256], P('zero'), may hold values from 0.5 to 1.5
- first_shift: bfloat16 [256], P('zero'), may hold values from -3 to 3
- second_gain: bfloat16 [256], P('zero'), may hold values from 0.5 to 1.5
- second_shift: bfloat16 [256], P('zero'), may hold values from -3 to 3
- cotangent: bfloat16 [64, 1024, 256], P(('dp', 'zero')), may hold values from -6 to 6
Outputs:
- layer_out: bfloat16 [64, 1024, 256], P(('dp', 'zero'))
- grad_tokens: float32 [64, 1024, 256], P(('dp', 'zero'))
- grad_query_weight: float32 [256, 256], P('zero')
- grad_key_weight: float32 [256, 256], P('zero')
- grad_value_weight: float32 [256, 256], P('zero')
- grad_out_weight: float32 [256, 256], P('zero')
- grad_up_weight: float32 [256, 2048], P('zero')
- grad_down_weight: float32 [2048, 256], P('zero')
- grad_query_bias: float32 [256], P('zero')
- grad_value_bias: float32 [256], P('zero')
- grad_out_bias: float32 [256], P('zero')
- grad_up_bias: float32 [2048], P('zero')
- grad_down_bias: float32 [256], P('zero')
- grad_first_gain: float32 [256], P('zero')
- grad_first_shift: float32 [256], P('zero')
- grad_second_gain: float32 [256], P('zero')
- grad_second_shift: float32 [256], P('zero')
The draws below stay inside these ranges and needn't reach their ends.
Inputs may be any that keep to these rules, and one draw needn't show every extreme that they name: `counts`: the largest count equals 1024 in every draw. `token_order`: each image's row holds every cell once.
All inputs are finite; a program needn't handle non-finite values. No bound on the sum of `key_mask` on one device may be relied on, other than what follows from the above.
Results may differ from the reference program's by a relative error of at most 0.015.
The reference program's roundings to bfloat16 on the way count: a program that leaves them out, or rounds other values in their place, can miss the bound.
Values may be sent and summed in bfloat16 or wider, within the bound.
No kernel may reach another device: no remote copies, remote signals or barrier semaphores. Data moves between devices by JAX's collectives and lax.ppermute only.
A program may use at most 256 MiB of HBM per device.

```python
import math
import jax
import jax.numpy as jnp
from jax import lax

D = 256
HEADS = 8
HD = 32
FF = 2048
GRID = 32
LEN = 1024
IMAGES = 64


def draw_counts(key, part):
    key = jax.random.fold_in(key, 5)
    first, second = jax.random.split(key)
    drawn = jax.random.randint(first, (IMAGES,), LEN // 4, LEN + 1)
    chosen = jax.random.randint(second, (), 0, IMAGES)
    return jnp.where(jnp.arange(IMAGES) == chosen, LEN, drawn).astype(jnp.int32)


def with_ends(array, own_key, smallest, high):
    index_at = [jax.random.randint(jax.random.fold_in(own_key, axis), (), 0, length) for axis, length in enumerate(array.shape)]
    longest = array.shape.index(max(array.shape))
    next_to = index_at[:longest] + [(index_at[longest] + 1) % array.shape[longest]] + index_at[longest + 1:]
    return array.at[tuple(index_at)].set(smallest).at[tuple(next_to)].set(high)


def level_of(rng, dims, shards, low, top_value):
    level = 1.0
    for dim, shards_of in shards:
        draws = jax.random.uniform(jax.random.fold_in(jax.random.fold_in(rng, 6), dim), (shards_of,), jnp.float32, low / len(shards), top_value / len(shards))
        level = level * jnp.repeat(jnp.exp(draws), dims[dim] // shards_of).reshape((-1,) + (1,) * (len(dims) - 1 - dim))
    return level


def gaussian(own_key, shape, scale, reach, shards=(), held_as=jnp.bfloat16):
    factor_of = level_of(own_key, shape, shards, -0.22, 0.18) if shards else 1.0
    values = jax.random.normal(own_key, shape, jnp.float32) * scale * factor_of
    return jnp.minimum(jnp.maximum(values, -reach), reach).astype(held_as)


def setup_inputs(seed: int = 0) -> dict:
    splits = jax.random.split(jax.random.key(seed), 22)
    tokens = gaussian(splits[0], (IMAGES, LEN, D), 1.0, 6.0, ((0, 32),))
    counts = draw_counts(jax.random.fold_in(splits[21], 71), 0)
    key_mask = with_ends((jax.random.randint(splits[2], (IMAGES, LEN), 0, 4) < 3).astype(jnp.int32), jax.random.fold_in(splits[2], 1), 0, 1)
    rotation = with_ends(jax.random.randint(splits[3], (IMAGES,), 0, 4), jax.random.fold_in(splits[3], 1), 0, 3).astype(jnp.int32)
    token_order = jax.vmap(lambda own: jax.random.permutation(own, LEN))(jax.random.split(splits[4], IMAGES)).reshape((IMAGES, LEN)).astype(jnp.int32)
    query_weight = gaussian(splits[5], (D, D), D ** -0.5, 0.375, ((0, 8),))
    key_weight = gaussian(splits[6], (D, D), D ** -0.5, 0.375, ((0, 8),))
    value_weight = gaussian(splits[7], (D, D), D ** -0.5, 0.375, ((0, 8),))
    out_weight = gaussian(splits[8], (D, D), (max(D // 128, 1)) ** -0.5, 4.0, ((0, 8),))
    up_weight = gaussian(splits[9], (D, FF), D ** -0.5, 0.375, ((0, 8),))
    down_weight = gaussian(splits[10], (FF, D), FF ** -0.5, 0.125, ((0, 8),))
    query_bias = gaussian(splits[11], (D,), 0.5, 3.0, ((0, 8),))
    value_bias = gaussian(splits[12], (D,), 0.5, 3.0, ((0, 8),))
    out_bias = gaussian(splits[13], (D,), 0.5, 3.0, ((0, 8),))
    up_bias = gaussian(splits[14], (FF,), 0.5, 3.0, ((0, 8),))
    down_bias = gaussian(splits[15], (D,), 0.5, 3.0, ((0, 8),))
    first_gain = jnp.clip(1.0 + 0.1 * jax.random.normal(splits[16], (D,), jnp.float32), 0.5, 1.5).astype(jnp.bfloat16)
    first_shift = gaussian(splits[17], (D,), 0.5, 3.0, ((0, 8),))
    second_gain = jnp.clip(1.0 + 0.1 * jax.random.normal(splits[18], (D,), jnp.float32), 0.5, 1.5).astype(jnp.bfloat16)
    second_shift = gaussian(splits[19], (D,), 0.5, 3.0, ((0, 8),))
    cotangent = gaussian(splits[20], (IMAGES, LEN, D), 1.0, 6.0, ((0, 32),))
    return dict(tokens=tokens, counts=counts, key_mask=key_mask, rotation=rotation, token_order=token_order, query_weight=query_weight, key_weight=key_weight, value_weight=value_weight, out_weight=out_weight, up_weight=up_weight, down_weight=down_weight, query_bias=query_bias, value_bias=value_bias, out_bias=out_bias, up_bias=up_bias, down_bias=down_bias, first_gain=first_gain, first_shift=first_shift, second_gain=second_gain, second_shift=second_shift, cotangent=cotangent)


EPS = 1e-05
HIGH = lax.Precision.HIGHEST

@jax.custom_vjp
def low(v):
    return lax.optimization_barrier(v.astype(jnp.bfloat16)).astype(jnp.float32)

@jax.custom_vjp
def low_back(v):
    return v

def low_keep(v):
    return (low(v), None)

def low_pass(kept, grad):
    return (grad,)

def back_keep(v):
    return (v, None)

def back_low(kept, grad):
    return (low(grad),)
low.defvjp(low_keep, low_pass)
low_back.defvjp(back_keep, back_low)

def positions(token_order, rotation, grid, width):
    half = width // 2
    row = token_order // grid
    column = token_order % grid
    turn = rotation[:, None]
    last = grid - 1
    ycoord = jnp.where(turn == 0, row, jnp.where(turn == 1, column, jnp.where(turn == 2, last - row, last - column)))
    xcoord = jnp.where(turn == 0, column, jnp.where(turn == 1, last - row, jnp.where(turn == 2, last - column, row)))
    index = jnp.arange(half)
    freq = 10000.0 ** ((2 * (index // 2)).astype(jnp.float32) / half)

    def embed(coord):
        angle = (coord.astype(jnp.float32) + 1.0) / (grid + 1e-06) * (2.0 * math.pi)
        angle = angle[..., None] / freq
        return jnp.where(index % 2 == 0, jnp.sin(angle), jnp.cos(angle))
    return jnp.concatenate([embed(ycoord), embed(xcoord)], axis=-1)

def layer_norm(field, gain, shift):
    middle = lax.optimization_barrier(jnp.mean(field, axis=-1, keepdims=True))
    center = field - middle
    spread = lax.optimization_barrier(jnp.mean(center * center, axis=-1, keepdims=True))
    return center * lax.rsqrt(spread + EPS) * gain + shift

def matmul(left, right):
    return jnp.dot(left, right, precision=HIGH)

def forward(tokens, params, pos, usable):
    query_weight, key_weight, value_weight, out_weight, up_weight, down_weight, query_bias, value_bias, out_bias, up_bias, down_bias, first_gain, first_shift, second_gain, second_shift = params
    length = tokens.shape[0]
    lifted = low(tokens + pos)
    query = low_back(low(matmul(lifted, query_weight) + query_bias)).reshape(length, HEADS, HD)
    key = low_back(low(matmul(lifted, key_weight))).reshape(length, HEADS, HD)
    value = low_back(low(matmul(tokens, value_weight) + value_bias)).reshape(length, HEADS, HD)
    scores = jnp.einsum('qhd,khd->hqk', query, key, precision=HIGH) * HD ** (-0.5)
    scores = low_back(scores)
    scores = jnp.where(usable[None, None, :], scores, -1e+30)
    probs = low(jax.nn.softmax(scores, axis=-1))
    mixed = jnp.einsum('hqk,khd->qhd', probs, value, precision=HIGH).reshape(length, HEADS * HD)
    mixed = low_back(low(mixed))
    branch = low_back(matmul(mixed, out_weight) + out_bias)
    first_norm = layer_norm(tokens + branch, first_gain, first_shift)
    first_low = low(first_norm)
    hidden_pre = low_back(matmul(first_low, up_weight) + up_bias)
    hidden = low(jax.nn.gelu(hidden_pre))
    ffn = low_back(matmul(hidden, down_weight) + down_bias)
    return layer_norm(first_norm + ffn, second_gain, second_shift)

def reference(tokens, counts, key_mask, rotation, token_order, query_weight, key_weight, value_weight, out_weight, up_weight, down_weight, query_bias, value_bias, out_bias, up_bias, down_bias, first_gain, first_shift, second_gain, second_shift, cotangent):
    params = tuple((w.astype(jnp.float32) for w in (query_weight, key_weight, value_weight, out_weight, up_weight, down_weight, query_bias, value_bias, out_bias, up_bias, down_bias, first_gain, first_shift, second_gain, second_shift)))
    pos = positions(token_order, rotation, GRID, D)
    slots = jnp.arange(LEN)
    usable = (slots[None, :] < counts[:, None]) & ((key_mask == 1) | (slots[None, :] == 0))

    def one_image(totals, item):
        image, pos_one, usable_one, cot_one = item
        result, pull = jax.vjp(lambda xin, pin: forward(xin, pin, pos_one, usable_one), image.astype(jnp.float32), params)
        grad_in, grad_params = pull(cot_one.astype(jnp.float32))
        totals = jax.tree.map(lambda left, right: left + right, totals, grad_params)
        return (totals, (result.astype(jnp.bfloat16), grad_in))
    start = tuple((jnp.zeros(w.shape, jnp.float32) for w in params))
    totals, (layer_out, grad_tokens) = lax.scan(one_image, start, (tokens, pos, usable, cotangent))
    return (layer_out, grad_tokens, totals[0], totals[1], totals[2], totals[3], totals[4], totals[5], totals[6], totals[7], totals[8], totals[9], totals[10], totals[11], totals[12], totals[13], totals[14])
```

```python
import functools
import math

import jax
import jax.numpy as jnp
import numpy as np
from jax import lax
from jax.experimental import pallas as pl
from jax.experimental.pallas import tpu as pltpu
from jax.sharding import PartitionSpec as P

HEADS = 8
GRID = 32
EPS = 1e-05
LOG2E = 1.4426950408889634
SAFE = 60.0

BF = jnp.bfloat16
F32 = jnp.float32
SMEM = pltpu.SMEM
VMEM_LIMIT = 60 << 20


def nn(left, right):
    return lax.dot_general(left, right, (((1,), (0,)), ((), ())), preferred_element_type=F32)


def nt(left, right):
    return lax.dot_general(left, right, (((1,), (1,)), ((), ())), preferred_element_type=F32)


def position_table(grid, width):
    half = width // 2
    index = np.arange(half)
    freq = np.power(np.float32(10000.0), (2 * (index // 2)).astype(np.float32) / np.float32(half)).astype(np.float32)
    coord = np.arange(grid).astype(np.float32)
    angle = ((coord + np.float32(1.0)) / np.float32(grid + 1e-06) * np.float32(2.0 * math.pi)).astype(np.float32)
    angle = (angle[:, None] / freq).astype(np.float32)
    table = np.where(index % 2 == 0, np.sin(angle), np.cos(angle)).astype(np.float32)
    high = table.astype(BF)
    rest = (table - high.astype(np.float32)).astype(BF)
    whole = np.zeros((4 * grid, width), dtype=BF)
    for group, piece in enumerate((high, high, rest, rest)):
        start = (group % 2) * half
        whole[group * grid : (group + 1) * grid, start : start + half] = piece
    return np.ascontiguousarray(whole.T)


def prep_kernel(counts, rotation, tokens, key_mask, token_order, table, lifted_t, lifted_ct, tokens_ct, rank_out, used):
    image = pl.program_id(0)
    length = tokens.shape[1]
    slot = lax.broadcasted_iota(jnp.int32, (1, length), 1)
    mask = key_mask[pl.ds(image, 1), :]
    usable = (slot < counts[image]) & ((mask == 1) | (slot == 0))
    flag = jnp.where(usable, 1, 0)
    used[image] = jnp.sum(flag)
    total = flag
    step = 1
    while step < length:
        total = total + jnp.where(slot >= step, pltpu.roll(total, step, 1), 0)
        step *= 2
    rank = jnp.where(usable, total - 1, -1)
    rank_out[pl.ds(image, 1), :] = rank
    cell = token_order[pl.ds(image, 1), :]
    row = cell // GRID
    column = cell - row * GRID
    turn = rotation[image]
    last = GRID - 1
    ycoord = jnp.where(turn == 0, row, jnp.where(turn == 1, column, jnp.where(turn == 2, last - row, last - column)))
    xcoord = jnp.where(turn == 0, column, jnp.where(turn == 1, last - row, jnp.where(turn == 2, last - column, row)))
    place = lax.broadcasted_iota(jnp.int32, (4 * GRID, length), 0)
    group = place // GRID
    wanted = jnp.where(group % 2 == 0, ycoord, xcoord)
    hot = jnp.where(place - group * GRID == wanted, 1.0, 0.0).astype(BF)
    pos_t = nn(table[...], hot)
    tokens_t = tokens[0].T
    low_t = (tokens_t.astype(F32) + pos_t).astype(BF)
    lifted_t[0] = low_t
    compact = lax.broadcasted_iota(jnp.int32, (length, length), 0)
    chosen = jnp.where(compact == rank, 1.0, 0.0).astype(BF)
    lifted_ct[0] = nt(low_t, chosen).astype(BF)
    tokens_ct[0] = nt(tokens_t, chosen).astype(BF)


def forward_kernel(
    heads_per_step, used, lifted_t, lifted_ct, tokens_ct, weights, vectors,
    kept, mixed_t, inverse, query_t, key_t, value_rows, key_rows, value_ext, calm,
):
    image = pl.program_id(0)
    step = pl.program_id(1)
    width, length = query_t.shape[1:]
    size = width // HEADS
    ext = size + 16
    scale = LOG2E * size ** (-0.5)
    count = used[image]

    @pl.when(step == 0)
    def _():
        columns = vectors[...].T
        query = (nn(weights[0].T, lifted_t[0]) + columns[:, 0:1]).astype(BF)
        query_t[0] = query
        key = nn(weights[1].T, lifted_ct[0]).astype(BF)
        key_t[0] = key
        value = (nn(weights[2].T, tokens_ct[0]) + columns[:, 1:2]).astype(BF)
        key_turned = key.T
        value_turned = value.T
        for block in range(width // 128):
            part = slice(block * 128, (block + 1) * 128)
            key_rows[block] = key_turned[:, part]
            value_rows[0, block] = value_turned[:, part]
        valid = lax.broadcasted_iota(jnp.int32, (size, length), 1) < count
        first = lax.broadcasted_iota(jnp.int32, (16, length), 0) == 0
        ones = jnp.where(first & valid[:16], 1.0, 0.0).astype(BF)
        for head in range(HEADS):
            value_ext[head * ext : head * ext + size, :] = jnp.where(valid, value[head * size : (head + 1) * size], 0).astype(BF)
            value_ext[head * ext + size : (head + 1) * ext, :] = ones
        wide_query = query.astype(F32)
        wide_key = key.astype(F32)
        query_norm = jnp.max(jnp.sum((wide_query * wide_query).reshape(HEADS, size, length), axis=1), axis=1, keepdims=True)
        key_norm = jnp.max(jnp.sum((wide_key * wide_key).reshape(HEADS, size, length), axis=1), axis=1, keepdims=True)
        reach = jnp.max(query_norm * key_norm) * (scale * scale)
        calm[0] = jnp.where(reach <= SAFE * SAFE, 1, 0)

    group_rows = lax.broadcasted_iota(jnp.int32, (128, length), 0) // size

    def one_head(index, blocks, safe):
        head = step * heads_per_step + index
        block = head // (128 // size)
        inner = head - block * (128 // size)
        span = blocks * 128
        around = query_t[0, pl.ds(pl.multiple_of(block * 128, 128), 128), :]
        own = jnp.where(group_rows == inner, around, 0).astype(BF)
        keys = key_rows[block, :span, :]
        values = value_ext[pl.ds(pl.multiple_of(head * ext, 16), ext), :span]
        piece = length // 2
        for part in range(length // piece):
            cut = slice(part * piece, (part + 1) * piece)
            scores = nn(keys, own[:, cut]) * scale
            if not safe:
                place = lax.broadcasted_iota(jnp.int32, scores.shape, 0)
                scores = jnp.where(place < count, scores, -1e30)
                scores = scores - jnp.max(scores, axis=0, keepdims=True)
            weight = jnp.exp2(scores).astype(BF)
            kept[0, index, :span, cut] = weight
            summed = nn(values, weight)
            turned = 1.0 / summed[size : size + 1, :]
            mixed_t[0, pl.ds(pl.multiple_of(head * size, 32), size), cut] = (summed[:size] * turned).astype(BF)
            inverse[0, pl.ds(head, 1), cut] = turned

    blocks_used = (count + 127) // 128
    for blocks in range(1, length // 128 + 1):

        @pl.when((calm[0] == 1) & (blocks_used == blocks))
        def _(blocks=blocks):
            for index in range(heads_per_step):
                one_head(index, blocks, True)

    @pl.when(calm[0] == 0)
    def _():
        for index in range(heads_per_step):
            one_head(index, length // 128, False)


def norm_parts(field):
    middle = jnp.mean(field, axis=-1, keepdims=True)
    center = field - middle
    spread = jnp.mean(center * center, axis=-1, keepdims=True)
    pull = lax.rsqrt(spread + EPS)
    return center * pull, pull


def norm_back(grad, normal, pull):
    return (grad - jnp.mean(grad, axis=-1, keepdims=True) - normal * jnp.mean(grad * normal, axis=-1, keepdims=True)) * pull


def ffn_kernel(
    chunk, tokens, mixed_t, inverse, cotangent, out_weight, up_weight, down_weight, vectors, up_bias,
    layer_out, grad_first, mixed_grad_t, center, grad_out, grad_up, grad_down, grad_vectors, grad_up_bias,
    out_sum, up_sum, down_sum, vector_sum, hidden_all, slope_all,
):
    step = pl.program_id(0)
    rows, width = tokens.shape
    inner = up_weight.shape[1]
    size = width // HEADS

    @pl.when(step == 0)
    def _():
        out_sum[...] = jnp.zeros_like(out_sum)
        up_sum[...] = jnp.zeros_like(up_sum)
        down_sum[...] = jnp.zeros_like(down_sum)
        vector_sum[...] = jnp.zeros_like(vector_sum)

    out_bias, down_bias, first_gain, first_shift, second_gain, second_shift = [vectors[k : k + 1, :] for k in range(2, 8)]
    mixed = mixed_t[0].T
    first_sum = tokens[...].astype(F32) + nn(mixed, out_weight[...]) + out_bias
    first_normal, first_pull = norm_parts(first_sum)
    first_norm = first_normal * first_gain + first_shift
    first_low = first_norm.astype(BF)
    second_sum = first_norm + down_bias
    root = math.sqrt(2.0 / math.pi)
    for start in range(0, inner, chunk):
        cut = slice(start, start + chunk)
        pre = nn(first_low, up_weight[:, cut]) + up_bias[:, cut]
        square = pre * pre
        bend = jnp.tanh(pre * (root + root * 0.044715 * square))
        half = 0.5 + 0.5 * bend
        hidden = (pre * half).astype(BF)
        slope_all[:, cut] = half + (0.5 * pre) * (1.0 - bend * bend) * (root + root * 3 * 0.044715 * square)
        hidden_all[:, cut] = hidden
        second_sum = second_sum + nn(hidden, down_weight[cut, :])
    second_normal, second_pull = norm_parts(second_sum)
    layer_out[...] = (second_normal * second_gain + second_shift).astype(BF)
    wide = cotangent[...].astype(F32)
    grad_second = norm_back(wide * second_gain, second_normal, second_pull)
    ffn_grad = grad_second.astype(BF)
    ffn_grad_t = ffn_grad.T
    first_low_t = first_low.T
    ones = jnp.where(lax.broadcasted_iota(jnp.int32, (16, rows), 0) == 0, 1.0, 0.0).astype(BF)
    first_ext = jnp.concatenate([first_low_t, ones], axis=0)
    back = grad_second
    for start in range(0, inner, chunk):
        cut = slice(start, start + chunk)
        hidden_grad = (nt(ffn_grad, down_weight[cut, :]) * slope_all[:, cut]).astype(BF)
        down_sum[:, cut] += nn(ffn_grad_t, hidden_all[:, cut])
        up_sum[:, cut] += nn(first_ext, hidden_grad)
        back = back + nt(hidden_grad, up_weight[:, cut])
    first = norm_back(back * first_gain, first_normal, first_pull)
    grad_first[...] = first
    branch_grad = first.astype(BF)
    out_sum[...] += nn(mixed_t[0], branch_grad)
    mixed_grad = nt(out_weight[...], branch_grad).reshape(HEADS, size, rows)
    turned = inverse[0]
    mixed_grad_t[0] = (mixed_grad * turned[:, None, :]).reshape(width, rows).astype(BF)
    center[0] = jnp.sum(mixed_grad * mixed_t[0].astype(F32).reshape(HEADS, size, rows), axis=1) * turned
    sums = (
        branch_grad.astype(F32), ffn_grad.astype(F32), back * first_normal, back, wide * second_normal, wide,
    )
    vector_sum[...] += jnp.concatenate(
        [jnp.zeros((2, width), F32)] + [jnp.sum(piece, axis=0, keepdims=True) for piece in sums], axis=0
    )

    @pl.when(step == pl.num_programs(0) - 1)
    def _():
        grad_out[...] = out_sum[...].astype(BF)
        grad_up[...] = up_sum[:width, :].astype(BF)
        grad_down[...] = down_sum[...].astype(BF).T
        grad_up_bias[...] = up_sum[width : width + 1, :]
        grad_vectors[...] = vector_sum[...]


def backward_kernel(
    heads_per_step, used, kept, value_rows, key_t, query_t, mixed_grad_t, center,
    query_grad_t, key_grad_t, value_grad_t,
):
    image = pl.program_id(0)
    step = pl.program_id(1)
    width, length = query_t.shape[1:]
    size = width // HEADS
    scale = size ** (-0.5)
    count = used[image]
    blocks_used = (count + 127) // 128
    group_rows = lax.broadcasted_iota(jnp.int32, (128, length), 0) // size

    @pl.when(step == 0)
    def _():
        key_grad_t[0] = jnp.zeros((width, length), BF)
        value_grad_t[0] = jnp.zeros((width, length), BF)

    def one_head(index, blocks):
        head = step * heads_per_step + index
        block = head // (128 // size)
        inner = head - block * (128 // size)
        span = blocks * 128
        own_rows = pl.ds(pl.multiple_of(head * size, 32), size)
        around = mixed_grad_t[0, pl.ds(pl.multiple_of(block * 128, 128), 128), :]
        own = jnp.where(group_rows == inner, around, 0).astype(BF)
        values = value_rows[0, block, :span, :]
        keys = key_t[0, own_rows, :span]
        value_sum = jnp.zeros((size, span), F32)
        key_sum = jnp.zeros((size, span), F32)
        piece = length // 2
        for part in range(length // piece):
            cut = slice(part * piece, (part + 1) * piece)
            pulled = nn(values, own[:, cut]) - center[0, pl.ds(head, 1), cut]
            weight = kept[0, index, :span, cut]
            score_grad = (weight.astype(F32) * pulled).astype(BF)
            query_grad_t[0, own_rows, cut] = (nn(keys, score_grad) * scale).astype(BF)
            value_sum = value_sum + nt(mixed_grad_t[0, own_rows, cut], weight)
            key_sum = key_sum + nt(query_t[0, own_rows, cut], score_grad)
        valid = lax.broadcasted_iota(jnp.int32, (size, span), 1) < count
        value_grad_t[0, own_rows, :span] = jnp.where(valid, value_sum, 0.0).astype(BF)
        key_grad_t[0, own_rows, :span] = jnp.where(valid, key_sum * scale, 0.0).astype(BF)

    for blocks in range(1, length // 128 + 1):

        @pl.when(blocks_used == blocks)
        def _(blocks=blocks):
            for index in range(heads_per_step):
                one_head(index, blocks)


def weights_kernel(
    lifted_t, lifted_ct, tokens_ct, query_grad_t, key_grad_t, value_grad_t, grads, grad_vectors, sums, vector_sum
):
    image = pl.program_id(0)
    length = lifted_t.shape[2]
    width = lifted_t.shape[1]

    @pl.when(image == 0)
    def _():
        sums[...] = jnp.zeros_like(sums)
        vector_sum[...] = jnp.zeros_like(vector_sum)

    ones = jnp.ones((16, length), BF)
    query_sum = nt(jnp.concatenate([lifted_t[0], ones], axis=0), query_grad_t[0])
    value_sum = nt(jnp.concatenate([tokens_ct[0], ones], axis=0), value_grad_t[0])
    sums[0] += query_sum[:width]
    sums[1] += nt(lifted_ct[0], key_grad_t[0])
    sums[2] += value_sum[:width]
    vector_sum[0:1, :] += query_sum[width : width + 1]
    vector_sum[1:2, :] += value_sum[width : width + 1]

    @pl.when(image == pl.num_programs(0) - 1)
    def _():
        grads[...] = sums[...].astype(BF)
        grad_vectors[...] = vector_sum[...]


def tokens_kernel(rank, grad_first, weights, query_grad_t, key_grad_t, value_grad_t, grad_tokens):
    image = pl.program_id(0)
    length = query_grad_t.shape[2]
    width = query_grad_t.shape[1]
    compact = lax.broadcasted_iota(jnp.int32, (length, length), 0)
    chosen = jnp.where(compact == rank[pl.ds(image, 1), :], 1.0, 0.0).astype(BF)
    both = nn(jnp.concatenate([key_grad_t[0], value_grad_t[0]], axis=0), chosen).astype(BF)
    total_t = nn(weights[0], query_grad_t[0]) + nn(weights[1], both[:width]) + nn(weights[2], both[width:])
    grad_tokens[0] = grad_first[0] + total_t.T


def params(*semantics):
    return pltpu.CompilerParams(dimension_semantics=semantics, vmem_limit_bytes=VMEM_LIMIT)


def whole(shape):
    return pl.BlockSpec(shape, lambda *_: (0,) * len(shape))


def per_image(shape):
    return pl.BlockSpec((1,) + shape, lambda i, *_: (i,) + (0,) * len(shape))


def scalars():
    return pl.BlockSpec(memory_space=SMEM)


def shaped(shape, dtype):
    return jax.ShapeDtypeStruct(shape, dtype)


def others(size):
    for far in range(1, size):
        if size & (size - 1) == 0:
            yield [(k, k ^ far) for k in range(size)], lambda me, far=far: me ^ far
        else:
            yield [(k, (k + far) % size) for k in range(size)], lambda me, far=far: (me + far) % size


def reduce_own(packed, axis, size):
    me = lax.axis_index(axis)
    total = lax.dynamic_index_in_dim(packed, me, 0, keepdims=False).astype(F32)
    for pairs, partner in others(size):
        piece = lax.dynamic_index_in_dim(packed, partner(me), 0, keepdims=False)
        total = total + lax.ppermute(piece, axis, pairs).astype(F32)
    return total


def reduce_all(field, axis, size):
    low = field.astype(BF)
    total = field
    for pairs, _ in others(size):
        total = total + lax.ppermute(low, axis, pairs).astype(F32)
    return total


def body(
    tokens, counts, key_mask, rotation, token_order, query_weight, key_weight, value_weight, out_weight, up_weight,
    down_weight, query_bias, value_bias, out_bias, up_bias, down_bias, first_gain, first_shift, second_gain,
    second_shift, cotangent, *, zero, dp,
):
    images, length, width = tokens.shape
    rows = images * length
    inner = up_weight.shape[1]
    share = width // zero
    inner_share = inner // zero
    heads_per_step = 2
    steps = HEADS // heads_per_step

    small = [query_bias, value_bias, out_bias, down_bias, first_gain, first_shift, second_gain, second_shift, up_bias]
    flat = jnp.concatenate(small)
    small_rows = -(-flat.shape[0] // width)
    flat = jnp.pad(flat, (0, small_rows * width - flat.shape[0])).reshape(small_rows, width)
    bundle = jnp.concatenate([query_weight, key_weight, value_weight, flat], axis=0)
    near = lax.all_gather(bundle, "zero", axis=0)
    weights = near[:, : 3 * share].reshape(zero, 3, share, width).transpose(1, 0, 2, 3).reshape(3, width, width)
    flats = near[:, 3 * share :].reshape(zero, small_rows * width)
    vectors = flats[:, : 8 * share].reshape(zero, 8, share).transpose(1, 0, 2).reshape(8, width).astype(F32)
    full_up_bias = flats[:, 8 * share : 8 * share + inner_share].reshape(1, inner).astype(F32)
    full_out = lax.all_gather(out_weight, "zero", axis=0, tiled=True)
    full_up = lax.all_gather(up_weight, "zero", axis=0, tiled=True)
    full_down = lax.all_gather(down_weight, "zero", axis=0, tiled=True)

    table = jnp.asarray(position_table(GRID, width))
    turned = shaped((images, width, length), BF)
    lifted_t, lifted_ct, tokens_ct, rank, used = pl.pallas_call(
        prep_kernel,
        grid=(images,),
        in_specs=[
            scalars(), scalars(), per_image((length, width)), whole((images, length)), whole((images, length)),
            whole(table.shape),
        ],
        out_specs=[per_image((width, length))] * 3 + [whole((images, length)), scalars()],
        out_shape=[turned] * 3 + [shaped((images, length), jnp.int32), shaped((images,), jnp.int32)],
        compiler_params=params("arbitrary"),
        name="prep",
    )(counts, rotation, tokens, key_mask, token_order, table)

    head_block = pl.BlockSpec((1, heads_per_step, length, length), lambda i, s: (i, s, 0, 0))
    kept, mixed_t, inverse, query_t, key_t, value_rows = pl.pallas_call(
        functools.partial(forward_kernel, heads_per_step),
        grid=(images, steps),
        in_specs=[scalars()] + [per_image((width, length))] * 3 + [whole((3, width, width)), whole((8, width))],
        out_specs=[
            head_block, per_image((width, length)), per_image((HEADS, length)), per_image((width, length)),
            per_image((width, length)), per_image((width // 128, length, 128)),
        ],
        out_shape=[
            shaped((images, HEADS, length, length), BF), turned, shaped((images, HEADS, length), F32), turned, turned,
            shaped((images, width // 128, length, 128), BF),
        ],
        scratch_shapes=[
            pltpu.VMEM((width // 128, length, 128), BF),
            pltpu.VMEM((width + 16 * HEADS, length), BF),
            pltpu.SMEM((1,), jnp.int32),
        ],
        compiler_params=params("arbitrary", "arbitrary"),
        cost_estimate=pl.CostEstimate(flops=8 * rows * length * width, bytes_accessed=4 << 20, transcendentals=rows * length * HEADS),
        name="attend_forward",
    )(used, lifted_t, lifted_ct, tokens_ct, weights, vectors)

    block = length // 2
    per = length // block
    row_block = pl.BlockSpec((block, width), lambda s: (s, 0))

    def turned_block(height):
        return pl.BlockSpec((1, height, block), lambda s: (s // per, 0, s % per))

    flat_tokens = tokens.reshape(rows, width)
    layer_out, grad_first, mixed_grad_t, center, grad_out, grad_up, grad_down, grad_vectors, grad_up_bias = pl.pallas_call(
        functools.partial(ffn_kernel, 512),
        grid=(rows // block,),
        in_specs=[
            row_block, turned_block(width), turned_block(HEADS), row_block, whole((width, width)), whole((width, inner)),
            whole((inner, width)), whole((8, width)), whole((1, inner)),
        ],
        out_specs=[
            row_block, row_block, turned_block(width), turned_block(HEADS), whole((width, width)), whole((width, inner)),
            whole((inner, width)), whole((8, width)), whole((1, inner)),
        ],
        out_shape=[
            shaped((rows, width), BF), shaped((rows, width), F32), turned, shaped((images, HEADS, length), F32),
            shaped((width, width), BF), shaped((width, inner), BF), shaped((inner, width), BF), shaped((8, width), F32),
            shaped((1, inner), F32),
        ],
        scratch_shapes=[
            pltpu.VMEM((width, width), F32), pltpu.VMEM((width + 16, inner), F32), pltpu.VMEM((width, inner), F32),
            pltpu.VMEM((8, width), F32), pltpu.VMEM((block, inner), BF), pltpu.VMEM((block, inner), F32),
        ],
        compiler_params=params("arbitrary"),
        cost_estimate=pl.CostEstimate(flops=12 * rows * width * inner, bytes_accessed=16 << 20, transcendentals=rows * inner),
        name="feed_forward",
    )(flat_tokens, mixed_t, inverse, cotangent.reshape(rows, width), full_out, full_up, full_down, vectors, full_up_bias)

    lanes = inner // width
    far_rows = share + share * lanes + inner_share
    early = jnp.concatenate(
        [
            grad_out.reshape(zero, share, width),
            grad_up.reshape(zero, share, lanes, width).transpose(0, 2, 1, 3).reshape(zero, share * lanes, width),
            grad_down.reshape(zero, inner_share, width),
        ],
        axis=1,
    )
    early = reduce_all(reduce_own(early, "zero", zero), "dp", dp)

    query_grad_t, key_grad_t, value_grad_t = pl.pallas_call(
        functools.partial(backward_kernel, heads_per_step),
        grid=(images, steps),
        in_specs=[scalars(), head_block, per_image((width // 128, length, 128))] + [per_image((width, length))] * 3 + [per_image((HEADS, length))],
        out_specs=[per_image((width, length))] * 3,
        out_shape=[turned] * 3,
        compiler_params=params("arbitrary", "arbitrary"),
        cost_estimate=pl.CostEstimate(flops=16 * rows * length * width, bytes_accessed=4 << 20, transcendentals=rows * length * HEADS),
        name="attend_backward",
    )(used, kept, value_rows, key_t, query_t, mixed_grad_t, center)

    grads, late_vectors = pl.pallas_call(
        weights_kernel,
        grid=(images,),
        in_specs=[per_image((width, length))] * 6,
        out_specs=[whole((3, width, width)), whole((8, width))],
        out_shape=[shaped((3, width, width), BF), shaped((8, width), F32)],
        scratch_shapes=[pltpu.VMEM((3, width, width), F32), pltpu.VMEM((8, width), F32)],
        compiler_params=params("arbitrary"),
        name="weight_grads",
    )(lifted_t, lifted_ct, tokens_ct, query_grad_t, key_grad_t, value_grad_t)

    all_vectors = (grad_vectors + late_vectors).reshape(8, zero, share).transpose(1, 0, 2).reshape(zero, 8 * share)
    all_vectors = jnp.concatenate([all_vectors, grad_up_bias.reshape(zero, inner_share)], axis=1)
    all_vectors = jnp.pad(all_vectors, ((0, 0), (0, small_rows * width - all_vectors.shape[1]))).reshape(zero, small_rows, width)
    late = jnp.concatenate([grads.reshape(3, zero, share, width).transpose(1, 0, 2, 3).reshape(zero, 3 * share, width), all_vectors.astype(BF)], axis=1)
    late = reduce_all(reduce_own(late, "zero", zero), "dp", dp)

    grad_tokens = pl.pallas_call(
        tokens_kernel,
        grid=(images,),
        in_specs=[whole((images, length)), per_image((length, width)), whole((3, width, width))] + [per_image((width, length))] * 3,
        out_specs=per_image((length, width)),
        out_shape=shaped((images, length, width), F32),
        compiler_params=params("arbitrary"),
        cost_estimate=pl.CostEstimate(flops=6 * rows * width * width + 4 * rows * length * width, bytes_accessed=8 << 20, transcendentals=0),
        name="token_grads",
    )(rank, grad_first.reshape(images, length, width), weights, query_grad_t, key_grad_t, value_grad_t)

    grad_out_own = early[:share]
    grad_up_own = early[share : share + share * lanes].reshape(lanes, share, width).transpose(1, 0, 2).reshape(share, inner)
    grad_down_own = early[share + share * lanes : far_rows]
    own = late[3 * share :].reshape(small_rows * width)
    cuts = [own[k * share : (k + 1) * share] for k in range(8)]
    up_bias_own = own[8 * share : 8 * share + inner_share]
    return (
        layer_out.reshape(images, length, width),
        grad_tokens,
        late[:share],
        late[share : 2 * share],
        late[2 * share : 3 * share],
        grad_out_own,
        grad_up_own,
        grad_down_own,
        cuts[0],
        cuts[1],
        cuts[2],
        up_bias_own,
        cuts[3],
        cuts[4],
        cuts[5],
        cuts[6],
        cuts[7],
    )


def solution(mesh):
    batch = P(("dp", "zero"))
    wide = P(("dp", "zero"), None, None)
    flat = P(("dp", "zero"), None)
    matrix = P("zero", None)
    vector = P("zero")
    in_specs = (wide, batch, flat, batch, flat) + (matrix,) * 6 + (vector,) * 9 + (wide,)
    out_specs = (wide, wide) + (matrix,) * 6 + (vector,) * 9
    run = functools.partial(body, zero=mesh.shape["zero"], dp=mesh.shape["dp"])
    return jax.shard_map(run, mesh=mesh, in_specs=in_specs, out_specs=out_specs, check_vma=False)
```

```python
import functools
import math

import jax
import jax.numpy as jnp
import numpy as np
from jax import lax
from jax.experimental import pallas as pl
from jax.experimental.pallas import tpu as pltpu
from jax.sharding import PartitionSpec as P

HEADS = 8
GRID = 32
EPS = 1e-05
LOG2E = 1.4426950408889634
SAFE = 60.0

BF = jnp.bfloat16
F32 = jnp.float32
SMEM = pltpu.SMEM
VMEM_LIMIT = 60 << 20
VIRTUAL = 8


def nn(left, right):
    return lax.dot_general(left, right, (((1,), (0,)), ((), ())), preferred_element_type=F32)


def nt(left, right):
    return lax.dot_general(left, right, (((1,), (1,)), ((), ())), preferred_element_type=F32)


def position_table(grid, width):
    half = width // 2
    index = np.arange(half)
    freq = np.power(np.float32(10000.0), (2 * (index // 2)).astype(np.float32) / np.float32(half)).astype(np.float32)
    coord = np.arange(grid).astype(np.float32)
    angle = ((coord + np.float32(1.0)) / np.float32(grid + 1e-06) * np.float32(2.0 * math.pi)).astype(np.float32)
    angle = (angle[:, None] / freq).astype(np.float32)
    table = np.where(index % 2 == 0, np.sin(angle), np.cos(angle)).astype(np.float32)
    high = table.astype(BF)
    rest = (table - high.astype(np.float32)).astype(BF)
    whole = np.zeros((4 * grid, width), dtype=BF)
    for group, piece in enumerate((high, high, rest, rest)):
        start = (group % 2) * half
        whole[group * grid : (group + 1) * grid, start : start + half] = piece
    return np.ascontiguousarray(whole.T)


def pack_kernel(where, query, key, value, out, down, up, *refs):
    vectors, up_bias, near, far, stack = refs[:8], refs[8], refs[9], refs[10], refs[11]
    share, width = query.shape
    for k, vector in enumerate(vectors):
        stack[k : k + 1, :] = vector[...].astype(F32).reshape(1, share)
    place = lax.broadcasted_iota(jnp.int32, (share, width), 1) - where[0] * share
    spread = jnp.where(place == lax.broadcasted_iota(jnp.int32, (share, width), 0), 1.0, 0.0).astype(BF)
    rows = nn(stack[...].astype(BF), spread)
    bias = jnp.broadcast_to(up_bias[...].astype(F32).reshape(1, width), (8, width))
    last = jnp.concatenate([rows, bias], axis=0).astype(BF)
    for d in range(near.shape[0]):
        near[d, 0:share, :] = query[...]
        near[d, share : 2 * share, :] = key[...]
        near[d, 2 * share : 3 * share, :] = value[...]
        near[d, 3 * share :, :] = last
        far[d, 0 : down.shape[0], :] = down[...]
        far[d, down.shape[0] : down.shape[0] + share, :] = out[...]
        for lane in range(up.shape[1] // width):
            start = down.shape[0] + share * (lane + 1)
            far[d, start : start + share, :] = up[:, lane * width : (lane + 1) * width]


def prep_kernel(counts, rotation, tokens, key_mask, token_order, table, lifted_t, lifted_ct, tokens_ct, rank_out, used):
    image = pl.program_id(0)
    length = tokens.shape[1]
    slot = lax.broadcasted_iota(jnp.int32, (1, length), 1)
    mask = key_mask[pl.ds(image, 1), :]
    usable = (slot < counts[image]) & ((mask == 1) | (slot == 0))
    flag = jnp.where(usable, 1, 0)
    used[image] = jnp.sum(flag)
    total = flag
    step = 1
    while step < length:
        total = total + jnp.where(slot >= step, pltpu.roll(total, step, 1), 0)
        step *= 2
    rank = jnp.where(usable, total - 1, -1)
    rank_out[pl.ds(image, 1), :] = rank
    cell = token_order[pl.ds(image, 1), :]
    row = cell // GRID
    column = cell - row * GRID
    turn = rotation[image]
    last = GRID - 1
    ycoord = jnp.where(turn == 0, row, jnp.where(turn == 1, column, jnp.where(turn == 2, last - row, last - column)))
    xcoord = jnp.where(turn == 0, column, jnp.where(turn == 1, last - row, jnp.where(turn == 2, last - column, row)))
    place = lax.broadcasted_iota(jnp.int32, (4 * GRID, length), 0)
    group = place // GRID
    wanted = jnp.where(group % 2 == 0, ycoord, xcoord)
    hot = jnp.where(place - group * GRID == wanted, 1.0, 0.0).astype(BF)
    pos_t = nn(table[...], hot)
    tokens_t = tokens[0].T
    low_t = (tokens_t.astype(F32) + pos_t).astype(BF)
    lifted_t[0] = low_t
    compact = lax.broadcasted_iota(jnp.int32, (length, length), 0)
    chosen = jnp.where(compact == rank, 1.0, 0.0).astype(BF)
    lifted_ct[0] = nt(low_t, chosen).astype(BF)
    tokens_ct[0] = nt(tokens_t, chosen).astype(BF)


def near_weight(near, k):
    share = near.shape[2] // VIRTUAL
    return jnp.concatenate([near[d, k * share : (k + 1) * share, :] for d in range(VIRTUAL)], axis=0)


def near_vectors(near):
    share = near.shape[2] // VIRTUAL
    total = near[0, 3 * share : 3 * share + 16, :].astype(F32)
    for d in range(1, VIRTUAL):
        total = total + near[d, 3 * share : 3 * share + 16, :].astype(F32)
    return total[:8]


def forward_kernel(
    heads_per_step, used, lifted_t, lifted_ct, tokens_ct, near,
    kept, mixed_t, inverse, query_t, key_t, value_rows, key_rows, value_ext, calm,
):
    image = pl.program_id(0)
    step = pl.program_id(1)
    width, length = query_t.shape[1:]
    size = width // HEADS
    ext = size + 16
    scale = LOG2E * size ** (-0.5)
    count = used[image]

    @pl.when(step == 0)
    def _():
        weights = [near_weight(near, k) for k in range(3)]
        columns = near_vectors(near).T
        query = (nn(weights[0].T, lifted_t[0]) + columns[:, 0:1]).astype(BF)
        query_t[0] = query
        key = nn(weights[1].T, lifted_ct[0]).astype(BF)
        key_t[0] = key
        value = (nn(weights[2].T, tokens_ct[0]) + columns[:, 1:2]).astype(BF)
        key_turned = key.T
        value_turned = value.T
        for block in range(width // 128):
            part = slice(block * 128, (block + 1) * 128)
            key_rows[block] = key_turned[:, part]
            value_rows[0, block] = value_turned[:, part]
        valid = lax.broadcasted_iota(jnp.int32, (size, length), 1) < count
        first = lax.broadcasted_iota(jnp.int32, (16, length), 0) == 0
        ones = jnp.where(first & valid[:16], 1.0, 0.0).astype(BF)
        for head in range(HEADS):
            value_ext[head * ext : head * ext + size, :] = jnp.where(valid, value[head * size : (head + 1) * size], 0).astype(BF)
            value_ext[head * ext + size : (head + 1) * ext, :] = ones
        wide_query = query.astype(F32)
        wide_key = key.astype(F32)
        query_norm = jnp.max(jnp.sum((wide_query * wide_query).reshape(HEADS, size, length), axis=1), axis=1, keepdims=True)
        key_norm = jnp.max(jnp.sum((wide_key * wide_key).reshape(HEADS, size, length), axis=1), axis=1, keepdims=True)
        reach = jnp.max(query_norm * key_norm) * (scale * scale)
        calm[0] = jnp.where(reach <= SAFE * SAFE, 1, 0)

    group_rows = lax.broadcasted_iota(jnp.int32, (128, length), 0) // size

    def one_head(index, blocks, safe):
        head = step * heads_per_step + index
        block = head // (128 // size)
        inner = head - block * (128 // size)
        span = blocks * 128
        around = query_t[0, pl.ds(pl.multiple_of(block * 128, 128), 128), :]
        own = jnp.where(group_rows == inner, around, 0).astype(BF)
        keys = key_rows[block, :span, :]
        values = value_ext[pl.ds(pl.multiple_of(head * ext, 16), ext), :span]
        piece = length // 2
        for part in range(length // piece):
            cut = slice(part * piece, (part + 1) * piece)
            scores = nn(keys, own[:, cut]) * scale
            if not safe:
                place = lax.broadcasted_iota(jnp.int32, scores.shape, 0)
                scores = jnp.where(place < count, scores, -1e30)
                scores = scores - jnp.max(scores, axis=0, keepdims=True)
            weight = jnp.exp2(scores).astype(BF)
            kept[0, index, :span, cut] = weight
            summed = nn(values, weight)
            turned = 1.0 / summed[size : size + 1, :]
            mixed_t[0, pl.ds(pl.multiple_of(head * size, 32), size), cut] = (summed[:size] * turned).astype(BF)
            inverse[0, pl.ds(head, 1), cut] = turned

    blocks_used = (count + 127) // 128
    for blocks in range(1, length // 128 + 1):

        @pl.when((calm[0] == 1) & (blocks_used == blocks))
        def _(blocks=blocks):
            for index in range(heads_per_step):
                one_head(index, blocks, True)

    @pl.when(calm[0] == 0)
    def _():
        for index in range(heads_per_step):
            one_head(index, length // 128, False)


def norm_parts(field):
    middle = jnp.mean(field, axis=-1, keepdims=True)
    center = field - middle
    spread = jnp.mean(center * center, axis=-1, keepdims=True)
    pull = lax.rsqrt(spread + EPS)
    return center * pull, pull


def norm_back(grad, normal, pull):
    return (grad - jnp.mean(grad, axis=-1, keepdims=True) - normal * jnp.mean(grad * normal, axis=-1, keepdims=True)) * pull


def ffn_kernel(
    chunk, core, tokens, mixed_t, inverse, cotangent, near, far,
    layer_out, grad_first, mixed_grad_t, center, keep, send, grad_vectors, grad_up_bias,
    out_sum, up_sum, down_sum, vector_sum, hidden_all, slope_all,
):
    step = pl.program_id(0)
    rows, width = tokens.shape
    inner = hidden_all.shape[1]
    size = width // HEADS
    share = width // VIRTUAL
    part = inner // VIRTUAL

    @pl.when(step == 0)
    def _():
        out_sum[...] = jnp.zeros_like(out_sum)
        up_sum[...] = jnp.zeros_like(up_sum)
        down_sum[...] = jnp.zeros_like(down_sum)
        vector_sum[...] = jnp.zeros_like(vector_sum)

    vectors = near_vectors(near)
    out_bias, down_bias, first_gain, first_shift, second_gain, second_shift = [vectors[k : k + 1, :] for k in range(2, 8)]
    out_weight = jnp.concatenate([far[d, part : part + share, :] for d in range(VIRTUAL)], axis=0)

    def up_weight(start):
        lanes = []
        for lane in range(start // width, (start + chunk) // width):
            strip = slice(part + share * (lane + 1), part + share * (lane + 2))
            lanes.append(jnp.concatenate([far[d, strip, :] for d in range(VIRTUAL)], axis=0))
        return jnp.concatenate(lanes, axis=1)

    def down_weight(start):
        return jnp.concatenate([far[d, :part, :] for d in range(start // part, (start + chunk) // part)], axis=0)

    def up_bias(start):
        pieces = [near[d, 3 * share : 3 * share + 16, :].astype(F32)[8:9] for d in range(start // part, (start + chunk) // part)]
        return jnp.concatenate(pieces, axis=1)

    mixed = mixed_t[0].T
    first_sum = tokens[...].astype(F32) + nn(mixed, out_weight) + out_bias
    first_normal, first_pull = norm_parts(first_sum)
    first_norm = first_normal * first_gain + first_shift
    first_low = first_norm.astype(BF)
    second_sum = first_norm + down_bias
    root = math.sqrt(2.0 / math.pi)
    for start in range(0, inner, chunk):
        cut = slice(start, start + chunk)
        pre = nn(first_low, up_weight(start)) + up_bias(start)
        square = pre * pre
        bend = jnp.tanh(pre * (root + root * 0.044715 * square))
        half = 0.5 + 0.5 * bend
        hidden = (pre * half).astype(BF)
        slope_all[:, cut] = half + (0.5 * pre) * (1.0 - bend * bend) * (root + root * 3 * 0.044715 * square)
        hidden_all[:, cut] = hidden
        second_sum = second_sum + nn(hidden, down_weight(start))
    second_normal, second_pull = norm_parts(second_sum)
    layer_out[...] = (second_normal * second_gain + second_shift).astype(BF)
    wide = cotangent[...].astype(F32)
    grad_second = norm_back(wide * second_gain, second_normal, second_pull)
    ffn_grad = grad_second.astype(BF)
    ffn_grad_t = ffn_grad.T
    first_low_t = first_low.T
    ones = jnp.where(lax.broadcasted_iota(jnp.int32, (16, rows), 0) == 0, 1.0, 0.0).astype(BF)
    first_ext = jnp.concatenate([first_low_t, ones], axis=0)
    back = grad_second
    for start in range(0, inner, chunk):
        cut = slice(start, start + chunk)
        hidden_grad = (nt(ffn_grad, down_weight(start)) * slope_all[:, cut]).astype(BF)
        down_sum[:, cut] += nn(ffn_grad_t, hidden_all[:, cut])
        up_sum[:, cut] += nn(first_ext, hidden_grad)
        back = back + nt(hidden_grad, up_weight(start))
    first = norm_back(back * first_gain, first_normal, first_pull)
    grad_first[...] = first
    branch_grad = first.astype(BF)
    out_sum[...] += nn(mixed_t[0], branch_grad)
    mixed_grad = nt(out_weight, branch_grad).reshape(HEADS, size, rows)
    turned = inverse[0]
    scaled = (mixed_grad * turned[:, None, :]).astype(BF)
    mixed_grad_t[0] = scaled.reshape(width, rows)
    center[0] = jnp.sum(scaled.astype(F32) * mixed_t[0].astype(F32).reshape(HEADS, size, rows), axis=1)
    sums = (
        branch_grad.astype(F32), ffn_grad.astype(F32), back * first_normal, back, wide * second_normal, wide,
    )
    vector_sum[...] += jnp.concatenate(
        [jnp.zeros((2, width), F32)] + [jnp.sum(piece, axis=0, keepdims=True) for piece in sums], axis=0
    )

    @pl.when(step == pl.num_programs(0) - 1)
    def _():
        for slot in range(VIRTUAL // 2):
            for ref, side in ((keep, core[0]), (send, 1 - core[0])):
                owner = 2 * slot + side
                strip = pl.ds(pl.multiple_of(owner * share, share), share)
                ref[slot, 0:share, :] = out_sum[strip, :].astype(BF)
                for lane in range(inner // width):
                    ref[slot, share * (lane + 1) : share * (lane + 2), :] = up_sum[strip, lane * width : (lane + 1) * width].astype(BF)
                turned_down = down_sum[:, pl.ds(pl.multiple_of(owner * part, part), part)].astype(BF)
                ref[slot, share + share * (inner // width) :, :] = turned_down.T
        for d in range(VIRTUAL):
            grad_up_bias[d : d + 1, :] = up_sum[width : width + 1, d * part : (d + 1) * part]
        grad_vectors[...] = vector_sum[...]


def backward_kernel(
    heads_per_step, first_unit, used, kept, value_rows, key_t, query_t, mixed_grad_t, center, *refs
):
    query_grad_t, key_grad_t, value_grad_t = refs[-3:]
    steps = HEADS // heads_per_step
    unit = pl.program_id(0) + first_unit
    image = unit // steps
    step = unit - image * steps
    width, length = query_t.shape[1:]
    size = width // HEADS
    scale = size ** (-0.5)
    count = used[image]
    blocks_used = (count + 127) // 128
    group_rows = lax.broadcasted_iota(jnp.int32, (128, length), 0) // size

    def one_head(index, blocks):
        head = step * heads_per_step + index
        block = head // (128 // size)
        inner = head - block * (128 // size)
        span = blocks * 128
        head_rows = pl.ds(pl.multiple_of(head * size, 32), size)
        own_rows = slice(index * size, (index + 1) * size)
        around = mixed_grad_t[0, pl.ds(pl.multiple_of(block * 128, 128), 128), :]
        own = jnp.where(group_rows == inner, around, 0).astype(BF)
        values = value_rows[0, block, :span, :]
        keys = key_t[0, head_rows, :span]
        value_sum = jnp.zeros((size, span), F32)
        key_sum = jnp.zeros((size, span), F32)
        piece = length // 2
        for part in range(length // piece):
            cut = slice(part * piece, (part + 1) * piece)
            pulled = nn(values, own[:, cut]) - center[0, pl.ds(head, 1), cut]
            weight = kept[0, index, :span, cut]
            score_grad = (weight.astype(F32) * pulled).astype(BF)
            query_grad_t[0, own_rows, cut] = (nn(keys, score_grad) * scale).astype(BF)
            value_sum = value_sum + nt(mixed_grad_t[0, head_rows, cut], weight)
            key_sum = key_sum + nt(query_t[0, head_rows, cut], score_grad)
        valid = lax.broadcasted_iota(jnp.int32, (size, span), 1) < count
        value_grad_t[0, own_rows, :span] = jnp.where(valid, value_sum, 0.0).astype(BF)
        key_grad_t[0, own_rows, :span] = jnp.where(valid, key_sum * scale, 0.0).astype(BF)
        if span < length:
            value_grad_t[0, own_rows, span:] = jnp.zeros((size, length - span), BF)
            key_grad_t[0, own_rows, span:] = jnp.zeros((size, length - span), BF)

    for blocks in range(1, length // 128 + 1):

        @pl.when(blocks_used == blocks)
        def _(blocks=blocks):
            for index in range(heads_per_step):
                one_head(index, blocks)


def weights_kernel(
    core, lifted_t, lifted_ct, tokens_ct, query_grad_t, key_grad_t, value_grad_t, early_vectors, up_bias,
    keep, send, sums, vector_sum,
):
    image = pl.program_id(0)
    length = lifted_t.shape[2]
    width = lifted_t.shape[1]
    share = width // VIRTUAL

    @pl.when(image == 0)
    def _():
        sums[...] = jnp.zeros_like(sums)
        vector_sum[...] = early_vectors[...]

    ones = jnp.ones((16, length), BF)
    query_sum = nt(jnp.concatenate([lifted_t[0], ones], axis=0), query_grad_t[0])
    value_sum = nt(jnp.concatenate([tokens_ct[0], ones], axis=0), value_grad_t[0])
    sums[0] += query_sum[:width]
    sums[1] += nt(lifted_ct[0], key_grad_t[0])
    sums[2] += value_sum[:width]
    vector_sum[0:1, :] += query_sum[width : width + 1]
    vector_sum[1:2, :] += value_sum[width : width + 1]

    @pl.when(image == pl.num_programs(0) - 1)
    def _():
        for slot in range(VIRTUAL // 2):
            for ref, side in ((keep, core[0]), (send, 1 - core[0])):
                owner = 2 * slot + side
                strip = pl.ds(pl.multiple_of(owner * share, share), share)
                for k in range(3):
                    ref[slot, k * share : (k + 1) * share, :] = sums[k, strip, :].astype(BF)
                bias = jnp.broadcast_to(up_bias[pl.ds(owner, 1), :], (8, width))
                ref[slot, 3 * share :, :] = jnp.concatenate([vector_sum[...], bias], axis=0).astype(BF)


def finish_kernel(place, *refs):
    pieces, (grad_out, grad_up, grad_down, total) = refs[:-4], refs[-4:]
    share = grad_out.shape[0]
    width = grad_out.shape[1]
    lanes = grad_up.shape[1] // width
    size = total.shape[0] // len(pieces)
    for far, piece in enumerate(pieces):
        owner = place[0] ^ far
        total[pl.ds(pl.multiple_of(owner * size, 8), size), :] = piece[...].astype(F32)
    grad_out[...] = total[:share]
    for lane in range(lanes):
        grad_up[:, lane * width : (lane + 1) * width] = total[share * (lane + 1) : share * (lane + 2)]
    grad_down[...] = total[share * (lanes + 1) :]


def tokens_kernel(first, rank, grad_first, near, query_grad_t, key_grad_t, value_grad_t, *refs):
    grad_tokens = refs[-1]
    image = pl.program_id(0) + first
    length = query_grad_t.shape[2]
    width = query_grad_t.shape[1]
    compact = lax.broadcasted_iota(jnp.int32, (length, length), 0)
    chosen = jnp.where(compact == rank[pl.ds(image, 1), :], 1.0, 0.0).astype(BF)
    both = nn(jnp.concatenate([key_grad_t[0], value_grad_t[0]], axis=0), chosen).astype(BF)
    weights = [near_weight(near, k) for k in range(3)]
    total_t = nn(weights[0], query_grad_t[0]) + nn(weights[1], both[:width]) + nn(weights[2], both[width:])
    grad_tokens[0] = grad_first[0] + total_t.T


def params(*semantics):
    return pltpu.CompilerParams(dimension_semantics=semantics, vmem_limit_bytes=VMEM_LIMIT)


def cost(microseconds):
    return pl.CostEstimate(flops=int(microseconds * 1.0e9), bytes_accessed=1 << 20, transcendentals=0)


def whole(shape):
    return pl.BlockSpec(shape, lambda *_: (0,) * len(shape))


def per_image(shape):
    return pl.BlockSpec((1,) + shape, lambda i, *_: (i,) + (0,) * len(shape))


def scalars():
    return pl.BlockSpec(memory_space=SMEM)


def shaped(shape, dtype):
    return jax.ShapeDtypeStruct(shape, dtype)


def exchange_dp(field, dp):
    return lax.all_to_all(jnp.broadcast_to(field, (dp,) + field.shape), "dp", 0, 0, tiled=True)


def same_core(zero):
    return [[k for k in range(zero) if k % 2 == side] for side in range(2)]


def swap_cores(send, zero):
    return lax.ppermute(send, "zero", [(k, k ^ 1) for k in range(zero)])


def by_owner(keep, send):
    return jnp.stack([keep, send], axis=1).reshape((VIRTUAL,) + keep.shape[1:])


def body(
    tokens, counts, key_mask, rotation, token_order, query_weight, key_weight, value_weight, out_weight, up_weight,
    down_weight, query_bias, value_bias, out_bias, up_bias, down_bias, first_gain, first_shift, second_gain,
    second_shift, cotangent, *, zero, dp,
):
    images, length, width = tokens.shape
    rows = images * length
    inner = up_weight.shape[1]
    share = width // zero
    inner_share = inner // zero
    direct = zero == VIRTUAL
    heads_per_step = 2
    steps = HEADS // heads_per_step
    me = lax.axis_index("zero")
    core = (me % 2 if direct else me * 0).astype(jnp.int32).reshape(1)

    small = [query_bias, value_bias, out_bias, down_bias, first_gain, first_shift, second_gain, second_shift]
    near_rows = 3 * (width // VIRTUAL) + 16
    far_rows = (2 * inner + width) // VIRTUAL
    if direct:
        near, far = pl.pallas_call(
            pack_kernel,
            in_specs=[scalars()] + [pl.BlockSpec(memory_space=pltpu.VMEM)] * 15,
            out_shape=[shaped((zero, near_rows, width), BF), shaped((zero, far_rows, width), BF)],
            scratch_shapes=[pltpu.VMEM((8, share), F32)],
            name="pack",
        )(me.astype(jnp.int32).reshape(1), query_weight, key_weight, value_weight, out_weight, down_weight, up_weight, *small, up_bias)
        near = lax.all_to_all(near, "zero", 0, 0, tiled=True)
        far = lax.all_to_all(far, "zero", 0, 0, tiled=True)
    else:
        gather = functools.partial(lax.all_gather, axis_name="zero", axis=0, tiled=True)
        shards = [gather(w).reshape(VIRTUAL, -1, width) for w in (query_weight, key_weight, value_weight)]
        vectors = jnp.zeros((VIRTUAL, 8, width), BF).at[0].set(jnp.stack([gather(v) for v in small]))
        biases = jnp.broadcast_to(gather(up_bias).reshape(VIRTUAL, 1, inner // VIRTUAL), (VIRTUAL, 8, inner // VIRTUAL))
        near = jnp.concatenate(shards + [vectors, biases], axis=1)
        lanes = gather(up_weight).reshape(VIRTUAL, width // VIRTUAL, inner // width, width).transpose(0, 2, 1, 3)
        shards = [gather(w).reshape(VIRTUAL, -1, width) for w in (down_weight, out_weight)]
        far = jnp.concatenate(shards + [lanes.reshape(VIRTUAL, -1, width)], axis=1)

    table = jnp.asarray(position_table(GRID, width))
    turned = shaped((images, width, length), BF)
    lifted_t, lifted_ct, tokens_ct, rank, used = pl.pallas_call(
        prep_kernel,
        grid=(images,),
        in_specs=[
            scalars(), scalars(), per_image((length, width)), whole((images, length)), whole((images, length)),
            whole(table.shape),
        ],
        out_specs=[per_image((width, length))] * 3 + [whole((images, length)), scalars()],
        out_shape=[turned] * 3 + [shaped((images, length), jnp.int32), shaped((images,), jnp.int32)],
        compiler_params=params("arbitrary"),
        name="prep",
    )(counts, rotation, tokens, key_mask, token_order, table)

    head_block = pl.BlockSpec((1, heads_per_step, length, length), lambda i, s: (i, s, 0, 0))
    kept, mixed_t, inverse, query_t, key_t, value_rows = pl.pallas_call(
        functools.partial(forward_kernel, heads_per_step),
        grid=(images, steps),
        in_specs=[scalars()] + [per_image((width, length))] * 3 + [whole(near.shape)],
        out_specs=[
            head_block, per_image((width, length)), per_image((HEADS, length)), per_image((width, length)),
            per_image((width, length)), per_image((width // 128, length, 128)),
        ],
        out_shape=[
            shaped((images, HEADS, length, length), BF), turned, shaped((images, HEADS, length), F32), turned, turned,
            shaped((images, width // 128, length, 128), BF),
        ],
        scratch_shapes=[
            pltpu.VMEM((width // 128, length, 128), BF),
            pltpu.VMEM((width + 16 * HEADS, length), BF),
            pltpu.SMEM((1,), jnp.int32),
        ],
        compiler_params=params("arbitrary", "arbitrary"),
        cost_estimate=cost(22),
        name="attend_forward",
    )(used, lifted_t, lifted_ct, tokens_ct, near)

    block = length // 2
    per = length // block
    row_block = pl.BlockSpec((block, width), lambda s: (s, 0))

    def turned_block(height):
        return pl.BlockSpec((1, height, block), lambda s: (s // per, 0, s % per))

    early_rows = (width + 2 * inner) // VIRTUAL
    half = shaped((VIRTUAL // 2, early_rows, width), BF)
    layer_out, grad_first, mixed_grad_t, center, keep, send, grad_vectors, grad_up_bias = pl.pallas_call(
        functools.partial(ffn_kernel, 512),
        grid=(rows // block,),
        in_specs=[
            scalars(), row_block, turned_block(width), turned_block(HEADS), row_block, whole(near.shape), whole(far.shape),
        ],
        out_specs=[
            row_block, row_block, turned_block(width), turned_block(HEADS), whole(half.shape), whole(half.shape),
            whole((8, width)), whole((VIRTUAL, inner // VIRTUAL)),
        ],
        out_shape=[
            shaped((rows, width), BF), shaped((rows, width), F32), turned, shaped((images, HEADS, length), F32),
            half, half, shaped((8, width), F32), shaped((VIRTUAL, inner // VIRTUAL), F32),
        ],
        scratch_shapes=[
            pltpu.VMEM((width, width), F32), pltpu.VMEM((width + 16, inner), F32), pltpu.VMEM((width, inner), F32),
            pltpu.VMEM((8, width), F32), pltpu.VMEM((block, inner), BF), pltpu.VMEM((block, inner), F32),
        ],
        compiler_params=params("arbitrary"),
        cost_estimate=cost(27),
        name="feed_forward",
    )(core, tokens.reshape(rows, width), mixed_t, inverse, cotangent.reshape(rows, width), near, far)

    units = images * steps
    unit_rows = shaped((units, heads_per_step * (width // HEADS), length), BF)

    def attend_backward(first, last, center, before):
        def unit_block(shape, index):
            return pl.BlockSpec((1,) + shape, lambda u: index(u + first))

        image = lambda u: (u // steps, 0, 0)
        grad_block = unit_block(unit_rows.shape[1:], lambda u: (u, 0, 0))
        return pl.pallas_call(
            functools.partial(backward_kernel, heads_per_step, first),
            grid=(last - first,),
            in_specs=[
                scalars(),
                unit_block((heads_per_step, length, length), lambda u: (u // steps, u % steps, 0, 0)),
                unit_block((width // 128, length, 128), lambda u: (u // steps, 0, 0, 0)),
            ]
            + [unit_block((width, length), image)] * 3
            + [unit_block((HEADS, length), image)]
            + [pl.BlockSpec(memory_space=pl.ANY)] * len(before),
            out_specs=[grad_block] * 3,
            out_shape=[unit_rows] * 3,
            input_output_aliases={7 + k: k for k in range(len(before))},
            compiler_params=params("arbitrary"),
            cost_estimate=cost(1),
            name="attend_backward",
        )(used, kept, value_rows, key_t, query_t, mixed_grad_t, center, *before)

    cuts = (units // 8, units * 5 // 8)
    if direct:
        came = swap_cores(send, zero)
        grads = attend_backward(0, cuts[0], center, ())
        came, grads = lax.optimization_barrier((came, grads))
        merged = (keep.astype(F32) + came.astype(F32)).astype(BF)
        shuffled = lax.all_to_all(merged, "zero", 0, 0, tiled=True, axis_index_groups=same_core(zero))
        merged, center = lax.optimization_barrier((merged, center))
        grads = attend_backward(cuts[0], cuts[1], center, grads)
        shuffled, grads = lax.optimization_barrier((shuffled, grads))
        early = jnp.sum(shuffled.astype(F32), axis=0).astype(BF)
        early, grads = lax.optimization_barrier((early, grads))
        early = lax.all_to_all(early.reshape(dp, early_rows // dp, width), "dp", 0, 0, tiled=True)
        grads = attend_backward(cuts[1], units, center, grads)
        early, grads = lax.optimization_barrier((early, grads))
        early = jnp.sum(early.astype(F32), axis=0).astype(BF)
        early = [early] + [lax.ppermute(early, "dp", [(k, k ^ far) for k in range(dp)]) for far in range(1, dp)]
    else:
        grads = attend_backward(0, units, center, ())
        halves = by_owner(keep, send)
        strip = width // VIRTUAL
        lanes = inner // width
        grad_out = halves[:, :strip].reshape(zero, share, width)
        grad_up = halves[:, strip : strip * (lanes + 1)].reshape(VIRTUAL, lanes, strip, width).transpose(0, 2, 1, 3)
        grad_up = grad_up.reshape(zero, share, lanes, width).transpose(0, 2, 1, 3).reshape(zero, share * lanes, width)
        grad_down = halves[:, strip * (lanes + 1) :].reshape(zero, inner_share, width)
        early = jnp.concatenate([grad_out, grad_up, grad_down], axis=1)
        early = jnp.sum(lax.all_to_all(early, "zero", 0, 0, tiled=True).astype(F32), axis=0).astype(BF)
        early = exchange_dp(early, dp)
    query_grad_t, key_grad_t, value_grad_t = [g.reshape(images, width, length) for g in grads]

    late_half = shaped((VIRTUAL // 2, near_rows, width), BF)
    keep, send = pl.pallas_call(
        weights_kernel,
        grid=(images,),
        in_specs=[scalars()] + [per_image((width, length))] * 6 + [whole((8, width)), whole((VIRTUAL, inner // VIRTUAL))],
        out_specs=[whole(late_half.shape)] * 2,
        out_shape=[late_half] * 2,
        scratch_shapes=[pltpu.VMEM((3, width, width), F32), pltpu.VMEM((8, width), F32)],
        compiler_params=params("arbitrary"),
        cost_estimate=cost(1),
        name="weight_grads",
    )(core, lifted_t, lifted_ct, tokens_ct, query_grad_t, key_grad_t, value_grad_t, grad_vectors, grad_up_bias)

    def token_grads(first, last, rank, before):
        def own(shape):
            return pl.BlockSpec((1,) + shape, lambda i: (i + first, 0, 0))

        return pl.pallas_call(
            functools.partial(tokens_kernel, first),
            grid=(last - first,),
            in_specs=[whole((images, length)), own((length, width)), whole(near.shape)]
            + [own((width, length))] * 3
            + [pl.BlockSpec(memory_space=pl.ANY)] * len(before),
            out_specs=own((length, width)),
            out_shape=shaped((images, length, width), F32),
            input_output_aliases={6: 0} if before else {},
            compiler_params=params("arbitrary"),
            cost_estimate=cost(1),
            name="token_grads",
        )(rank, grad_first.reshape(images, length, width), near, query_grad_t, key_grad_t, value_grad_t, *before)

    if direct:
        came = swap_cores(send, zero)
        merged = (keep.astype(F32) + came.astype(F32)).astype(BF)
        late = lax.all_to_all(merged, "zero", 0, 0, tiled=True, axis_index_groups=same_core(zero))
        late = jnp.sum(late.astype(F32), axis=0).astype(BF)
        start = me * share
        grad_tokens = token_grads(0, images // 2, rank, ())
        late, early, rank = lax.optimization_barrier((late, early, rank))
        grad_tokens = token_grads(images // 2, images, rank, (grad_tokens,))
    else:
        halves = by_owner(keep, send)
        strip = width // VIRTUAL
        three = halves[:, : 3 * strip].reshape(VIRTUAL, 3, strip, width).transpose(1, 0, 2, 3).reshape(3, zero, share, width)
        three = three.transpose(1, 0, 2, 3).reshape(zero, 3 * share, width)
        vectors = halves[:, 3 * strip : 3 * strip + 8].reshape(VIRTUAL, 8, width)[0]
        vectors = vectors.reshape(8, zero, share).transpose(1, 0, 2)
        vectors = jnp.pad(vectors, ((0, 0), (0, 0), (0, width - share)))
        bias = jnp.pad(halves[:, -1].reshape(zero, 1, inner_share), ((0, 0), (0, 7), (0, width - inner_share)))
        late = jnp.concatenate([three, vectors, bias], axis=1)
        late = jnp.sum(lax.all_to_all(late, "zero", 0, 0, tiled=True).astype(F32), axis=0).astype(BF)
        start = me * 0
        grad_tokens = token_grads(0, images, rank, ())
    late = jnp.sum(exchange_dp(late, dp).astype(F32), axis=0)

    own_shapes = [shaped((share, width), F32), shaped((share, inner), F32), shaped((inner_share, width), F32)]
    if direct:
        grad_out_own, grad_up_own, grad_down_own = pl.pallas_call(
            finish_kernel,
            in_specs=[scalars()] + [pl.BlockSpec(memory_space=pltpu.VMEM)] * dp,
            out_shape=own_shapes,
            scratch_shapes=[pltpu.VMEM((early_rows, width), F32)],
            compiler_params=pltpu.CompilerParams(vmem_limit_bytes=16 << 20),
            name="finish",
        )(lax.axis_index("dp").astype(jnp.int32).reshape(1), *early)
    else:
        lanes = inner // width
        total = jnp.sum(early.astype(F32), axis=0)
        grad_out_own = total[:share]
        grad_up_own = total[share : share * (lanes + 1)].reshape(lanes, share, width).transpose(1, 0, 2).reshape(share, inner)
        grad_down_own = total[share * (lanes + 1) :]
    cuts = [lax.dynamic_slice(late, (3 * share + k, start), (1, share)).reshape(share) for k in range(8)]
    up_bias_own = late[3 * share + 8, :inner_share]
    return (
        layer_out.reshape(images, length, width),
        grad_tokens,
        late[:share],
        late[share : 2 * share],
        late[2 * share : 3 * share],
        grad_out_own,
        grad_up_own,
        grad_down_own,
        cuts[0],
        cuts[1],
        cuts[2],
        up_bias_own,
        cuts[3],
        cuts[4],
        cuts[5],
        cuts[6],
        cuts[7],
    )


def solution(mesh):
    batch = P(("dp", "zero"))
    wide = P(("dp", "zero"), None, None)
    flat = P(("dp", "zero"), None)
    matrix = P("zero", None)
    vector = P("zero")
    in_specs = (wide, batch, flat, batch, flat) + (matrix,) * 6 + (vector,) * 9 + (wide,)
    out_specs = (wide, wide) + (matrix,) * 6 + (vector,) * 9
    run = functools.partial(body, zero=mesh.shape["zero"], dp=mesh.shape["dp"])
    return jax.shard_map(run, mesh=mesh, in_specs=in_specs, out_specs=out_specs, check_vma=False)
```

```python
import functools
import math

import jax
import jax.numpy as jnp
import numpy as np
from jax import lax
from jax.experimental import pallas as pl
from jax.experimental.pallas import tpu as pltpu
from jax.sharding import PartitionSpec as P

HEADS = 8
GRID = 32
EPS = 1e-05
LOG2E = 1.4426950408889634
SAFE = 60.0

BF = jnp.bfloat16
F32 = jnp.float32
SMEM = pltpu.SMEM
VIRTUAL = 8


def nn(left, right):
    return lax.dot_general(left, right, (((1,), (0,)), ((), ())), preferred_element_type=F32)


def nt(left, right):
    return lax.dot_general(left, right, (((1,), (1,)), ((), ())), preferred_element_type=F32)


def position_table(grid, width):
    half = width // 2
    index = np.arange(half)
    freq = np.power(np.float32(10000.0), (2 * (index // 2)).astype(np.float32) / np.float32(half)).astype(np.float32)
    coord = np.arange(grid).astype(np.float32)
    angle = ((coord + np.float32(1.0)) / np.float32(grid + 1e-06) * np.float32(2.0 * math.pi)).astype(np.float32)
    angle = (angle[:, None] / freq).astype(np.float32)
    table = np.where(index % 2 == 0, np.sin(angle), np.cos(angle)).astype(np.float32)
    high = table.astype(BF)
    rest = (table - high.astype(np.float32)).astype(BF)
    whole = np.zeros((4 * grid, width), dtype=BF)
    for group, piece in enumerate((high, high, rest, rest)):
        start = (group % 2) * half
        whole[group * grid : (group + 1) * grid, start : start + half] = piece
    return np.ascontiguousarray(whole.T)


def pack_kernel(where, query, key, value, *refs):
    vectors, up_bias, near, stack = refs[:8], refs[8], refs[9], refs[10]
    share, width = query.shape
    for k, vector in enumerate(vectors):
        stack[k : k + 1, :] = vector[...].astype(F32).reshape(1, share)
    place = lax.broadcasted_iota(jnp.int32, (share, width), 1) - where[0] * share
    spread = jnp.where(place == lax.broadcasted_iota(jnp.int32, (share, width), 0), 1.0, 0.0).astype(BF)
    rows = nn(stack[...].astype(BF), spread)
    bias = jnp.broadcast_to(up_bias[...].astype(F32).reshape(1, width), (8, width))
    last = jnp.concatenate([rows, bias], axis=0).astype(BF)
    for d in range(near.shape[0]):
        near[d, 0:share, :] = query[...]
        near[d, share : 2 * share, :] = key[...]
        near[d, 2 * share : 3 * share, :] = value[...]
        near[d, 3 * share :, :] = last


def prep_kernel(
    counts, rotation, tokens, key_mask, token_order, table, out, down, up,
    lifted_t, lifted_ct, tokens_ct, rank_out, used, *far,
):
    image = pl.program_id(0)
    length = tokens.shape[1]
    slot = lax.broadcasted_iota(jnp.int32, (1, length), 1)
    mask = key_mask[pl.ds(image, 1), :]
    usable = (slot < counts[image]) & ((mask == 1) | (slot == 0))
    flag = jnp.where(usable, 1, 0)
    used[image] = jnp.sum(flag)
    total = flag
    step = 1
    while step < length:
        total = total + jnp.where(slot >= step, pltpu.roll(total, step, 1), 0)
        step *= 2
    rank = jnp.where(usable, total - 1, -1)
    rank_out[pl.ds(image, 1), :] = rank
    cell = token_order[pl.ds(image, 1), :]
    row = cell // GRID
    column = cell - row * GRID
    turn = rotation[image]
    last = GRID - 1
    ycoord = jnp.where(turn == 0, row, jnp.where(turn == 1, column, jnp.where(turn == 2, last - row, last - column)))
    xcoord = jnp.where(turn == 0, column, jnp.where(turn == 1, last - row, jnp.where(turn == 2, last - column, row)))
    place = lax.broadcasted_iota(jnp.int32, (4 * GRID, length), 0)
    group = place // GRID
    wanted = jnp.where(group % 2 == 0, ycoord, xcoord)
    hot = jnp.where(place - group * GRID == wanted, 1.0, 0.0).astype(BF)
    pos_t = nn(table[...], hot)
    tokens_t = tokens[0].T
    low_t = (tokens_t.astype(F32) + pos_t).astype(BF)
    lifted_t[0] = low_t
    compact = lax.broadcasted_iota(jnp.int32, (length, length), 0)
    chosen = jnp.where(compact == rank, 1.0, 0.0).astype(BF)
    lifted_ct[0] = nt(low_t, chosen).astype(BF)
    tokens_ct[0] = nt(tokens_t, chosen).astype(BF)
    if far:

        @pl.when(image == 0)
        def _():
            (bundle,) = far
            share, width = out.shape
            for d in range(bundle.shape[0]):
                bundle[d, 0 : down.shape[0], :] = down[...]
                bundle[d, down.shape[0] : down.shape[0] + share, :] = out[...]
                for lane in range(up.shape[1] // width):
                    start = down.shape[0] + share * (lane + 1)
                    bundle[d, start : start + share, :] = up[:, lane * width : (lane + 1) * width]


def near_weight(near, k):
    share = near.shape[2] // VIRTUAL
    return jnp.concatenate([near[d, k * share : (k + 1) * share, :] for d in range(VIRTUAL)], axis=0)


def near_vectors(near):
    share = near.shape[2] // VIRTUAL
    total = near[0, 3 * share : 3 * share + 16, :].astype(F32)
    for d in range(1, VIRTUAL):
        total = total + near[d, 3 * share : 3 * share + 16, :].astype(F32)
    return total[:8]


def forward_kernel(
    heads_per_step, used, lifted_t, lifted_ct, tokens_ct, near,
    kept, mixed_t, inverse, query_t, key_t, value_rows, key_rows, value_ext, calm,
):
    image = pl.program_id(0)
    step = pl.program_id(1)
    width, length = query_t.shape[1:]
    size = width // HEADS
    ext = size + 16
    scale = LOG2E * size ** (-0.5)
    count = used[image]

    @pl.when(step == 0)
    def _():
        weights = [near_weight(near, k) for k in range(3)]
        columns = near_vectors(near).T
        query = (nn(weights[0].T, lifted_t[0]) + columns[:, 0:1]).astype(BF)
        query_t[0] = query
        key = nn(weights[1].T, lifted_ct[0]).astype(BF)
        key_t[0] = key
        value = (nn(weights[2].T, tokens_ct[0]) + columns[:, 1:2]).astype(BF)
        key_turned = key.T
        value_turned = value.T
        for block in range(width // 128):
            part = slice(block * 128, (block + 1) * 128)
            key_rows[block] = key_turned[:, part]
            value_rows[0, block] = value_turned[:, part]
        valid = lax.broadcasted_iota(jnp.int32, (size, length), 1) < count
        first = lax.broadcasted_iota(jnp.int32, (16, length), 0) == 0
        ones = jnp.where(first & valid[:16], 1.0, 0.0).astype(BF)
        for head in range(HEADS):
            value_ext[head * ext : head * ext + size, :] = jnp.where(valid, value[head * size : (head + 1) * size], 0).astype(BF)
            value_ext[head * ext + size : (head + 1) * ext, :] = ones
        wide_query = query.astype(F32)
        wide_key = key.astype(F32)
        query_norm = jnp.max(jnp.sum((wide_query * wide_query).reshape(HEADS, size, length), axis=1), axis=1, keepdims=True)
        key_norm = jnp.max(jnp.sum((wide_key * wide_key).reshape(HEADS, size, length), axis=1), axis=1, keepdims=True)
        reach = jnp.max(query_norm * key_norm) * (scale * scale)
        calm[0] = jnp.where(reach <= SAFE * SAFE, 1, 0)

    group_rows = lax.broadcasted_iota(jnp.int32, (128, length), 0) // size

    def one_head(index, blocks, safe):
        head = step * heads_per_step + index
        block = head // (128 // size)
        inner = head - block * (128 // size)
        span = blocks * 128
        around = query_t[0, pl.ds(pl.multiple_of(block * 128, 128), 128), :]
        own = jnp.where(group_rows == inner, around, 0).astype(BF)
        keys = key_rows[block, :span, :]
        values = value_ext[pl.ds(pl.multiple_of(head * ext, 16), ext), :span]
        piece = length // 2
        for part in range(length // piece):
            cut = slice(part * piece, (part + 1) * piece)
            scores = nn(keys, own[:, cut]) * scale
            if not safe:
                place = lax.broadcasted_iota(jnp.int32, scores.shape, 0)
                scores = jnp.where(place < count, scores, -1e30)
                scores = scores - jnp.max(scores, axis=0, keepdims=True)
            weight = jnp.exp2(scores).astype(BF)
            kept[0, index, :span, cut] = weight
            summed = nn(values, weight)
            turned = 1.0 / summed[size : size + 1, :]
            mixed_t[0, pl.ds(pl.multiple_of(head * size, 32), size), cut] = (summed[:size] * turned).astype(BF)
            inverse[0, pl.ds(head, 1), cut] = turned

    blocks_used = (count + 127) // 128
    for blocks in range(1, length // 128 + 1):

        @pl.when((calm[0] == 1) & (blocks_used == blocks))
        def _(blocks=blocks):
            for index in range(heads_per_step):
                one_head(index, blocks, True)

    @pl.when(calm[0] == 0)
    def _():
        for index in range(heads_per_step):
            one_head(index, length // 128, False)


def norm_parts(field):
    middle = jnp.mean(field, axis=-1, keepdims=True)
    center = field - middle
    spread = jnp.mean(center * center, axis=-1, keepdims=True)
    pull = lax.rsqrt(spread + EPS)
    return center * pull, pull


def norm_back(grad, normal, pull):
    return (grad - jnp.mean(grad, axis=-1, keepdims=True) - normal * jnp.mean(grad * normal, axis=-1, keepdims=True)) * pull


def ffn_kernel(
    chunk, core, tokens, mixed_t, inverse, cotangent, near, far, far_other,
    layer_out, grad_first, mixed_grad_t, center, keep, send, grad_vectors, grad_up_bias,
    out_sum, up_sum, down_sum, vector_sum, hidden_all, slope_all, up_weight, down_weight, out_weight, up_bias,
):
    step = pl.program_id(0)
    rows, width = tokens.shape
    inner = hidden_all.shape[1]
    size = width // HEADS
    share = width // VIRTUAL
    part = inner // VIRTUAL

    @pl.when(step == 0)
    def _():
        out_sum[...] = jnp.zeros_like(out_sum)
        up_sum[...] = jnp.zeros_like(up_sum)
        down_sum[...] = jnp.zeros_like(down_sum)
        vector_sum[...] = jnp.zeros_like(vector_sum)
        for slot in range(VIRTUAL // 2):
            for ref, side in ((far, core[0]), (far_other, 1 - core[0])):
                owner = 2 * slot + side
                strip = pl.ds(pl.multiple_of(owner * share, share), share)
                down_weight[pl.ds(pl.multiple_of(owner * part, part), part), :] = ref[slot, :part, :]
                out_weight[strip, :] = ref[slot, part : part + share, :]
                for lane in range(inner // width):
                    cut = slice(part + share * (lane + 1), part + share * (lane + 2))
                    up_weight[strip, lane * width : (lane + 1) * width] = ref[slot, cut, :]
        for d in range(VIRTUAL):
            up_bias[:, d * part : (d + 1) * part] = near[d, 3 * share : 3 * share + 16, :].astype(F32)[8:9]

    vectors = near_vectors(near)
    out_bias, down_bias, first_gain, first_shift, second_gain, second_shift = [vectors[k : k + 1, :] for k in range(2, 8)]
    mixed = mixed_t[0].T
    first_sum = tokens[...].astype(F32) + nn(mixed, out_weight[...]) + out_bias
    first_normal, first_pull = norm_parts(first_sum)
    first_norm = first_normal * first_gain + first_shift
    first_low = first_norm.astype(BF)
    second_sum = first_norm + down_bias
    root = math.sqrt(2.0 / math.pi)
    for start in range(0, inner, chunk):
        cut = slice(start, start + chunk)
        pre = (nn(first_low, up_weight[:, cut]) + up_bias[:, cut]).astype(BF)
        square = pre * pre
        gate = jnp.bfloat16(0.5) + jnp.bfloat16(0.5) * jnp.tanh(pre * (jnp.bfloat16(root) + jnp.bfloat16(root * 0.044715) * square))
        hidden = pre * gate
        slope_all[:, cut] = gate + hidden * (jnp.bfloat16(1.0) - gate) * (jnp.bfloat16(2.0 * root) + jnp.bfloat16(6.0 * root * 0.044715) * square)
        hidden_all[:, cut] = hidden
        second_sum = second_sum + nn(hidden, down_weight[cut, :])
    second_normal, second_pull = norm_parts(second_sum)
    layer_out[...] = (second_normal * second_gain + second_shift).astype(BF)
    wide = cotangent[...].astype(F32)
    grad_second = norm_back(wide * second_gain, second_normal, second_pull)
    ffn_grad = grad_second.astype(BF)
    ffn_grad_t = ffn_grad.T
    first_low_t = first_low.T
    ones = jnp.where(lax.broadcasted_iota(jnp.int32, (16, rows), 0) == 0, 1.0, 0.0).astype(BF)
    first_ext = jnp.concatenate([first_low_t, ones], axis=0)
    back = grad_second
    for start in range(0, inner, chunk):
        cut = slice(start, start + chunk)
        hidden_grad = nt(ffn_grad, down_weight[cut, :]).astype(BF) * slope_all[:, cut]
        down_sum[:, cut] += nn(ffn_grad_t, hidden_all[:, cut])
        up_sum[:, cut] += nn(first_ext, hidden_grad)
        back = back + nt(hidden_grad, up_weight[:, cut])
    first = norm_back(back * first_gain, first_normal, first_pull)
    grad_first[...] = first
    branch_grad = first.astype(BF)
    out_sum[...] += nn(mixed_t[0], branch_grad)
    mixed_grad = nt(out_weight[...], branch_grad).reshape(HEADS, size, rows)
    turned = inverse[0]
    scaled = (mixed_grad * turned[:, None, :]).astype(BF)
    mixed_grad_t[0] = scaled.reshape(width, rows)
    center[0] = jnp.sum(scaled.astype(F32) * mixed_t[0].astype(F32).reshape(HEADS, size, rows), axis=1)
    sums = (
        branch_grad.astype(F32), ffn_grad.astype(F32), back * first_normal, back, wide * second_normal, wide,
    )
    vector_sum[...] += jnp.concatenate(
        [jnp.zeros((2, width), F32)] + [jnp.sum(piece, axis=0, keepdims=True) for piece in sums], axis=0
    )

    @pl.when(step == pl.num_programs(0) - 1)
    def _():
        for slot in range(VIRTUAL // 2):
            for ref, side in ((keep, core[0]), (send, 1 - core[0])):
                owner = 2 * slot + side
                strip = pl.ds(pl.multiple_of(owner * share, share), share)
                ref[slot, 0:share, :] = out_sum[strip, :].astype(BF)
                for lane in range(inner // width):
                    ref[slot, share * (lane + 1) : share * (lane + 2), :] = up_sum[strip, lane * width : (lane + 1) * width].astype(BF)
                turned_down = down_sum[:, pl.ds(pl.multiple_of(owner * part, part), part)].astype(BF)
                ref[slot, share + share * (inner // width) :, :] = turned_down.T
        for d in range(VIRTUAL):
            grad_up_bias[d : d + 1, :] = up_sum[width : width + 1, d * part : (d + 1) * part]
        grad_vectors[...] = vector_sum[...]


def backward_kernel(
    heads_per_step, first_unit, used, kept, value_rows, key_t, query_t, mixed_grad_t, center, *refs
):
    query_grad_t, key_grad_t, value_grad_t = refs[-3:]
    steps = HEADS // heads_per_step
    unit = pl.program_id(0) + first_unit
    image = unit // steps
    step = unit - image * steps
    width, length = query_t.shape[1:]
    size = width // HEADS
    scale = size ** (-0.5)
    count = used[image]
    blocks_used = (count + 127) // 128
    group_rows = lax.broadcasted_iota(jnp.int32, (128, length), 0) // size

    def one_head(index, blocks):
        head = step * heads_per_step + index
        block = head // (128 // size)
        inner = head - block * (128 // size)
        span = blocks * 128
        head_rows = pl.ds(pl.multiple_of(head * size, 32), size)
        own_rows = slice(index * size, (index + 1) * size)
        around = mixed_grad_t[0, pl.ds(pl.multiple_of(block * 128, 128), 128), :]
        own = jnp.where(group_rows == inner, around, 0).astype(BF)
        values = value_rows[0, block, :span, :]
        keys = key_t[0, head_rows, :span]
        value_sum = jnp.zeros((size, span), F32)
        key_sum = jnp.zeros((size, span), F32)
        piece = length // 2
        for part in range(length // piece):
            cut = slice(part * piece, (part + 1) * piece)
            pulled = nn(values, own[:, cut]) - center[0, pl.ds(head, 1), cut]
            weight = kept[0, index, :span, cut]
            score_grad = (weight.astype(F32) * pulled).astype(BF)
            query_grad_t[0, own_rows, cut] = (nn(keys, score_grad) * scale).astype(BF)
            value_sum = value_sum + nt(mixed_grad_t[0, head_rows, cut], weight)
            key_sum = key_sum + nt(query_t[0, head_rows, cut], score_grad)
        valid = lax.broadcasted_iota(jnp.int32, (size, span), 1) < count
        value_grad_t[0, own_rows, :span] = jnp.where(valid, value_sum, 0.0).astype(BF)
        key_grad_t[0, own_rows, :span] = jnp.where(valid, key_sum * scale, 0.0).astype(BF)
        if span < length:
            value_grad_t[0, own_rows, span:] = jnp.zeros((size, length - span), BF)
            key_grad_t[0, own_rows, span:] = jnp.zeros((size, length - span), BF)

    for blocks in range(1, length // 128 + 1):

        @pl.when(blocks_used == blocks)
        def _(blocks=blocks):
            for index in range(heads_per_step):
                one_head(index, blocks)


def weights_kernel(
    core, lifted_t, lifted_ct, tokens_ct, query_grad_t, key_grad_t, value_grad_t, early_vectors, up_bias,
    keep, send, sums, vector_sum,
):
    image = pl.program_id(0)
    length = lifted_t.shape[2]
    width = lifted_t.shape[1]
    share = width // VIRTUAL

    @pl.when(image == 0)
    def _():
        sums[...] = jnp.zeros_like(sums)
        vector_sum[...] = early_vectors[...]

    ones = jnp.ones((16, length), BF)
    query_sum = nt(jnp.concatenate([lifted_t[0], ones], axis=0), query_grad_t[0])
    value_sum = nt(jnp.concatenate([tokens_ct[0], ones], axis=0), value_grad_t[0])
    sums[0] += query_sum[:width]
    sums[1] += nt(lifted_ct[0], key_grad_t[0])
    sums[2] += value_sum[:width]
    vector_sum[0:1, :] += query_sum[width : width + 1]
    vector_sum[1:2, :] += value_sum[width : width + 1]

    @pl.when(image == pl.num_programs(0) - 1)
    def _():
        for slot in range(VIRTUAL // 2):
            for ref, side in ((keep, core[0]), (send, 1 - core[0])):
                owner = 2 * slot + side
                strip = pl.ds(pl.multiple_of(owner * share, share), share)
                for k in range(3):
                    ref[slot, k * share : (k + 1) * share, :] = sums[k, strip, :].astype(BF)
                bias = jnp.broadcast_to(up_bias[pl.ds(owner, 1), :], (8, width))
                ref[slot, 3 * share :, :] = jnp.concatenate([vector_sum[...], bias], axis=0).astype(BF)


def finish_kernel(place, *refs):
    pieces, (grad_out, grad_up, grad_down, three, vectors, total) = refs[:-6], refs[-6:]
    share = grad_out.shape[0]
    width = grad_out.shape[1]
    lanes = grad_up.shape[1] // width
    size = total.shape[0] // len(pieces)
    for far, piece in enumerate(pieces):
        owner = place[0] ^ far
        total[pl.ds(pl.multiple_of(owner * size, 8), size), :] = piece[:size, :].astype(F32)
    grad_out[...] = total[:share]
    for lane in range(lanes):
        grad_up[:, lane * width : (lane + 1) * width] = total[share * (lane + 1) : share * (lane + 2)]
    grad_down[...] = total[share * (lanes + 1) :]
    sums = [piece[...].astype(F32)[size:, :] for piece in pieces]
    while len(sums) > 1:
        sums = [sums[k] + sums[k + 1] for k in range(0, len(sums), 2)]
    for k in range(3):
        three[k] = sums[0][k * share : (k + 1) * share]
    vectors[...] = sums[0][3 * share :]


def tokens_kernel(first, rank, grad_first, near, query_grad_t, key_grad_t, value_grad_t, *refs):
    grad_tokens = refs[-1]
    image = pl.program_id(0) + first
    length = query_grad_t.shape[2]
    width = query_grad_t.shape[1]
    compact = lax.broadcasted_iota(jnp.int32, (length, length), 0)
    chosen = jnp.where(compact == rank[pl.ds(image, 1), :], 1.0, 0.0).astype(BF)
    both = nn(jnp.concatenate([key_grad_t[0], value_grad_t[0]], axis=0), chosen).astype(BF)
    weights = [near_weight(near, k) for k in range(3)]
    total_t = nn(weights[0], query_grad_t[0]) + nn(weights[1], both[:width]) + nn(weights[2], both[width:])
    grad_tokens[0] = grad_first[0] + total_t.T


def params(mebibytes, *semantics):
    return pltpu.CompilerParams(dimension_semantics=semantics, vmem_limit_bytes=mebibytes << 20)


def cost(microseconds):
    return pl.CostEstimate(flops=int(microseconds * 1.0e9), bytes_accessed=1 << 20, transcendentals=0)


def whole(shape):
    return pl.BlockSpec(shape, lambda *_: (0,) * len(shape))


def per_image(shape):
    return pl.BlockSpec((1,) + shape, lambda i, *_: (i,) + (0,) * len(shape))


def scalars():
    return pl.BlockSpec(memory_space=SMEM)


def shaped(shape, dtype):
    return jax.ShapeDtypeStruct(shape, dtype)


def resident(shape, dtype):
    return pltpu.VMEM(shape, dtype)


def stored(shape, dtype):
    return pltpu.HBM(shape, dtype)


def near_by(*arrays):
    return [pltpu.with_memory_space_constraint(array, pltpu.VMEM) for array in arrays]


def far_off(*arrays):
    return [pltpu.with_memory_space_constraint(array, pltpu.HBM) for array in arrays]


def exchange_dp(field, dp):
    return lax.all_to_all(jnp.broadcast_to(field, (dp,) + field.shape), "dp", 0, 0, tiled=True)


def same_core(zero):
    return [[k for k in range(zero) if k % 2 == side] for side in range(2)]


def swap_cores(send, zero):
    return lax.ppermute(send, "zero", [(k, k ^ 1) for k in range(zero)])


def by_owner(keep, send):
    return jnp.stack([keep, send], axis=1).reshape((VIRTUAL,) + keep.shape[1:])


def body(
    tokens, counts, key_mask, rotation, token_order, query_weight, key_weight, value_weight, out_weight, up_weight,
    down_weight, query_bias, value_bias, out_bias, up_bias, down_bias, first_gain, first_shift, second_gain,
    second_shift, cotangent, *, zero, dp,
):
    images, length, width = tokens.shape
    rows = images * length
    inner = up_weight.shape[1]
    share = width // zero
    inner_share = inner // zero
    direct = zero == VIRTUAL
    heads_per_step = 2
    steps = HEADS // heads_per_step
    me = lax.axis_index("zero")
    core = (me % 2 if direct else me * 0).astype(jnp.int32).reshape(1)

    small = [query_bias, value_bias, out_bias, down_bias, first_gain, first_shift, second_gain, second_shift]
    near_rows = 3 * (width // VIRTUAL) + 16
    far_rows = (2 * inner + width) // VIRTUAL
    if direct:
        near = pl.pallas_call(
            pack_kernel,
            in_specs=[scalars()] + [pl.BlockSpec(memory_space=pltpu.VMEM)] * 12,
            out_shape=shaped((zero, near_rows, width), BF),
            scratch_shapes=[pltpu.VMEM((8, share), F32)],
            name="pack",
        )(me.astype(jnp.int32).reshape(1), query_weight, key_weight, value_weight, *small, up_bias)
        near = lax.all_to_all(near, "zero", 0, 0, tiled=True)
    else:
        gather = functools.partial(lax.all_gather, axis_name="zero", axis=0, tiled=True)
        shards = [gather(w).reshape(VIRTUAL, -1, width) for w in (query_weight, key_weight, value_weight)]
        vectors = jnp.zeros((VIRTUAL, 8, width), BF).at[0].set(jnp.stack([gather(v) for v in small]))
        biases = jnp.broadcast_to(gather(up_bias).reshape(VIRTUAL, 1, inner // VIRTUAL), (VIRTUAL, 8, inner // VIRTUAL))
        near = jnp.concatenate(shards + [vectors, biases], axis=1)
        lanes = gather(up_weight).reshape(VIRTUAL, width // VIRTUAL, inner // width, width).transpose(0, 2, 1, 3)
        shards = [gather(w).reshape(VIRTUAL, -1, width) for w in (down_weight, out_weight)]
        far = jnp.concatenate(shards + [lanes.reshape(VIRTUAL, -1, width)], axis=1)
        far = [far[0::2], far[1::2]]

    table = jnp.asarray(position_table(GRID, width))
    turned = stored((images, width, length), BF)
    bundle = [shaped((VIRTUAL // 2, far_rows, width), BF)] if direct else []
    lifted_t, lifted_ct, tokens_ct, rank, used, *mine = pl.pallas_call(
        prep_kernel,
        grid=(images,),
        in_specs=[
            scalars(), scalars(), per_image((length, width)), whole((images, length)), whole((images, length)),
            whole(table.shape), whole(out_weight.shape), whole(down_weight.shape), whole(up_weight.shape),
        ],
        out_specs=[per_image((width, length))] * 3 + [whole((images, length)), scalars()] + [whole(b.shape) for b in bundle],
        out_shape=[turned] * 3 + [stored((images, length), jnp.int32), shaped((images,), jnp.int32)] + bundle,
        compiler_params=params(40, "arbitrary"),
        name="prep",
    )(counts, rotation, *far_off(tokens, key_mask, token_order, table, out_weight, down_weight, up_weight))
    if direct:
        (mine,) = mine
        mine = lax.all_to_all(mine, "zero", 0, 0, tiled=True, axis_index_groups=same_core(zero))

    head_block = pl.BlockSpec((1, heads_per_step, length, length), lambda i, s: (i, s, 0, 0))
    kept, mixed_t, inverse, query_t, key_t, value_rows = pl.pallas_call(
        functools.partial(forward_kernel, heads_per_step),
        grid=(images, steps),
        in_specs=[scalars()] + [per_image((width, length))] * 3 + [whole(near.shape)],
        out_specs=[
            head_block, per_image((width, length)), per_image((HEADS, length)), per_image((width, length)),
            per_image((width, length)), per_image((width // 128, length, 128)),
        ],
        out_shape=[
            stored((images, HEADS, length, length), BF), turned, stored((images, HEADS, length), F32), turned, turned,
            stored((images, width // 128, length, 128), BF),
        ],
        scratch_shapes=[
            pltpu.VMEM((width // 128, length, 128), BF),
            pltpu.VMEM((width + 16 * HEADS, length), BF),
            pltpu.SMEM((1,), jnp.int32),
        ],
        compiler_params=params(30, "arbitrary", "arbitrary"),
        cost_estimate=cost(22),
        name="attend_forward",
    )(used, *far_off(lifted_t, lifted_ct, tokens_ct), *near_by(near))

    if direct:
        mine, mixed_t = lax.optimization_barrier((mine, mixed_t))
        far = [mine, swap_cores(mine, zero)]
    block = length
    per = length // block
    row_block = pl.BlockSpec((block, width), lambda s: (s, 0))

    def turned_block(height):
        return pl.BlockSpec((1, height, block), lambda s: (s // per, 0, s % per))

    early_rows = (width + 2 * inner) // VIRTUAL
    half = resident((VIRTUAL // 2, early_rows, width), BF)
    layer_out, grad_first, mixed_grad_t, center, keep, send, grad_vectors, grad_up_bias = pl.pallas_call(
        functools.partial(ffn_kernel, 256),
        grid=(rows // block,),
        in_specs=[
            scalars(), row_block, turned_block(width), turned_block(HEADS), row_block, whole(near.shape), whole(far[0].shape),
            whole(far[1].shape),
        ],
        out_specs=[
            row_block, row_block, turned_block(width), turned_block(HEADS), whole(half.shape), whole(half.shape),
            whole((8, width)), whole((VIRTUAL, inner // VIRTUAL)),
        ],
        out_shape=[
            stored((rows, width), BF), stored((rows, width), F32), turned, stored((images, HEADS, length), F32),
            half, half, shaped((8, width), F32), shaped((VIRTUAL, inner // VIRTUAL), F32),
        ],
        scratch_shapes=[
            pltpu.VMEM((width, width), F32), pltpu.VMEM((width + 16, inner), F32), pltpu.VMEM((width, inner), F32),
            pltpu.VMEM((8, width), F32), pltpu.VMEM((block, inner), BF), pltpu.VMEM((block, inner), BF),
            pltpu.VMEM((width, inner), BF), pltpu.VMEM((inner, width), BF), pltpu.VMEM((width, width), BF),
            pltpu.VMEM((1, inner), F32),
        ],
        compiler_params=params(50, "arbitrary"),
        cost_estimate=cost(27),
        name="feed_forward",
    )(
        core, *far_off(tokens.reshape(rows, width)), *far_off(mixed_t, inverse),
        *far_off(cotangent.reshape(rows, width), near), *near_by(*far),
    )

    units = images * steps
    unit_rows = resident((units, heads_per_step * (width // HEADS), length), BF)

    def attend_backward(first, last, center, before):
        def unit_block(shape, index):
            return pl.BlockSpec((1,) + shape, lambda u: index(u + first))

        image = lambda u: (u // steps, 0, 0)
        grad_block = unit_block(unit_rows.shape[1:], lambda u: (u, 0, 0))
        return pl.pallas_call(
            functools.partial(backward_kernel, heads_per_step, first),
            grid=(last - first,),
            in_specs=[
                scalars(),
                unit_block((heads_per_step, length, length), lambda u: (u // steps, u % steps, 0, 0)),
                unit_block((width // 128, length, 128), lambda u: (u // steps, 0, 0, 0)),
            ]
            + [unit_block((width, length), image)] * 3
            + [unit_block((HEADS, length), image)]
            + [pl.BlockSpec(memory_space=pl.ANY)] * len(before),
            out_specs=[grad_block] * 3,
            out_shape=[unit_rows] * 3,
            input_output_aliases={7 + k: k for k in range(len(before))},
            compiler_params=params(26, "arbitrary"),
            cost_estimate=cost(1),
            name="attend_backward",
        )(used, *far_off(kept), *far_off(value_rows, key_t, query_t, mixed_grad_t, center), *near_by(*before))

    cuts = (units // 8, units * 5 // 8)
    if direct:
        came = swap_cores(send, zero)
        grads = attend_backward(0, cuts[0], center, ())
        came, grads = lax.optimization_barrier((came, grads))
        merged = (keep.astype(F32) + came.astype(F32)).astype(BF)
        shuffled = lax.all_to_all(merged, "zero", 0, 0, tiled=True, axis_index_groups=same_core(zero))
        merged, center = lax.optimization_barrier((merged, center))
        grads = attend_backward(cuts[0], cuts[1], center, grads)
        shuffled, grads = lax.optimization_barrier((shuffled, grads))
        early = jnp.sum(shuffled.astype(F32), axis=0).astype(BF)
        early, grads = lax.optimization_barrier((early, grads))
        early = lax.all_to_all(early.reshape(dp, early_rows // dp, width), "dp", 0, 0, tiled=True)
        grads = attend_backward(cuts[1], units, center, grads)
        early, grads = lax.optimization_barrier((early, grads))
        early = jnp.sum(early.astype(F32), axis=0).astype(BF)
    else:
        grads = attend_backward(0, units, center, ())
        halves = by_owner(keep, send)
        strip = width // VIRTUAL
        lanes = inner // width
        grad_out = halves[:, :strip].reshape(zero, share, width)
        grad_up = halves[:, strip : strip * (lanes + 1)].reshape(VIRTUAL, lanes, strip, width).transpose(0, 2, 1, 3)
        grad_up = grad_up.reshape(zero, share, lanes, width).transpose(0, 2, 1, 3).reshape(zero, share * lanes, width)
        grad_down = halves[:, strip * (lanes + 1) :].reshape(zero, inner_share, width)
        early = jnp.concatenate([grad_out, grad_up, grad_down], axis=1)
        early = jnp.sum(lax.all_to_all(early, "zero", 0, 0, tiled=True).astype(F32), axis=0).astype(BF)
        early = exchange_dp(early, dp)
    query_grad_t, key_grad_t, value_grad_t = [g.reshape(images, width, length) for g in grads]

    late_half = resident((VIRTUAL // 2, near_rows, width), BF)
    keep, send = pl.pallas_call(
        weights_kernel,
        grid=(images,),
        in_specs=[scalars()] + [per_image((width, length))] * 6 + [whole((8, width)), whole((VIRTUAL, inner // VIRTUAL))],
        out_specs=[whole(late_half.shape)] * 2,
        out_shape=[late_half] * 2,
        scratch_shapes=[pltpu.VMEM((3, width, width), F32), pltpu.VMEM((8, width), F32)],
        compiler_params=params(16, "arbitrary"),
        cost_estimate=cost(1),
        name="weight_grads",
    )(core, *far_off(lifted_t, lifted_ct, tokens_ct), *near_by(query_grad_t, key_grad_t, value_grad_t), grad_vectors, grad_up_bias)

    def token_grads(first, last, rank, before):
        def own(shape):
            return pl.BlockSpec((1,) + shape, lambda i: (i + first, 0, 0))

        return pl.pallas_call(
            functools.partial(tokens_kernel, first),
            grid=(last - first,),
            in_specs=[whole((images, length)), own((length, width)), whole(near.shape)]
            + [own((width, length))] * 3
            + [pl.BlockSpec(memory_space=pl.ANY)] * len(before),
            out_specs=own((length, width)),
            out_shape=stored((images, length, width), F32),
            input_output_aliases={6: 0} if before else {},
            compiler_params=params(24, "arbitrary"),
            cost_estimate=cost(1),
            name="token_grads",
        )(
            *far_off(rank, grad_first.reshape(images, length, width), near),
            *near_by(query_grad_t, key_grad_t, value_grad_t),
            *far_off(*before),
        )

    if direct:
        came = swap_cores(send, zero)
        merged = (keep.astype(F32) + came.astype(F32)).astype(BF)
        late = lax.all_to_all(merged, "zero", 0, 0, tiled=True, axis_index_groups=same_core(zero))
        grad_tokens = token_grads(0, images // 2, rank, ())
        late, grad_tokens = lax.optimization_barrier((late, grad_tokens))
        late = jnp.sum(late.astype(F32), axis=0).astype(BF)
        start = me * share
        tail = jnp.concatenate([early, late], axis=0)
        tail, rank = lax.optimization_barrier((tail, rank))
        tail = [tail] + [lax.ppermute(tail, "dp", [(k, k ^ step) for k in range(dp)]) for step in range(1, dp)]
        grad_tokens = token_grads(images // 2, images, rank, (grad_tokens,))
    else:
        halves = by_owner(keep, send)
        strip = width // VIRTUAL
        three = halves[:, : 3 * strip].reshape(VIRTUAL, 3, strip, width).transpose(1, 0, 2, 3).reshape(3, zero, share, width)
        three = three.transpose(1, 0, 2, 3).reshape(zero, 3 * share, width)
        vectors = halves[:, 3 * strip : 3 * strip + 8].reshape(VIRTUAL, 8, width)[0]
        vectors = vectors.reshape(8, zero, share).transpose(1, 0, 2)
        vectors = jnp.pad(vectors, ((0, 0), (0, 0), (0, width - share)))
        bias = jnp.pad(halves[:, -1].reshape(zero, 1, inner_share), ((0, 0), (0, 7), (0, width - inner_share)))
        late = jnp.concatenate([three, vectors, bias], axis=1)
        late = jnp.sum(lax.all_to_all(late, "zero", 0, 0, tiled=True).astype(F32), axis=0).astype(BF)
        start = me * 0
        grad_tokens = token_grads(0, images, rank, ())
        late = jnp.sum(exchange_dp(late, dp).astype(F32), axis=0)

    if direct:
        grad_out_own, grad_up_own, grad_down_own, three, vectors = pl.pallas_call(
            finish_kernel,
            in_specs=[scalars()] + [pl.BlockSpec(memory_space=pltpu.VMEM)] * dp,
            out_shape=[
                stored((share, width), F32), stored((share, inner), F32), stored((inner_share, width), F32),
                shaped((3, share, width), F32), shaped((near_rows - 3 * share, width), F32),
            ],
            scratch_shapes=[pltpu.VMEM((early_rows, width), F32)],
            compiler_params=pltpu.CompilerParams(vmem_limit_bytes=16 << 20),
            name="finish",
        )(lax.axis_index("dp").astype(jnp.int32).reshape(1), *tail)
    else:
        lanes = inner // width
        total = jnp.sum(early.astype(F32), axis=0)
        grad_out_own = total[:share]
        grad_up_own = total[share : share * (lanes + 1)].reshape(lanes, share, width).transpose(1, 0, 2).reshape(share, inner)
        grad_down_own = total[share * (lanes + 1) :]
        three = late[: 3 * share].reshape(3, share, width)
        vectors = late[3 * share :]
    cuts = [lax.dynamic_slice(vectors, (k, start), (1, share)).reshape(share) for k in range(8)]
    up_bias_own = vectors[8, :inner_share]
    return (
        layer_out.reshape(images, length, width),
        grad_tokens,
        three[0],
        three[1],
        three[2],
        grad_out_own,
        grad_up_own,
        grad_down_own,
        cuts[0],
        cuts[1],
        cuts[2],
        up_bias_own,
        cuts[3],
        cuts[4],
        cuts[5],
        cuts[6],
        cuts[7],
    )


def solution(mesh):
    batch = P(("dp", "zero"))
    wide = P(("dp", "zero"), None, None)
    flat = P(("dp", "zero"), None)
    matrix = P("zero", None)
    vector = P("zero")
    in_specs = (wide, batch, flat, batch, flat) + (matrix,) * 6 + (vector,) * 9 + (wide,)
    out_specs = (wide, wide) + (matrix,) * 6 + (vector,) * 9
    run = functools.partial(body, zero=mesh.shape["zero"], dp=mesh.shape["dp"])
    return jax.shard_map(run, mesh=mesh, in_specs=in_specs, out_specs=out_specs, check_vma=False)
```

```python
import functools
import math

import jax
import jax.numpy as jnp
import numpy as np
from jax import lax
from jax.experimental import pallas as pl
from jax.experimental.pallas import tpu as pltpu
from jax.sharding import PartitionSpec as P

HEADS = 8
GRID = 32
EPS = 1e-05
LOG2E = 1.4426950408889634
SAFE = 60.0

BF = jnp.bfloat16
F32 = jnp.float32
SMEM = pltpu.SMEM
VIRTUAL = 8
QUARTERS = 4


def nn(left, right):
    return lax.dot_general(left, right, (((1,), (0,)), ((), ())), preferred_element_type=F32)


def nt(left, right):
    return lax.dot_general(left, right, (((1,), (1,)), ((), ())), preferred_element_type=F32)


def position_table(grid, width):
    half = width // 2
    index = np.arange(half)
    freq = np.power(np.float32(10000.0), (2 * (index // 2)).astype(np.float32) / np.float32(half)).astype(np.float32)
    coord = np.arange(grid).astype(np.float32)
    angle = ((coord + np.float32(1.0)) / np.float32(grid + 1e-06) * np.float32(2.0 * math.pi)).astype(np.float32)
    angle = (angle[:, None] / freq).astype(np.float32)
    table = np.where(index % 2 == 0, np.sin(angle), np.cos(angle)).astype(np.float32)
    high = table.astype(BF)
    rest = (table - high.astype(np.float32)).astype(BF)
    whole = np.zeros((4 * grid, width), dtype=BF)
    for group, piece in enumerate((high, high, rest, rest)):
        start = (group % 2) * half
        whole[group * grid : (group + 1) * grid, start : start + half] = piece
    return np.ascontiguousarray(whole.T)


def pack_kernel(where, query, key, value, *refs):
    vectors, up_bias, near, stack = refs[:8], refs[8], refs[9], refs[10]
    share, width = query.shape
    for k, vector in enumerate(vectors):
        stack[k : k + 1, :] = vector[...].astype(F32).reshape(1, share)
    place = lax.broadcasted_iota(jnp.int32, (share, width), 1) - where[0] * share
    spread = jnp.where(place == lax.broadcasted_iota(jnp.int32, (share, width), 0), 1.0, 0.0).astype(BF)
    rows = nn(stack[...].astype(BF), spread)
    bias = jnp.broadcast_to(up_bias[...].astype(F32).reshape(1, width), (8, width))
    last = jnp.concatenate([rows, bias], axis=0).astype(BF)
    for d in range(near.shape[0]):
        near[d, 0:share, :] = query[...]
        near[d, share : 2 * share, :] = key[...]
        near[d, 2 * share : 3 * share, :] = value[...]
        near[d, 3 * share :, :] = last


def prep_kernel(
    counts, rotation, tokens, key_mask, token_order, table, out, down, up,
    lifted_t, lifted_ct, tokens_ct, rank_out, used, *far,
):
    image = pl.program_id(0)
    length = tokens.shape[1]
    slot = lax.broadcasted_iota(jnp.int32, (1, length), 1)
    mask = key_mask[pl.ds(image, 1), :]
    usable = (slot < counts[image]) & ((mask == 1) | (slot == 0))
    flag = jnp.where(usable, 1, 0)
    used[image] = jnp.sum(flag)
    total = flag
    step = 1
    while step < length:
        total = total + jnp.where(slot >= step, pltpu.roll(total, step, 1), 0)
        step *= 2
    rank = jnp.where(usable, total - 1, -1)
    rank_out[pl.ds(image, 1), :] = rank
    cell = token_order[pl.ds(image, 1), :]
    row = cell // GRID
    column = cell - row * GRID
    turn = rotation[image]
    last = GRID - 1
    ycoord = jnp.where(turn == 0, row, jnp.where(turn == 1, column, jnp.where(turn == 2, last - row, last - column)))
    xcoord = jnp.where(turn == 0, column, jnp.where(turn == 1, last - row, jnp.where(turn == 2, last - column, row)))
    place = lax.broadcasted_iota(jnp.int32, (4 * GRID, length), 0)
    group = place // GRID
    wanted = jnp.where(group % 2 == 0, ycoord, xcoord)
    hot = jnp.where(place - group * GRID == wanted, 1.0, 0.0).astype(BF)
    pos_t = nn(table[...], hot)
    tokens_t = tokens[0].T
    low_t = (tokens_t.astype(F32) + pos_t).astype(BF)
    lifted_t[0] = low_t
    compact = lax.broadcasted_iota(jnp.int32, (length, length), 0)
    chosen = jnp.where(compact == rank, 1.0, 0.0).astype(BF)
    lifted_ct[0] = nt(low_t, chosen).astype(BF)
    tokens_ct[0] = nt(tokens_t, chosen).astype(BF)
    if far:

        @pl.when(image == 0)
        def _():
            (bundle,) = far
            share, width = out.shape
            bundle[0 : down.shape[0], :] = down[...]
            bundle[down.shape[0] : down.shape[0] + share, :] = out[...]
            for lane in range(up.shape[1] // width):
                start = down.shape[0] + share * (lane + 1)
                bundle[start : start + share, :] = up[:, lane * width : (lane + 1) * width]


def near_weight(near, k):
    share = near.shape[2] // VIRTUAL
    return jnp.concatenate([near[d, k * share : (k + 1) * share, :] for d in range(VIRTUAL)], axis=0)


def near_vectors(near):
    share = near.shape[2] // VIRTUAL
    total = near[0, 3 * share : 3 * share + 16, :].astype(F32)
    for d in range(1, VIRTUAL):
        total = total + near[d, 3 * share : 3 * share + 16, :].astype(F32)
    return total[:8]


def forward_kernel(
    heads_per_step, used, lifted_t, lifted_ct, tokens_ct, near,
    kept, mixed_t, inverse, query_t, key_t, value_rows, key_rows, value_ext, calm,
):
    image = pl.program_id(0)
    step = pl.program_id(1)
    width, length = query_t.shape[1:]
    size = width // HEADS
    ext = size + 16
    scale = LOG2E * size ** (-0.5)
    count = used[image]

    @pl.when(step == 0)
    def _():
        weights = [near_weight(near, k) for k in range(3)]
        columns = near_vectors(near).T
        query = (nn(weights[0].T, lifted_t[0]) + columns[:, 0:1]).astype(BF)
        query_t[0] = query
        key = nn(weights[1].T, lifted_ct[0]).astype(BF)
        key_t[0] = key
        value = (nn(weights[2].T, tokens_ct[0]) + columns[:, 1:2]).astype(BF)
        key_turned = key.T
        value_turned = value.T
        for block in range(width // 128):
            part = slice(block * 128, (block + 1) * 128)
            key_rows[block] = key_turned[:, part]
            value_rows[0, block] = value_turned[:, part]
        valid = lax.broadcasted_iota(jnp.int32, (size, length), 1) < count
        first = lax.broadcasted_iota(jnp.int32, (16, length), 0) == 0
        ones = jnp.where(first & valid[:16], 1.0, 0.0).astype(BF)
        for head in range(HEADS):
            value_ext[head * ext : head * ext + size, :] = jnp.where(valid, value[head * size : (head + 1) * size], 0).astype(BF)
            value_ext[head * ext + size : (head + 1) * ext, :] = ones
        wide_query = query.astype(F32)
        wide_key = key.astype(F32)
        query_norm = jnp.max(jnp.sum((wide_query * wide_query).reshape(HEADS, size, length), axis=1), axis=1, keepdims=True)
        key_norm = jnp.max(jnp.sum((wide_key * wide_key).reshape(HEADS, size, length), axis=1), axis=1, keepdims=True)
        reach = jnp.max(query_norm * key_norm) * (scale * scale)
        calm[0] = jnp.where(reach <= SAFE * SAFE, 1, 0)

    group_rows = lax.broadcasted_iota(jnp.int32, (128, length), 0) // size

    def one_head(index, blocks, safe):
        head = step * heads_per_step + index
        block = head // (128 // size)
        inner = head - block * (128 // size)
        span = blocks * 128
        around = query_t[0, pl.ds(pl.multiple_of(block * 128, 128), 128), :]
        own = jnp.where(group_rows == inner, around, 0).astype(BF)
        keys = key_rows[block, :span, :]
        values = value_ext[pl.ds(pl.multiple_of(head * ext, 16), ext), :span]
        piece = length // 2
        for part in range(length // piece):
            cut = slice(part * piece, (part + 1) * piece)
            scores = nn(keys, own[:, cut]) * scale
            if not safe:
                place = lax.broadcasted_iota(jnp.int32, scores.shape, 0)
                scores = jnp.where(place < count, scores, -1e30)
                scores = scores - jnp.max(scores, axis=0, keepdims=True)
            weight = jnp.exp2(scores).astype(BF)
            kept[0, index, :span, cut] = weight
            summed = nn(values, weight)
            turned = 1.0 / summed[size : size + 1, :]
            mixed_t[0, pl.ds(pl.multiple_of(head * size, 32), size), cut] = (summed[:size] * turned).astype(BF)
            inverse[0, pl.ds(head, 1), cut] = turned

    blocks_used = (count + 127) // 128
    for blocks in range(1, length // 128 + 1):

        @pl.when((calm[0] == 1) & (blocks_used == blocks))
        def _(blocks=blocks):
            for index in range(heads_per_step):
                one_head(index, blocks, True)

    @pl.when(calm[0] == 0)
    def _():
        for index in range(heads_per_step):
            one_head(index, length // 128, False)


def norm_parts(field):
    middle = jnp.mean(field, axis=-1, keepdims=True)
    center = field - middle
    spread = jnp.mean(center * center, axis=-1, keepdims=True)
    pull = lax.rsqrt(spread + EPS)
    return center * pull, pull


def norm_back(grad, normal, pull):
    return (grad - jnp.mean(grad, axis=-1, keepdims=True) - normal * jnp.mean(grad * normal, axis=-1, keepdims=True)) * pull


def ffn_kernel(chunk, where, tokens, mixed_t, inverse, cotangent, near, *refs):
    far, refs = refs[:VIRTUAL], refs[VIRTUAL:]
    layer_out, grad_first, mixed_grad_t, center, keep, send, grad_vectors, grad_up_bias = refs[:8]
    out_sum, up_sum, down_sum, vector_sum, hidden_all, slope_all, up_weight, down_weight, out_weight, up_bias = refs[8:]
    step = pl.program_id(0)
    rows, width = tokens.shape
    inner = hidden_all.shape[1]
    size = width // HEADS
    share = width // VIRTUAL
    part = inner // VIRTUAL

    @pl.when(step == 0)
    def _():
        out_sum[...] = jnp.zeros_like(out_sum)
        up_sum[...] = jnp.zeros_like(up_sum)
        down_sum[...] = jnp.zeros_like(down_sum)
        vector_sum[...] = jnp.zeros_like(vector_sum)
        for side in range(2):
            for slot in range(VIRTUAL // 2):
                ref = far[side * (VIRTUAL // 2) + slot]
                owner = where[0] ^ (2 * slot + side)
                strip = pl.ds(pl.multiple_of(owner * share, share), share)
                down_weight[pl.ds(pl.multiple_of(owner * part, part), part), :] = ref[:part, :]
                out_weight[strip, :] = ref[part : part + share, :]
                for lane in range(inner // width):
                    cut = slice(part + share * (lane + 1), part + share * (lane + 2))
                    up_weight[strip, lane * width : (lane + 1) * width] = ref[cut, :]
        for d in range(VIRTUAL):
            up_bias[:, d * part : (d + 1) * part] = near[d, 3 * share : 3 * share + 16, :].astype(F32)[8:9]

    vectors = near_vectors(near)
    out_bias, down_bias, first_gain, first_shift, second_gain, second_shift = [vectors[k : k + 1, :] for k in range(2, 8)]
    mixed = mixed_t[0].T
    first_sum = tokens[...].astype(F32) + nn(mixed, out_weight[...]) + out_bias
    first_normal, first_pull = norm_parts(first_sum)
    first_norm = first_normal * first_gain + first_shift
    first_low = first_norm.astype(BF)
    second_sum = first_norm + down_bias
    root = math.sqrt(2.0 / math.pi)
    for start in range(0, inner, chunk):
        cut = slice(start, start + chunk)
        pre = (nn(first_low, up_weight[:, cut]) + up_bias[:, cut]).astype(BF)
        square = pre * pre
        gate = jnp.bfloat16(0.5) + jnp.bfloat16(0.5) * jnp.tanh(pre * (jnp.bfloat16(root) + jnp.bfloat16(root * 0.044715) * square))
        hidden = pre * gate
        slope_all[:, cut] = gate + hidden * (jnp.bfloat16(1.0) - gate) * (jnp.bfloat16(2.0 * root) + jnp.bfloat16(6.0 * root * 0.044715) * square)
        hidden_all[:, cut] = hidden
        second_sum = second_sum + nn(hidden, down_weight[cut, :])
    second_normal, second_pull = norm_parts(second_sum)
    layer_out[...] = (second_normal * second_gain + second_shift).astype(BF)
    wide = cotangent[...].astype(F32)
    grad_second = norm_back(wide * second_gain, second_normal, second_pull)
    ffn_grad = grad_second.astype(BF)
    ffn_grad_t = ffn_grad.T
    first_low_t = first_low.T
    ones = jnp.where(lax.broadcasted_iota(jnp.int32, (16, rows), 0) == 0, 1.0, 0.0).astype(BF)
    first_ext = jnp.concatenate([first_low_t, ones], axis=0)
    back = grad_second
    for start in range(0, inner, chunk):
        cut = slice(start, start + chunk)
        hidden_grad = nt(ffn_grad, down_weight[cut, :]).astype(BF) * slope_all[:, cut]
        down_sum[:, cut] += nn(ffn_grad_t, hidden_all[:, cut])
        up_sum[:, cut] += nn(first_ext, hidden_grad)
        back = back + nt(hidden_grad, up_weight[:, cut])
    first = norm_back(back * first_gain, first_normal, first_pull)
    grad_first[...] = first
    branch_grad = first.astype(BF)
    out_sum[...] += nn(mixed_t[0], branch_grad)
    mixed_grad = nt(out_weight[...], branch_grad).reshape(HEADS, size, rows)
    turned = inverse[0]
    scaled = (mixed_grad * turned[:, None, :]).astype(BF)
    mixed_grad_t[0] = scaled.reshape(width, rows)
    center[0] = jnp.sum(scaled.astype(F32) * mixed_t[0].astype(F32).reshape(HEADS, size, rows), axis=1)
    sums = (
        branch_grad.astype(F32), ffn_grad.astype(F32), back * first_normal, back, wide * second_normal, wide,
    )
    vector_sum[...] += jnp.concatenate(
        [jnp.zeros((2, width), F32)] + [jnp.sum(piece, axis=0, keepdims=True) for piece in sums], axis=0
    )

    @pl.when(step == pl.num_programs(0) - 1)
    def _():
        lanes = inner // width // QUARTERS
        few = share // QUARTERS
        for slot in range(VIRTUAL // 2):
            for ref, side in ((keep, where[0] % 2), (send, 1 - where[0] % 2)):
                owner = 2 * slot + side
                start = pl.multiple_of(owner * share, share)
                turned_down = down_sum[:, pl.ds(pl.multiple_of(owner * part, part), part)].astype(BF).T
                for quarter in range(QUARTERS):
                    for lane in range(lanes):
                        place = (quarter * lanes + lane) * width
                        ref[quarter, slot, lane * share : (lane + 1) * share, :] = up_sum[pl.ds(start, share), place : place + width].astype(BF)
                    low = lanes * share
                    high = low + part // QUARTERS
                    ref[quarter, slot, low:high, :] = turned_down[quarter * (part // QUARTERS) : (quarter + 1) * (part // QUARTERS)]
                    out = out_sum[pl.ds(start + quarter * few, few), :]
                    ref[quarter, slot, high:, :] = jnp.concatenate([out] * (16 // few), axis=0).astype(BF)
        for d in range(VIRTUAL):
            grad_up_bias[d : d + 1, :] = up_sum[width : width + 1, d * part : (d + 1) * part]
        grad_vectors[...] = vector_sum[...]


def backward_kernel(heads_per_step, first_unit, last_unit, used, kept, value_rows, key_t, query_t, mixed_grad_t, center, *refs):
    whole_job = len(refs) > 3
    if whole_job:
        earlier, (where, lifted_t, lifted_ct, tokens_ct, early_vectors, up_bias), refs = refs[:3], refs[3:9], refs[9:]
        query_grad_t, key_grad_t, value_grad_t, keep, send, held, arrived = refs
    else:
        query_grad_t, key_grad_t, value_grad_t = refs
    steps = HEADS // heads_per_step
    unit = pl.program_id(0) + first_unit
    image = unit // steps
    step = unit - image * steps
    width, length = query_t.shape[1:]
    size = width // HEADS
    share = width // VIRTUAL
    scale = size ** (-0.5)
    count = used[image]
    blocks_used = (count + 127) // 128
    group_rows = lax.broadcasted_iota(jnp.int32, (128, length), 0) // size
    at = unit if whole_job else 0

    if whole_job:
        copies = [
            pltpu.make_async_copy(source, held.at[k], arrived.at[k]) for k, source in enumerate((lifted_t, lifted_ct, tokens_ct))
        ]

        @pl.when(unit == first_unit)
        def _():
            for copy in copies:
                copy.start()
            for ref, source in zip((query_grad_t, key_grad_t, value_grad_t), earlier):
                ref[0:first_unit] = source[...]

    def one_head(index, blocks):
        head = step * heads_per_step + index
        block = head // (128 // size)
        inner = head - block * (128 // size)
        span = blocks * 128
        head_rows = pl.ds(pl.multiple_of(head * size, 32), size)
        own_rows = slice(index * size, (index + 1) * size)
        around = mixed_grad_t[0, pl.ds(pl.multiple_of(block * 128, 128), 128), :]
        own = jnp.where(group_rows == inner, around, 0).astype(BF)
        values = value_rows[0, block, :span, :]
        keys = key_t[0, head_rows, :span]
        value_sum = jnp.zeros((size, span), F32)
        key_sum = jnp.zeros((size, span), F32)
        piece = length // 2
        for part in range(length // piece):
            cut = slice(part * piece, (part + 1) * piece)
            pulled = nn(values, own[:, cut]) - center[0, pl.ds(head, 1), cut]
            weight = kept[0, index, :span, cut]
            score_grad = (weight.astype(F32) * pulled).astype(BF)
            query_grad_t[at, own_rows, cut] = (nn(keys, score_grad) * scale).astype(BF)
            value_sum = value_sum + nt(mixed_grad_t[0, head_rows, cut], weight)
            key_sum = key_sum + nt(query_t[0, head_rows, cut], score_grad)
        valid = lax.broadcasted_iota(jnp.int32, (size, span), 1) < count
        value_grad_t[at, own_rows, :span] = jnp.where(valid, value_sum, 0.0).astype(BF)
        key_grad_t[at, own_rows, :span] = jnp.where(valid, key_sum * scale, 0.0).astype(BF)
        if span < length:
            value_grad_t[at, own_rows, span:] = jnp.zeros((size, length - span), BF)
            key_grad_t[at, own_rows, span:] = jnp.zeros((size, length - span), BF)

    for blocks in range(1, length // 128 + 1):

        @pl.when(blocks_used == blocks)
        def _(blocks=blocks):
            for index in range(heads_per_step):
                one_head(index, blocks)

    if whole_job:

        @pl.when(unit == last_unit)
        def _():
            for copy in copies:
                copy.wait()
            ones = jnp.ones((16, length), BF)
            sums = [None] * 3
            for one in range(held.shape[1]):
                units = slice(one * steps, (one + 1) * steps)
                turned = [ref[units].reshape(width, length) for ref in (query_grad_t, key_grad_t, value_grad_t)]
                for k in range(3):
                    left = held[k, one]
                    added = nt(left if k == 1 else jnp.concatenate([left, ones], axis=0), turned[k])
                    sums[k] = added if sums[k] is None else sums[k] + added
            vectors = jnp.concatenate([sums[0][width : width + 1], sums[2][width : width + 1], early_vectors[2:8, :]], axis=0)
            for k in range(3):
                low = sums[k][:width].astype(BF)
                for owner in range(VIRTUAL):
                    mine = where[0] % 2 == owner % 2
                    piece = low[owner * share : (owner + 1) * share]

                    @pl.when(mine)
                    def _(owner=owner, piece=piece, k=k):
                        keep[owner // 2, k * share : (k + 1) * share, :] = piece

                    @pl.when(jnp.logical_not(mine))
                    def _(owner=owner, piece=piece, k=k):
                        send[owner // 2, k * share : (k + 1) * share, :] = piece

            for slot in range(VIRTUAL // 2):
                for ref, side in ((keep, where[0] % 2), (send, 1 - where[0] % 2)):
                    bias = jnp.broadcast_to(up_bias[pl.ds(2 * slot + side, 1), :], (8, width))
                    ref[slot, 3 * share :, :] = jnp.concatenate([vectors, bias], axis=0).astype(BF)


def finish_kernel(place, *refs):
    pieces, (grad_out, grad_up, grad_down, *three, vectors) = refs[:QUARTERS], refs[QUARTERS:]
    share, width = grad_out.shape
    lanes = grad_up.shape[1] // width // QUARTERS
    part = grad_down.shape[0] // QUARTERS
    few = share // QUARTERS
    size = lanes * share + part + 16
    for far, ref in enumerate(pieces):
        owner = place[0] ^ far
        piece = ref[:size, :].astype(F32)
        for lane in range(lanes):
            at = pl.multiple_of((owner * lanes + lane) * width, width)
            grad_up[:, pl.ds(at, width)] = piece[lane * share : (lane + 1) * share]
        grad_down[pl.ds(pl.multiple_of(owner * part, part), part), :] = piece[lanes * share : lanes * share + part]
        grad_out[pl.ds(pl.multiple_of(owner * few, few), few), :] = piece[lanes * share + part : lanes * share + part + few]
    sums = [ref[size:, :].astype(F32) for ref in pieces]
    while len(sums) > 1:
        sums = [sums[k] + sums[k + 1] for k in range(0, len(sums), 2)]
    for k in range(3):
        three[k][...] = sums[0][k * share : (k + 1) * share]
    vectors[...] = sums[0][3 * share :]


def tokens_kernel(first, rank, grad_first, near, query_grad_t, key_grad_t, value_grad_t, *refs):
    grad_tokens = refs[-1]
    image = pl.program_id(0) + first
    length = query_grad_t.shape[2]
    width = query_grad_t.shape[1]
    compact = lax.broadcasted_iota(jnp.int32, (length, length), 0)
    chosen = jnp.where(compact == rank[pl.ds(image, 1), :], 1.0, 0.0).astype(BF)
    both = nn(jnp.concatenate([key_grad_t[0], value_grad_t[0]], axis=0), chosen).astype(BF)
    weights = [near_weight(near, k) for k in range(3)]
    total_t = nn(weights[0], query_grad_t[0]) + nn(weights[1], both[:width]) + nn(weights[2], both[width:])
    grad_tokens[0] = grad_first[0] + total_t.T


def params(mebibytes, *semantics):
    return pltpu.CompilerParams(dimension_semantics=semantics, vmem_limit_bytes=mebibytes << 20)


def cost(microseconds):
    return pl.CostEstimate(flops=int(microseconds * 1.0e9), bytes_accessed=1 << 20, transcendentals=0)


def whole(shape):
    return pl.BlockSpec(shape, lambda *_: (0,) * len(shape))


def per_image(shape):
    return pl.BlockSpec((1,) + shape, lambda i, *_: (i,) + (0,) * len(shape))


def scalars():
    return pl.BlockSpec(memory_space=SMEM)


def shaped(shape, dtype):
    return jax.ShapeDtypeStruct(shape, dtype)


def resident(shape, dtype):
    return pltpu.VMEM(shape, dtype)


def stored(shape, dtype):
    return pltpu.HBM(shape, dtype)


def near_by(*arrays):
    return [pltpu.with_memory_space_constraint(array, pltpu.VMEM) for array in arrays]


def far_off(*arrays):
    return [pltpu.with_memory_space_constraint(array, pltpu.HBM) for array in arrays]


def exchange_dp(field, dp):
    return lax.all_to_all(jnp.broadcast_to(field, (dp,) + field.shape), "dp", 0, 0, tiled=True)


def same_core(zero):
    return [[k for k in range(zero) if k % 2 == side] for side in range(2)]


def swap_cores(send, zero):
    return lax.ppermute(send, "zero", [(k, k ^ 1) for k in range(zero)])


def by_owner(keep, send):
    return jnp.stack([keep, send], axis=1).reshape((VIRTUAL,) + keep.shape[1:])


def body(
    tokens, counts, key_mask, rotation, token_order, query_weight, key_weight, value_weight, out_weight, up_weight,
    down_weight, query_bias, value_bias, out_bias, up_bias, down_bias, first_gain, first_shift, second_gain,
    second_shift, cotangent, *, zero, dp,
):
    images, length, width = tokens.shape
    rows = images * length
    inner = up_weight.shape[1]
    share = width // zero
    inner_share = inner // zero
    direct = zero == VIRTUAL and dp == QUARTERS
    heads_per_step = 2
    steps = HEADS // heads_per_step
    me = lax.axis_index("zero")
    spot = (me if direct else me * 0).astype(jnp.int32).reshape(1)

    small = [query_bias, value_bias, out_bias, down_bias, first_gain, first_shift, second_gain, second_shift]
    near_rows = 3 * (width // VIRTUAL) + 16
    far_rows = (2 * inner + width) // VIRTUAL
    if direct:
        near = pl.pallas_call(
            pack_kernel,
            in_specs=[scalars()] + [pl.BlockSpec(memory_space=pltpu.VMEM)] * 12,
            out_shape=shaped((zero, near_rows, width), BF),
            scratch_shapes=[pltpu.VMEM((8, share), F32)],
            name="pack",
        )(me.astype(jnp.int32).reshape(1), query_weight, key_weight, value_weight, *small, up_bias)
        near = lax.all_to_all(near, "zero", 0, 0, tiled=True)
    else:
        gather = functools.partial(lax.all_gather, axis_name="zero", axis=0, tiled=True)
        shards = [gather(w).reshape(VIRTUAL, -1, width) for w in (query_weight, key_weight, value_weight)]
        vectors = jnp.zeros((VIRTUAL, 8, width), BF).at[0].set(jnp.stack([gather(v) for v in small]))
        biases = jnp.broadcast_to(gather(up_bias).reshape(VIRTUAL, 1, inner // VIRTUAL), (VIRTUAL, 8, inner // VIRTUAL))
        near = jnp.concatenate(shards + [vectors, biases], axis=1)
        lanes = gather(up_weight).reshape(VIRTUAL, width // VIRTUAL, inner // width, width).transpose(0, 2, 1, 3)
        shards = [gather(w).reshape(VIRTUAL, -1, width) for w in (down_weight, out_weight)]
        far = jnp.concatenate(shards + [lanes.reshape(VIRTUAL, -1, width)], axis=1)
        far = [far[2 * slot + side] for side in range(2) for slot in range(VIRTUAL // 2)]

    table = jnp.asarray(position_table(GRID, width))
    turned = stored((images, width, length), BF)
    bundle = [shaped((far_rows, width), BF)] if direct else []
    lifted_t, lifted_ct, tokens_ct, rank, used, *mine = pl.pallas_call(
        prep_kernel,
        grid=(images,),
        in_specs=[
            scalars(), scalars(), per_image((length, width)), whole((images, length)), whole((images, length)),
            whole(table.shape), whole(out_weight.shape), whole(down_weight.shape), whole(up_weight.shape),
        ],
        out_specs=[per_image((width, length))] * 3 + [whole((images, length)), scalars()] + [whole(b.shape) for b in bundle],
        out_shape=[turned] * 3 + [stored((images, length), jnp.int32), shaped((images,), jnp.int32)] + bundle,
        compiler_params=params(40, "arbitrary"),
        name="prep",
    )(counts, rotation, *far_off(tokens, key_mask, token_order, table, out_weight, down_weight, up_weight))
    if direct:
        mine = mine + [lax.ppermute(mine[0], "zero", [(k, k ^ (2 * step)) for k in range(zero)]) for step in range(1, zero // 2)]

    head_block = pl.BlockSpec((1, heads_per_step, length, length), lambda i, s: (i, s, 0, 0))
    kept, mixed_t, inverse, query_t, key_t, value_rows = pl.pallas_call(
        functools.partial(forward_kernel, heads_per_step),
        grid=(images, steps),
        in_specs=[scalars()] + [per_image((width, length))] * 3 + [whole(near.shape)],
        out_specs=[
            head_block, per_image((width, length)), per_image((HEADS, length)), per_image((width, length)),
            per_image((width, length)), per_image((width // 128, length, 128)),
        ],
        out_shape=[
            stored((images, HEADS, length, length), BF), turned, stored((images, HEADS, length), F32), turned, turned,
            stored((images, width // 128, length, 128), BF),
        ],
        scratch_shapes=[
            pltpu.VMEM((width // 128, length, 128), BF),
            pltpu.VMEM((width + 16 * HEADS, length), BF),
            pltpu.SMEM((1,), jnp.int32),
        ],
        compiler_params=params(30, "arbitrary", "arbitrary"),
        cost_estimate=cost(22),
        name="attend_forward",
    )(used, *far_off(lifted_t, lifted_ct, tokens_ct), *near_by(near))

    if direct:
        mine, mixed_t = lax.optimization_barrier((mine, mixed_t))
        far = mine + [swap_cores(piece, zero) for piece in mine]
    block = length
    per = length // block
    row_block = pl.BlockSpec((block, width), lambda s: (s, 0))

    def turned_block(height):
        return pl.BlockSpec((1, height, block), lambda s: (s // per, 0, s % per))

    early_rows = 2 * inner // VIRTUAL // QUARTERS + 16
    half = resident((QUARTERS, VIRTUAL // 2, early_rows, width), BF)
    layer_out, grad_first, mixed_grad_t, center, keep, send, grad_vectors, grad_up_bias = pl.pallas_call(
        functools.partial(ffn_kernel, 256),
        grid=(rows // block,),
        in_specs=[
            scalars(), row_block, turned_block(width), turned_block(HEADS), row_block, whole(near.shape),
        ]
        + [whole(piece.shape) for piece in far],
        out_specs=[
            row_block, row_block, turned_block(width), turned_block(HEADS), whole(half.shape), whole(half.shape),
            whole((8, width)), whole((VIRTUAL, inner // VIRTUAL)),
        ],
        out_shape=[
            stored((rows, width), BF), stored((rows, width), F32), turned, stored((images, HEADS, length), F32),
            half, half, shaped((8, width), F32), shaped((VIRTUAL, inner // VIRTUAL), F32),
        ],
        scratch_shapes=[
            pltpu.VMEM((width, width), F32), pltpu.VMEM((width + 16, inner), F32), pltpu.VMEM((width, inner), F32),
            pltpu.VMEM((8, width), F32), pltpu.VMEM((block, inner), BF), pltpu.VMEM((block, inner), BF),
            pltpu.VMEM((width, inner), BF), pltpu.VMEM((inner, width), BF), pltpu.VMEM((width, width), BF),
            pltpu.VMEM((1, inner), F32),
        ],
        compiler_params=params(50, "arbitrary"),
        cost_estimate=cost(27),
        name="feed_forward",
    )(
        spot, *far_off(tokens.reshape(rows, width)), *far_off(mixed_t, inverse),
        *far_off(cotangent.reshape(rows, width), near), *near_by(*far),
    )

    units = images * steps
    unit_shape = (heads_per_step * (width // HEADS), length)

    def attend_backward(first, last, center, before, more=()):
        def unit_block(shape, index):
            return pl.BlockSpec((1,) + shape, lambda u: index(u + first))

        image = lambda u: (u // steps, 0, 0)
        out = resident((last,) + unit_shape, BF)
        late_half = resident((VIRTUAL // 2, near_rows, width), BF)
        return pl.pallas_call(
            functools.partial(backward_kernel, heads_per_step, first, last - 1),
            grid=(last - first,),
            in_specs=[
                scalars(),
                unit_block((heads_per_step, length, length), lambda u: (u // steps, u % steps, 0, 0)),
                unit_block((width // 128, length, 128), lambda u: (u // steps, 0, 0, 0)),
            ]
            + [unit_block((width, length), image)] * 3
            + [unit_block((HEADS, length), image)]
            + ([whole((first,) + unit_shape)] * 3 + [scalars()] + [pl.BlockSpec(memory_space=pl.ANY)] * 3 if more else [])
            + ([whole((8, width)), whole((VIRTUAL, inner // VIRTUAL))] if more else []),
            out_specs=[whole(out.shape)] * 3 + [whole(late_half.shape)] * (2 if more else 0),
            out_shape=[out] * 3 + [late_half] * (2 if more else 0),
            scratch_shapes=[pltpu.VMEM((3, images, width, length), BF), pltpu.SemaphoreType.DMA((3,))] if more else [],
            compiler_params=params(30, "arbitrary"),
            cost_estimate=cost(1),
            name="attend_backward",
        )(used, *far_off(kept, value_rows, key_t, query_t, mixed_grad_t, center), *near_by(*before), *more)

    rest = (spot, *far_off(lifted_t, lifted_ct, tokens_ct), grad_vectors, grad_up_bias)
    if direct:
        came = swap_cores(send, zero)
        grads = attend_backward(0, 1, center, ())
        came, grads = lax.optimization_barrier((came, grads))
        merged = (keep.astype(F32) + came.astype(F32)).astype(BF).reshape(zero // 2 * dp, early_rows, width)
        groups = [[d * zero + 2 * q + side for d in range(dp) for q in range(zero // 2)] for side in range(2)]
        merged, center = lax.optimization_barrier((merged, center))
        early = lax.all_to_all(merged, ("dp", "zero"), 0, 0, tiled=True, axis_index_groups=groups)
        *grads, keep, send = attend_backward(1, units, center, grads, rest)
        early, keep, send = lax.optimization_barrier((early, keep, send))
        early = jnp.sum(early.astype(F32), axis=0).astype(BF)
    else:
        grads = attend_backward(0, 1, center, ())
        lanes = inner // width
        strip = width // VIRTUAL
        cuts = (lanes // QUARTERS * strip, (lanes // QUARTERS * strip) + inner // VIRTUAL // QUARTERS)
        halves = jnp.stack([keep, send], axis=2).reshape((QUARTERS, VIRTUAL) + keep.shape[2:])
        grad_up = halves[:, :, : cuts[0]].reshape(QUARTERS, VIRTUAL, lanes // QUARTERS, strip, width)
        grad_up = grad_up.transpose(1, 3, 0, 2, 4).reshape(zero, share, lanes, width).transpose(0, 2, 1, 3)
        grad_down = halves[:, :, cuts[0] : cuts[1]].transpose(1, 0, 2, 3).reshape(zero, inner_share, width)
        grad_out = halves[:, :, cuts[1] : cuts[1] + strip // QUARTERS].transpose(1, 0, 2, 3).reshape(zero, share, width)
        early = jnp.concatenate([grad_out, grad_up.reshape(zero, share * lanes, width), grad_down], axis=1)
        early = jnp.sum(lax.all_to_all(early, "zero", 0, 0, tiled=True).astype(F32), axis=0).astype(BF)
        early = exchange_dp(early, dp)
        *grads, keep, send = attend_backward(1, units, center, grads, rest)
    query_grad_t, key_grad_t, value_grad_t = [g.reshape(images, width, length) for g in grads]

    def token_grads(first, last, rank, before):
        def own(shape):
            return pl.BlockSpec((1,) + shape, lambda i: (i + first, 0, 0))

        return pl.pallas_call(
            functools.partial(tokens_kernel, first),
            grid=(last - first,),
            in_specs=[whole((images, length)), own((length, width)), whole(near.shape)]
            + [own((width, length))] * 3
            + [pl.BlockSpec(memory_space=pl.ANY)] * len(before),
            out_specs=own((length, width)),
            out_shape=stored((images, length, width), F32),
            input_output_aliases={6: 0} if before else {},
            compiler_params=params(24, "arbitrary"),
            cost_estimate=cost(1),
            name="token_grads",
        )(
            *far_off(rank, grad_first.reshape(images, length, width), near),
            *near_by(query_grad_t, key_grad_t, value_grad_t),
            *far_off(*before),
        )

    if direct:
        came = swap_cores(send, zero)
        merged = (keep.astype(F32) + came.astype(F32)).astype(BF)
        late = lax.all_to_all(merged, "zero", 0, 0, tiled=True, axis_index_groups=same_core(zero))
        grad_tokens = token_grads(0, images // 2, rank, ())
        late, grad_tokens = lax.optimization_barrier((late, grad_tokens))
        late = jnp.sum(late.astype(F32), axis=0).astype(BF)
        start = me * share
        tail = jnp.concatenate([early, late], axis=0)
        tail, rank = lax.optimization_barrier((tail, rank))
        tail = [tail] + [lax.ppermute(tail, "dp", [(k, k ^ step) for k in range(dp)]) for step in range(1, dp)]
        grad_tokens = token_grads(images // 2, images, rank, (grad_tokens,))
    else:
        halves = by_owner(keep, send)
        strip = width // VIRTUAL
        three = halves[:, : 3 * strip].reshape(VIRTUAL, 3, strip, width).transpose(1, 0, 2, 3).reshape(3, zero, share, width)
        three = three.transpose(1, 0, 2, 3).reshape(zero, 3 * share, width)
        vectors = halves[:, 3 * strip : 3 * strip + 8].reshape(VIRTUAL, 8, width)[0]
        vectors = vectors.reshape(8, zero, share).transpose(1, 0, 2)
        vectors = jnp.pad(vectors, ((0, 0), (0, 0), (0, width - share)))
        bias = jnp.pad(halves[:, -1].reshape(zero, 1, inner_share), ((0, 0), (0, 7), (0, width - inner_share)))
        late = jnp.concatenate([three, vectors, bias], axis=1)
        late = jnp.sum(lax.all_to_all(late, "zero", 0, 0, tiled=True).astype(F32), axis=0).astype(BF)
        start = me * 0
        grad_tokens = token_grads(0, images, rank, ())
        late = jnp.sum(exchange_dp(late, dp).astype(F32), axis=0)

    if direct:
        grad_out_own, grad_up_own, grad_down_own, *three, vectors = pl.pallas_call(
            finish_kernel,
            in_specs=[scalars()] + [pl.BlockSpec(memory_space=pltpu.VMEM)] * dp,
            out_shape=[stored((share, width), F32), stored((share, inner), F32), stored((inner_share, width), F32)]
            + [stored((share, width), F32)] * 3
            + [shaped((near_rows - 3 * share, width), F32)],
            compiler_params=pltpu.CompilerParams(vmem_limit_bytes=16 << 20),
            name="finish",
        )(lax.axis_index("dp").astype(jnp.int32).reshape(1), *tail)
    else:
        lanes = inner // width
        total = jnp.sum(early.astype(F32), axis=0)
        grad_out_own = total[:share]
        grad_up_own = total[share : share * (lanes + 1)].reshape(lanes, share, width).transpose(1, 0, 2).reshape(share, inner)
        grad_down_own = total[share * (lanes + 1) :]
        three = late[: 3 * share].reshape(3, share, width)
        vectors = late[3 * share :]
    cuts = [lax.dynamic_slice(vectors, (k, start), (1, share)).reshape(share) for k in range(8)]
    up_bias_own = vectors[8, :inner_share]
    return (
        layer_out.reshape(images, length, width),
        grad_tokens,
        three[0],
        three[1],
        three[2],
        grad_out_own,
        grad_up_own,
        grad_down_own,
        cuts[0],
        cuts[1],
        cuts[2],
        up_bias_own,
        cuts[3],
        cuts[4],
        cuts[5],
        cuts[6],
        cuts[7],
    )


def solution(mesh):
    batch = P(("dp", "zero"))
    wide = P(("dp", "zero"), None, None)
    flat = P(("dp", "zero"), None)
    matrix = P("zero", None)
    vector = P("zero")
    in_specs = (wide, batch, flat, batch, flat) + (matrix,) * 6 + (vector,) * 9 + (wide,)
    out_specs = (wide, wide) + (matrix,) * 6 + (vector,) * 9
    run = functools.partial(body, zero=mesh.shape["zero"], dp=mesh.shape["dp"])
    return jax.shard_map(run, mesh=mesh, in_specs=in_specs, out_specs=out_specs, check_vma=False)
```

```python
import functools
import math

import jax
import jax.numpy as jnp
import numpy as np
from jax import lax
from jax.experimental import pallas as pl
from jax.experimental.pallas import tpu as pltpu
from jax.sharding import PartitionSpec as P

HEADS = 8
GRID = 32
EPS = 1e-05
LOG2E = 1.4426950408889634
SAFE = 60.0

BF = jnp.bfloat16
F32 = jnp.float32
SMEM = pltpu.SMEM
VIRTUAL = 8
QUARTERS = 4


def nn(left, right):
    return lax.dot_general(left, right, (((1,), (0,)), ((), ())), preferred_element_type=F32)


def nt(left, right):
    return lax.dot_general(left, right, (((1,), (1,)), ((), ())), preferred_element_type=F32)


def position_table(grid, width):
    half = width // 2
    index = np.arange(half)
    freq = np.power(np.float32(10000.0), (2 * (index // 2)).astype(np.float32) / np.float32(half)).astype(np.float32)
    coord = np.arange(grid).astype(np.float32)
    angle = ((coord + np.float32(1.0)) / np.float32(grid + 1e-06) * np.float32(2.0 * math.pi)).astype(np.float32)
    angle = (angle[:, None] / freq).astype(np.float32)
    table = np.where(index % 2 == 0, np.sin(angle), np.cos(angle)).astype(np.float32)
    high = table.astype(BF)
    rest = (table - high.astype(np.float32)).astype(BF)
    whole = np.zeros((4 * grid, width), dtype=BF)
    for group, piece in enumerate((high, high, rest, rest)):
        start = (group % 2) * half
        whole[group * grid : (group + 1) * grid, start : start + half] = piece
    return np.ascontiguousarray(whole.T)


def pack_kernel(where, query, key, value, *refs):
    vectors, up_bias, near, stack = refs[:8], refs[8], refs[9], refs[10]
    share, width = query.shape
    for k, vector in enumerate(vectors):
        stack[k : k + 1, :] = vector[...].astype(F32).reshape(1, share)
    place = lax.broadcasted_iota(jnp.int32, (share, width), 1) - where[0] * share
    spread = jnp.where(place == lax.broadcasted_iota(jnp.int32, (share, width), 0), 1.0, 0.0).astype(BF)
    rows = nn(stack[...].astype(BF), spread)
    bias = jnp.broadcast_to(up_bias[...].astype(F32).reshape(1, width), (8, width))
    last = jnp.concatenate([rows, bias], axis=0).astype(BF)
    for d in range(near.shape[0]):
        near[d, 0:share, :] = query[...]
        near[d, share : 2 * share, :] = key[...]
        near[d, 2 * share : 3 * share, :] = value[...]
        near[d, 3 * share :, :] = last


def prep_kernel(
    counts, rotation, tokens, key_mask, token_order, table, out, down, up,
    lifted_t, lifted_ct, tokens_ct, rank_out, used, *far,
):
    image = pl.program_id(0)
    length = tokens.shape[1]
    slot = lax.broadcasted_iota(jnp.int32, (1, length), 1)
    mask = key_mask[pl.ds(image, 1), :]
    usable = (slot < counts[image]) & ((mask == 1) | (slot == 0))
    flag = jnp.where(usable, 1, 0)
    used[image] = jnp.sum(flag)
    total = flag
    step = 1
    while step < length:
        total = total + jnp.where(slot >= step, pltpu.roll(total, step, 1), 0)
        step *= 2
    rank = jnp.where(usable, total - 1, -1)
    rank_out[pl.ds(image, 1), :] = rank
    cell = token_order[pl.ds(image, 1), :]
    row = cell // GRID
    column = cell - row * GRID
    turn = rotation[image]
    last = GRID - 1
    ycoord = jnp.where(turn == 0, row, jnp.where(turn == 1, column, jnp.where(turn == 2, last - row, last - column)))
    xcoord = jnp.where(turn == 0, column, jnp.where(turn == 1, last - row, jnp.where(turn == 2, last - column, row)))
    place = lax.broadcasted_iota(jnp.int32, (4 * GRID, length), 0)
    group = place // GRID
    wanted = jnp.where(group % 2 == 0, ycoord, xcoord)
    hot = jnp.where(place - group * GRID == wanted, 1.0, 0.0).astype(BF)
    pos_t = nn(table[...], hot)
    tokens_t = tokens[0].T
    low_t = (tokens_t.astype(F32) + pos_t).astype(BF)
    lifted_t[0] = low_t
    both = jnp.concatenate([low_t, tokens_t], axis=0)
    width = low_t.shape[0]
    few = 256
    for block in range(length // few):
        own = slice(block * few, (block + 1) * few)

        @pl.when(block * few < used[image])
        def _(block=block, own=own):
            place = lax.broadcasted_iota(jnp.int32, (few, length), 0) + block * few
            taken = nt(both, jnp.where(place == rank, 1.0, 0.0).astype(BF)).astype(BF)
            lifted_ct[0, :, own] = taken[:width]
            tokens_ct[0, :, own] = taken[width:]

        @pl.when(block * few >= used[image])
        def _(own=own):
            lifted_ct[0, :, own] = jnp.zeros((width, few), BF)
            tokens_ct[0, :, own] = jnp.zeros((width, few), BF)

    if far:

        @pl.when(image == 0)
        def _():
            (bundle,) = far
            share, width = out.shape
            bundle[0 : down.shape[0], :] = down[...]
            bundle[down.shape[0] : down.shape[0] + share, :] = out[...]
            for lane in range(up.shape[1] // width):
                start = down.shape[0] + share * (lane + 1)
                bundle[start : start + share, :] = up[:, lane * width : (lane + 1) * width]


def near_weight(near, k):
    share = near.shape[2] // VIRTUAL
    return jnp.concatenate([near[d, k * share : (k + 1) * share, :] for d in range(VIRTUAL)], axis=0)


def near_vectors(near):
    share = near.shape[2] // VIRTUAL
    total = near[0, 3 * share : 3 * share + 16, :].astype(F32)
    for d in range(1, VIRTUAL):
        total = total + near[d, 3 * share : 3 * share + 16, :].astype(F32)
    return total[:8]


def forward_kernel(
    heads_per_step, used, lifted_t, lifted_ct, tokens_ct, near,
    kept, mixed_t, mixed_rest, inverse, query_t, key_t, value_rows, key_rows, value_ext, spare, calm,
):
    image = pl.program_id(0)
    step = pl.program_id(1)
    width, length = query_t.shape[1:]
    size = width // HEADS
    ext = size + 16
    scale = LOG2E * size ** (-0.5)
    count = used[image]

    @pl.when(step == 0)
    def _():
        weights = [near_weight(near, k) for k in range(3)]
        columns = near_vectors(near).T
        query = (nn(weights[0].T, lifted_t[0]) + columns[:, 0:1]).astype(BF)
        query_t[0] = query
        key = nn(weights[1].T, lifted_ct[0]).astype(BF)
        key_t[0] = key
        value = (nn(weights[2].T, tokens_ct[0]) + columns[:, 1:2]).astype(BF)
        key_turned = key.T
        value_turned = value.T
        for block in range(width // 128):
            part = slice(block * 128, (block + 1) * 128)
            key_rows[block] = key_turned[:, part]
            value_rows[0, block] = value_turned[:, part]
        valid = lax.broadcasted_iota(jnp.int32, (size, length), 1) < count
        first = lax.broadcasted_iota(jnp.int32, (16, length), 0) == 0
        ones = jnp.where(first & valid[:16], 1.0, 0.0).astype(BF)
        for head in range(HEADS):
            value_ext[head * ext : head * ext + size, :] = jnp.where(valid, value[head * size : (head + 1) * size], 0).astype(BF)
            value_ext[head * ext + size : (head + 1) * ext, :] = ones
        wide_query = query.astype(F32)
        wide_key = key.astype(F32)
        query_norm = jnp.max(jnp.sum((wide_query * wide_query).reshape(HEADS, size, length), axis=1), axis=1, keepdims=True)
        key_norm = jnp.max(jnp.sum((wide_key * wide_key).reshape(HEADS, size, length), axis=1), axis=1, keepdims=True)
        reach = jnp.max(query_norm * key_norm) * (scale * scale)
        calm[0] = jnp.where(reach <= SAFE * SAFE, 1, 0)

    group_rows = lax.broadcasted_iota(jnp.int32, (128, length), 0) // size

    def one_head(index, blocks, safe):
        head = step * heads_per_step + index
        block = head // (128 // size)
        inner = head - block * (128 // size)
        span = blocks * 128
        around = query_t[0, pl.ds(pl.multiple_of(block * 128, 128), 128), :]
        own = jnp.where(group_rows == inner, around, 0).astype(BF)
        keys = key_rows[block, :span, :]
        values = value_ext[pl.ds(pl.multiple_of(head * ext, 16), ext), :span]
        def some(cut):
            scores = nn(keys, own[:, cut] if safe else spare[:, cut]) * scale
            if not safe:
                place = lax.broadcasted_iota(jnp.int32, scores.shape, 0)
                scores = jnp.where(place < count, scores, -1e30)
                scores = scores - jnp.max(scores, axis=0, keepdims=True)
            weight = jnp.exp2(scores).astype(BF)
            kept[0, index, :span, cut] = weight
            summed = nn(values, weight)
            turned = 1.0 / summed[size : size + 1, :]
            mixed = summed[:size] * turned
            low = mixed.astype(BF)
            rows = pl.ds(pl.multiple_of(head * size, 32), size)
            mixed_t[0, rows, cut] = low
            mixed_rest[0, rows, cut] = (mixed - low.astype(F32)).astype(BF)
            inverse[0, pl.ds(head, 1), cut] = turned

        if safe:
            some(slice(0, length))
            if blocks % 2:
                kept[0, index, span : span + 128, :] = jnp.zeros((128, length), BF)
        else:
            spare[...] = own
            lax.fori_loop(0, length // 256, lambda part, carry: some(pl.ds(pl.multiple_of(part * 256, 256), 256)), None)

    blocks_used = (count + 127) // 128
    for blocks in range(1, length // 128 + 1):

        @pl.when((calm[0] == 1) & (blocks_used == blocks))
        def _(blocks=blocks):
            for index in range(heads_per_step):
                one_head(index, blocks, True)

    @pl.when(calm[0] == 0)
    def _():
        lax.fori_loop(0, heads_per_step, lambda index, carry: one_head(index, length // 128, False), None)


def norm_parts(field):
    middle = jnp.mean(field, axis=-1, keepdims=True)
    center = field - middle
    spread = jnp.mean(center * center, axis=-1, keepdims=True)
    pull = lax.rsqrt(spread + EPS)
    return center * pull, pull


def norm_back(grad, normal, pull):
    return (grad - jnp.mean(grad, axis=-1, keepdims=True) - normal * jnp.mean(grad * normal, axis=-1, keepdims=True)) * pull


def ffn_kernel(chunk, where, tokens, mixed_t, mixed_rest, inverse, cotangent, near, *refs):
    far, refs = refs[:VIRTUAL], refs[VIRTUAL:]
    layer_out, grad_first, mixed_grad_t, center, keep, send, grad_vectors, grad_up_bias = refs[:8]
    out_sum, up_sum, down_sum, vector_sum, hidden_all, slope_all, up_weight, down_weight, out_weight, up_bias = refs[8:]
    step = pl.program_id(0)
    rows, width = tokens.shape
    inner = hidden_all.shape[1]
    size = width // HEADS
    share = width // VIRTUAL
    part = inner // VIRTUAL

    @pl.when(step == 0)
    def _():
        out_sum[...] = jnp.zeros_like(out_sum)
        up_sum[...] = jnp.zeros_like(up_sum)
        down_sum[...] = jnp.zeros_like(down_sum)
        vector_sum[...] = jnp.zeros_like(vector_sum)
        for side in range(2):
            for slot in range(VIRTUAL // 2):
                ref = far[side * (VIRTUAL // 2) + slot]
                owner = where[0] ^ (2 * slot + side)
                strip = pl.ds(pl.multiple_of(owner * share, share), share)
                down_weight[pl.ds(pl.multiple_of(owner * part, part), part), :] = ref[:part, :]
                out_weight[strip, :] = ref[part : part + share, :]
                for lane in range(inner // width):
                    cut = slice(part + share * (lane + 1), part + share * (lane + 2))
                    up_weight[strip, lane * width : (lane + 1) * width] = ref[cut, :]
        for d in range(VIRTUAL):
            up_bias[:, d * part : (d + 1) * part] = near[d, 3 * share : 3 * share + 16, :].astype(F32)[8:9]

    vectors = near_vectors(near)
    out_bias, down_bias, first_gain, first_shift, second_gain, second_shift = [vectors[k : k + 1, :] for k in range(2, 8)]
    mixed = mixed_t[0].T
    first_sum = tokens[...].astype(F32) + nn(mixed, out_weight[...]) + out_bias
    first_normal, first_pull = norm_parts(first_sum)
    first_norm = first_normal * first_gain + first_shift
    first_low = first_norm.astype(BF)
    second_sum = first_norm + down_bias
    root = math.sqrt(2.0 / math.pi)
    for start in range(0, inner, chunk):
        cut = slice(start, start + chunk)
        pre = (nn(first_low, up_weight[:, cut]) + up_bias[:, cut]).astype(BF)
        square = pre * pre
        gate = jnp.bfloat16(0.5) + jnp.bfloat16(0.5) * jnp.tanh(pre * (jnp.bfloat16(root) + jnp.bfloat16(root * 0.044715) * square))
        hidden = pre * gate
        slope_all[:, cut] = gate + hidden * (jnp.bfloat16(1.0) - gate) * (jnp.bfloat16(2.0 * root) + jnp.bfloat16(6.0 * root * 0.044715) * square)
        hidden_all[:, cut] = hidden
        second_sum = second_sum + nn(hidden, down_weight[cut, :])
    second_normal, second_pull = norm_parts(second_sum)
    layer_out[...] = (second_normal * second_gain + second_shift).astype(BF)
    wide = cotangent[...].astype(F32)
    grad_second = norm_back(wide * second_gain, second_normal, second_pull)
    ffn_grad = grad_second.astype(BF)
    ffn_grad_t = ffn_grad.T
    first_low_t = first_low.T
    ones = jnp.where(lax.broadcasted_iota(jnp.int32, (16, rows), 0) == 0, 1.0, 0.0).astype(BF)
    first_ext = jnp.concatenate([first_low_t, ones], axis=0)
    back = grad_second
    for start in range(0, inner, chunk):
        cut = slice(start, start + chunk)
        hidden_grad = nt(ffn_grad, down_weight[cut, :]).astype(BF) * slope_all[:, cut]
        down_sum[:, cut] += nn(ffn_grad_t, hidden_all[:, cut])
        up_sum[:, cut] += nn(first_ext, hidden_grad)
        back = back + nt(hidden_grad, up_weight[:, cut])
    first = norm_back(back * first_gain, first_normal, first_pull)
    grad_first[...] = first
    branch_grad = first.astype(BF)
    out_sum[...] += nn(mixed_t[0], branch_grad)
    mixed_grad = nt(out_weight[...], branch_grad).reshape(HEADS, size, rows)
    turned = inverse[0]
    scaled = (mixed_grad * turned[:, None, :]).astype(BF)
    mixed_grad_t[0] = scaled.reshape(width, rows)
    mixed_whole = mixed_t[0].astype(F32) + mixed_rest[0].astype(F32)
    center[0] = jnp.sum(scaled.astype(F32) * mixed_whole.reshape(HEADS, size, rows), axis=1)
    sums = (
        branch_grad.astype(F32), ffn_grad.astype(F32), back * first_normal, back, wide * second_normal, wide,
    )
    vector_sum[...] += jnp.concatenate(
        [jnp.zeros((2, width), F32)] + [jnp.sum(piece, axis=0, keepdims=True) for piece in sums], axis=0
    )

    @pl.when(step == pl.num_programs(0) - 1)
    def _():
        lanes = inner // width // QUARTERS
        few = share // QUARTERS
        for slot in range(VIRTUAL // 2):
            for ref, side in ((keep, where[0] % 2), (send, 1 - where[0] % 2)):
                owner = 2 * slot + side
                start = pl.multiple_of(owner * share, share)
                turned_down = down_sum[:, pl.ds(pl.multiple_of(owner * part, part), part)].astype(BF).T
                for quarter in range(QUARTERS):
                    for lane in range(lanes):
                        place = (quarter * lanes + lane) * width
                        ref[quarter, slot, lane * share : (lane + 1) * share, :] = up_sum[pl.ds(start, share), place : place + width].astype(BF)
                    low = lanes * share
                    high = low + part // QUARTERS
                    ref[quarter, slot, low:high, :] = turned_down[quarter * (part // QUARTERS) : (quarter + 1) * (part // QUARTERS)]
                    out = out_sum[pl.ds(start + quarter * few, few), :]
                    ref[quarter, slot, high:, :] = jnp.concatenate([out] * (16 // few), axis=0).astype(BF)
        for d in range(VIRTUAL):
            grad_up_bias[d : d + 1, :] = up_sum[width : width + 1, d * part : (d + 1) * part]
        grad_vectors[...] = vector_sum[...]


def backward_kernel(heads_per_step, first_unit, last_unit, used, kept, value_rows, key_t, query_t, mixed_grad_t, center, *refs):
    whole_job = len(refs) > 5
    if whole_job:
        earlier, (where, lifted_t, lifted_ct, tokens_ct, early_vectors, up_bias), refs = refs[:3], refs[3:9], refs[9:]
        query_grad_t, key_grad_t, value_grad_t, keep, send, weight_turned, grad_turned, held, arrived = refs
    else:
        query_grad_t, key_grad_t, value_grad_t, weight_turned, grad_turned = refs
    steps = HEADS // heads_per_step
    unit = pl.program_id(0) + first_unit
    image = unit // steps
    step = unit - image * steps
    width, length = query_t.shape[1:]
    size = width // HEADS
    share = width // VIRTUAL
    scale = size ** (-0.5)
    count = used[image]
    blocks_used = (count + 127) // 128
    group_rows = lax.broadcasted_iota(jnp.int32, (128, length), 0) // size
    at = unit if whole_job else 0

    if whole_job:
        targets = [held.at[k] for k in range(3)] + [ref.at[0:first_unit] for ref in (query_grad_t, key_grad_t, value_grad_t)]
        copies = [
            pltpu.make_async_copy(source, target, arrived.at[k])
            for k, (source, target) in enumerate(zip((lifted_t, lifted_ct, tokens_ct, *earlier), targets))
        ]

        @pl.when(unit == first_unit + 2)
        def _():
            for copy in copies:
                copy.start()

    def one_head(index, blocks):
        head = step * heads_per_step + index
        block = head // (128 // size)
        inner = head - block * (128 // size)
        span = blocks * 128
        head_rows = pl.ds(pl.multiple_of(head * size, 32), size)
        own_rows = slice(index * size, (index + 1) * size)
        around = mixed_grad_t[0, pl.ds(pl.multiple_of(block * 128, 128), 128), :]
        own = jnp.where(group_rows == inner, around, 0).astype(BF)
        values = value_rows[0, block, :span, :]
        keys = key_t[0, head_rows, :span]
        weight = kept[0, index, :span, :]
        weight_turned[index, :, :span] = weight.T
        pulled = nn(values, own) - center[0, pl.ds(head, 1), :]
        score_grad = (weight.astype(F32) * pulled).astype(BF)
        grad_turned[index, :, :span] = score_grad.T
        query_grad_t[at, own_rows, :] = (nn(keys, score_grad) * scale).astype(BF)
        value_sum = nn(mixed_grad_t[0, head_rows, :], weight_turned[index, :, :span])
        key_sum = nn(query_t[0, head_rows, :], grad_turned[index, :, :span])
        valid = lax.broadcasted_iota(jnp.int32, (size, span), 1) < count
        value_grad_t[at, own_rows, :span] = jnp.where(valid, value_sum, 0.0).astype(BF)
        key_grad_t[at, own_rows, :span] = jnp.where(valid, key_sum * scale, 0.0).astype(BF)
        if span < length:
            value_grad_t[at, own_rows, span:] = jnp.zeros((size, length - span), BF)
            key_grad_t[at, own_rows, span:] = jnp.zeros((size, length - span), BF)

    for blocks in range(2, length // 128 + 1, 2):

        @pl.when((blocks_used == blocks) | (blocks_used == blocks - 1))
        def _(blocks=blocks):
            for index in range(heads_per_step):
                one_head(index, blocks)

    if whole_job:

        @pl.when(unit == last_unit)
        def _():
            for copy in copies:
                copy.wait()
            ones = jnp.ones((16, length), BF)
            sums = [None] * 3
            for one in range(held.shape[1]):
                units = slice(one * steps, (one + 1) * steps)
                turned = [ref[units].reshape(width, length) for ref in (query_grad_t, key_grad_t, value_grad_t)]
                for k in range(3):
                    left = held[k, one]
                    added = nt(left if k == 1 else jnp.concatenate([left, ones], axis=0), turned[k])
                    sums[k] = added if sums[k] is None else sums[k] + added
            vectors = jnp.concatenate([sums[0][width : width + 1], sums[2][width : width + 1], early_vectors[2:8, :]], axis=0)
            for k in range(3):
                low = sums[k][:width].astype(BF)
                for owner in range(VIRTUAL):
                    mine = where[0] % 2 == owner % 2
                    piece = low[owner * share : (owner + 1) * share]

                    @pl.when(mine)
                    def _(owner=owner, piece=piece, k=k):
                        keep[owner // 2, k * share : (k + 1) * share, :] = piece

                    @pl.when(jnp.logical_not(mine))
                    def _(owner=owner, piece=piece, k=k):
                        send[owner // 2, k * share : (k + 1) * share, :] = piece

            for slot in range(VIRTUAL // 2):
                for ref, side in ((keep, where[0] % 2), (send, 1 - where[0] % 2)):
                    bias = jnp.broadcast_to(up_bias[pl.ds(2 * slot + side, 1), :], (8, width))
                    ref[slot, 3 * share :, :] = jnp.concatenate([vectors, bias], axis=0).astype(BF)


def finish_kernel(place, *refs):
    pieces, others, (grad_out, grad_up, grad_down, *rest) = refs[:QUARTERS], refs[:QUARTERS], refs[QUARTERS:]
    share, width = grad_out.shape
    lanes = grad_up.shape[1] // width // QUARTERS
    part = grad_down.shape[0] // QUARTERS
    few = share // QUARTERS
    early_rows = lanes * share + part + 16
    for far, ref in enumerate(pieces):
        owner = place[0] ^ far
        piece = ref[:early_rows, :].astype(F32)
        for lane in range(lanes):
            at = pl.multiple_of((owner * lanes + lane) * width, width)
            grad_up[:, pl.ds(at, width)] = piece[lane * share : (lane + 1) * share]
        grad_down[pl.ds(pl.multiple_of(owner * part, part), part), :] = piece[lanes * share : lanes * share + part]
        grad_out[pl.ds(pl.multiple_of(owner * few, few), few), :] = piece[lanes * share + part : lanes * share + part + few]
    sums = [ref[early_rows:, :].astype(F32) for ref in others]
    while len(sums) > 1:
        sums = [sums[k] + sums[k + 1] for k in range(0, len(sums), 2)]
    for k in range(3):
        rest[k][...] = sums[0][k * share : (k + 1) * share]
    vectors = sums[0][3 * share :]
    rest[11][...] = vectors[8, :]
    turned = pltpu.roll(vectors, width - place[1] * share, 1)
    for k in range(8):
        rest[3 + k][...] = turned[k, :share]


def tokens_kernel(first, rank, grad_first, near, query_grad_t, key_grad_t, value_grad_t, *refs):
    grad_tokens = refs[-1]
    image = pl.program_id(0) + first
    length = query_grad_t.shape[2]
    width = query_grad_t.shape[1]
    compact = lax.broadcasted_iota(jnp.int32, (length, length), 0)
    chosen = jnp.where(compact == rank[pl.ds(image, 1), :], 1.0, 0.0).astype(BF)
    both = nn(jnp.concatenate([key_grad_t[0], value_grad_t[0]], axis=0), chosen).astype(BF)
    weights = [near_weight(near, k) for k in range(3)]
    total_t = nn(weights[0], query_grad_t[0]) + nn(weights[1], both[:width]) + nn(weights[2], both[width:])
    grad_tokens[0] = grad_first[0] + total_t.T


def params(mebibytes, *semantics):
    return pltpu.CompilerParams(dimension_semantics=semantics, vmem_limit_bytes=mebibytes << 20)


def cost(microseconds):
    return pl.CostEstimate(flops=int(microseconds * 1.0e9), bytes_accessed=1 << 20, transcendentals=0)


def whole(shape):
    return pl.BlockSpec(shape, lambda *_: (0,) * len(shape))


def per_image(shape):
    return pl.BlockSpec((1,) + shape, lambda i, *_: (i,) + (0,) * len(shape))


def scalars():
    return pl.BlockSpec(memory_space=SMEM)


def shaped(shape, dtype):
    return jax.ShapeDtypeStruct(shape, dtype)


def resident(shape, dtype):
    return pltpu.VMEM(shape, dtype)


def stored(shape, dtype):
    return pltpu.HBM(shape, dtype)


def near_by(*arrays):
    return [pltpu.with_memory_space_constraint(array, pltpu.VMEM) for array in arrays]


def far_off(*arrays):
    return [pltpu.with_memory_space_constraint(array, pltpu.HBM) for array in arrays]


def exchange_dp(field, dp):
    return lax.all_to_all(jnp.broadcast_to(field, (dp,) + field.shape), "dp", 0, 0, tiled=True)


def same_core(zero):
    return [[k for k in range(zero) if k % 2 == side] for side in range(2)]


def swap_cores(send, zero):
    return lax.ppermute(send, "zero", [(k, k ^ 1) for k in range(zero)])


def by_owner(keep, send):
    return jnp.stack([keep, send], axis=1).reshape((VIRTUAL,) + keep.shape[1:])


def body(
    tokens, counts, key_mask, rotation, token_order, query_weight, key_weight, value_weight, out_weight, up_weight,
    down_weight, query_bias, value_bias, out_bias, up_bias, down_bias, first_gain, first_shift, second_gain,
    second_shift, cotangent, *, zero, dp,
):
    images, length, width = tokens.shape
    rows = images * length
    inner = up_weight.shape[1]
    share = width // zero
    inner_share = inner // zero
    direct = zero == VIRTUAL and dp == QUARTERS
    heads_per_step = 2
    steps = HEADS // heads_per_step
    me = lax.axis_index("zero")
    spot = (me if direct else me * 0).astype(jnp.int32).reshape(1)

    small = [query_bias, value_bias, out_bias, down_bias, first_gain, first_shift, second_gain, second_shift]
    near_rows = 3 * (width // VIRTUAL) + 16
    far_rows = (2 * inner + width) // VIRTUAL
    if direct:
        near = pl.pallas_call(
            pack_kernel,
            in_specs=[scalars()] + [pl.BlockSpec(memory_space=pltpu.VMEM)] * 12,
            out_shape=shaped((zero, near_rows, width), BF),
            scratch_shapes=[pltpu.VMEM((8, share), F32)],
            name="pack",
        )(me.astype(jnp.int32).reshape(1), query_weight, key_weight, value_weight, *small, up_bias)
        near = lax.all_to_all(near, "zero", 0, 0, tiled=True)
    else:
        gather = functools.partial(lax.all_gather, axis_name="zero", axis=0, tiled=True)
        shards = [gather(w).reshape(VIRTUAL, -1, width) for w in (query_weight, key_weight, value_weight)]
        vectors = jnp.zeros((VIRTUAL, 8, width), BF).at[0].set(jnp.stack([gather(v) for v in small]))
        biases = jnp.broadcast_to(gather(up_bias).reshape(VIRTUAL, 1, inner // VIRTUAL), (VIRTUAL, 8, inner // VIRTUAL))
        near = jnp.concatenate(shards + [vectors, biases], axis=1)
        lanes = gather(up_weight).reshape(VIRTUAL, width // VIRTUAL, inner // width, width).transpose(0, 2, 1, 3)
        shards = [gather(w).reshape(VIRTUAL, -1, width) for w in (down_weight, out_weight)]
        far = jnp.concatenate(shards + [lanes.reshape(VIRTUAL, -1, width)], axis=1)
        far = [far[2 * slot + side] for side in range(2) for slot in range(VIRTUAL // 2)]

    table = jnp.asarray(position_table(GRID, width))
    turned = stored((images, width, length), BF)
    bundle = [shaped((far_rows, width), BF)] if direct else []
    lifted_t, lifted_ct, tokens_ct, rank, used, *mine = pl.pallas_call(
        prep_kernel,
        grid=(images,),
        in_specs=[
            scalars(), scalars(), per_image((length, width)), whole((images, length)), whole((images, length)),
            whole(table.shape), whole(out_weight.shape), whole(down_weight.shape), whole(up_weight.shape),
        ],
        out_specs=[per_image((width, length))] * 3 + [whole((images, length)), scalars()] + [whole(b.shape) for b in bundle],
        out_shape=[turned] * 3 + [stored((images, length), jnp.int32), shaped((images,), jnp.int32)] + bundle,
        compiler_params=params(40, "arbitrary"),
        name="prep",
    )(counts, rotation, *far_off(tokens, key_mask, token_order, table, out_weight, down_weight, up_weight))
    if direct:
        mine = mine + [lax.ppermute(mine[0], "zero", [(k, k ^ (2 * step)) for k in range(zero)]) for step in range(1, zero // 2)]

    head_block = pl.BlockSpec((1, heads_per_step, length, length), lambda i, s: (i, s, 0, 0))
    kept, mixed_t, mixed_rest, inverse, query_t, key_t, value_rows = pl.pallas_call(
        functools.partial(forward_kernel, heads_per_step),
        grid=(images, steps),
        in_specs=[scalars()] + [per_image((width, length))] * 3 + [whole(near.shape)],
        out_specs=[
            head_block, per_image((width, length)), per_image((width, length)), per_image((HEADS, length)), per_image((width, length)),
            per_image((width, length)), per_image((width // 128, length, 128)),
        ],
        out_shape=[
            stored((images, HEADS, length, length), BF), turned, turned, stored((images, HEADS, length), F32), turned, turned,
            stored((images, width // 128, length, 128), BF),
        ],
        scratch_shapes=[
            pltpu.VMEM((width // 128, length, 128), BF),
            pltpu.VMEM((width + 16 * HEADS, length), BF),
            pltpu.VMEM((128, length), BF),
            pltpu.SMEM((1,), jnp.int32),
        ],
        compiler_params=params(30, "arbitrary", "arbitrary"),
        cost_estimate=cost(22),
        name="attend_forward",
    )(used, *far_off(lifted_t, lifted_ct, tokens_ct), *near_by(near))

    if direct:
        mine, mixed_t = lax.optimization_barrier((mine, mixed_t))
        far = mine + [swap_cores(piece, zero) for piece in mine]
    block = length
    per = length // block
    row_block = pl.BlockSpec((block, width), lambda s: (s, 0))

    def turned_block(height):
        return pl.BlockSpec((1, height, block), lambda s: (s // per, 0, s % per))

    early_rows = 2 * inner // VIRTUAL // QUARTERS + 16
    half = resident((QUARTERS, VIRTUAL // 2, early_rows, width), BF)
    layer_out, grad_first, mixed_grad_t, center, keep, send, grad_vectors, grad_up_bias = pl.pallas_call(
        functools.partial(ffn_kernel, 256),
        grid=(rows // block,),
        in_specs=[
            scalars(), row_block, turned_block(width), turned_block(width), turned_block(HEADS), row_block, whole(near.shape),
        ]
        + [whole(piece.shape) for piece in far],
        out_specs=[
            row_block, row_block, turned_block(width), turned_block(HEADS), whole(half.shape), whole(half.shape),
            whole((8, width)), whole((VIRTUAL, inner // VIRTUAL)),
        ],
        out_shape=[
            stored((rows, width), BF), stored((rows, width), F32), turned, stored((images, HEADS, length), F32),
            half, half, shaped((8, width), F32), shaped((VIRTUAL, inner // VIRTUAL), F32),
        ],
        scratch_shapes=[
            pltpu.VMEM((width, width), F32), pltpu.VMEM((width + 16, inner), F32), pltpu.VMEM((width, inner), F32),
            pltpu.VMEM((8, width), F32), pltpu.VMEM((block, inner), BF), pltpu.VMEM((block, inner), BF),
            pltpu.VMEM((width, inner), BF), pltpu.VMEM((inner, width), BF), pltpu.VMEM((width, width), BF),
            pltpu.VMEM((1, inner), F32),
        ],
        compiler_params=params(50, "arbitrary"),
        cost_estimate=cost(27),
        name="feed_forward",
    )(
        spot, *far_off(tokens.reshape(rows, width)), *far_off(mixed_t, mixed_rest, inverse),
        *far_off(cotangent.reshape(rows, width), near), *near_by(*far),
    )

    units = images * steps
    unit_shape = (heads_per_step * (width // HEADS), length)

    def attend_backward(first, last, center, before, more=()):
        def unit_block(shape, index):
            return pl.BlockSpec((1,) + shape, lambda u: index(u + first))

        image = lambda u: (u // steps, 0, 0)
        out = (resident if more else stored)((last,) + unit_shape, BF)
        late_half = stored((VIRTUAL // 2, near_rows, width), BF)
        return pl.pallas_call(
            functools.partial(backward_kernel, heads_per_step, first, last - 1),
            grid=(last - first,),
            in_specs=[
                scalars(),
                unit_block((heads_per_step, length, length), lambda u: (u // steps, u % steps, 0, 0)),
                unit_block((width // 128, length, 128), lambda u: (u // steps, 0, 0, 0)),
            ]
            + [unit_block((width, length), image)] * 3
            + [unit_block((HEADS, length), image)]
            + ([pl.BlockSpec(memory_space=pl.ANY)] * 3 + [scalars()] + [pl.BlockSpec(memory_space=pl.ANY)] * 3 if more else [])
            + ([whole((8, width)), whole((VIRTUAL, inner // VIRTUAL))] if more else []),
            out_specs=[whole(out.shape)] * 3 + [whole(late_half.shape)] * (2 if more else 0),
            out_shape=[out] * 3 + [late_half] * (2 if more else 0),
            scratch_shapes=[pltpu.VMEM((heads_per_step, length, length), BF)] * 2
            + ([pltpu.VMEM((3, images, width, length), BF), pltpu.SemaphoreType.DMA((6,))] if more else []),
            compiler_params=params(40, "arbitrary"),
            cost_estimate=cost(1),
            name="attend_backward",
        )(used, *far_off(kept, value_rows, key_t, query_t, mixed_grad_t, center, *before), *more)

    rest = (spot, *far_off(lifted_t, lifted_ct, tokens_ct), grad_vectors, grad_up_bias)
    if direct:
        came = swap_cores(send, zero)
        grads = attend_backward(0, 1, center, ())
        came, grads = lax.optimization_barrier((came, grads))
        merged = (keep.astype(F32) + came.astype(F32)).astype(BF).reshape(zero // 2 * dp, early_rows, width)
        groups = [[d * zero + 2 * q + side for d in range(dp) for q in range(zero // 2)] for side in range(2)]
        merged, center = lax.optimization_barrier((merged, center))
        early = lax.all_to_all(merged, ("dp", "zero"), 0, 0, tiled=True, axis_index_groups=groups)
        *grads, keep, send = attend_backward(1, units, center, grads, rest)
        early, send = lax.optimization_barrier((early, send))
        early = jnp.sum(early.astype(F32), axis=0).astype(BF)
    else:
        grads = attend_backward(0, 1, center, ())
        lanes = inner // width
        strip = width // VIRTUAL
        cuts = (lanes // QUARTERS * strip, (lanes // QUARTERS * strip) + inner // VIRTUAL // QUARTERS)
        halves = jnp.stack([keep, send], axis=2).reshape((QUARTERS, VIRTUAL) + keep.shape[2:])
        grad_up = halves[:, :, : cuts[0]].reshape(QUARTERS, VIRTUAL, lanes // QUARTERS, strip, width)
        grad_up = grad_up.transpose(1, 3, 0, 2, 4).reshape(zero, share, lanes, width).transpose(0, 2, 1, 3)
        grad_down = halves[:, :, cuts[0] : cuts[1]].transpose(1, 0, 2, 3).reshape(zero, inner_share, width)
        grad_out = halves[:, :, cuts[1] : cuts[1] + strip // QUARTERS].transpose(1, 0, 2, 3).reshape(zero, share, width)
        early = jnp.concatenate([grad_out, grad_up.reshape(zero, share * lanes, width), grad_down], axis=1)
        early = jnp.sum(lax.all_to_all(early, "zero", 0, 0, tiled=True).astype(F32), axis=0).astype(BF)
        early = exchange_dp(early, dp)
        *grads, keep, send = attend_backward(1, units, center, grads, rest)
    query_grad_t, key_grad_t, value_grad_t = [g.reshape(images, width, length) for g in grads]

    def token_grads(first, last, rank, before):
        def own(shape):
            return pl.BlockSpec((1,) + shape, lambda i: (i + first, 0, 0))

        return pl.pallas_call(
            functools.partial(tokens_kernel, first),
            grid=(last - first,),
            in_specs=[whole((images, length)), own((length, width)), whole(near.shape)]
            + [own((width, length))] * 3
            + [pl.BlockSpec(memory_space=pl.ANY)] * len(before),
            out_specs=own((length, width)),
            out_shape=stored((images, length, width), F32),
            input_output_aliases={6: 0} if before else {},
            compiler_params=params(24, "arbitrary"),
            cost_estimate=cost(1),
            name="token_grads",
        )(
            *far_off(rank, grad_first.reshape(images, length, width), near),
            *near_by(query_grad_t, key_grad_t, value_grad_t),
            *far_off(*before),
        )

    if direct:
        came = swap_cores(send, zero)
        early, came = lax.optimization_barrier((early, came))
        merged = (keep.astype(F32) + came.astype(F32)).astype(BF)
        late = lax.all_to_all(merged, "zero", 0, 0, tiled=True, axis_index_groups=same_core(zero))
        grad_tokens = token_grads(0, images // 2, rank, ())
        late, grad_tokens = lax.optimization_barrier((late, grad_tokens))
        late = jnp.sum(late.astype(F32), axis=0).astype(BF)
        tail = jnp.concatenate([early, late], axis=0)
        tail, rank = lax.optimization_barrier((tail, rank))
        tail = [tail] + [lax.ppermute(tail, "dp", [(k, k ^ step) for k in range(dp)]) for step in range(1, dp)]
        grad_tokens = token_grads(images // 2, images, rank, (grad_tokens,))
    else:
        halves = by_owner(keep, send)
        strip = width // VIRTUAL
        three = halves[:, : 3 * strip].reshape(VIRTUAL, 3, strip, width).transpose(1, 0, 2, 3).reshape(3, zero, share, width)
        three = three.transpose(1, 0, 2, 3).reshape(zero, 3 * share, width)
        vectors = halves[:, 3 * strip : 3 * strip + 8].reshape(VIRTUAL, 8, width)[0]
        vectors = vectors.reshape(8, zero, share).transpose(1, 0, 2)
        vectors = jnp.pad(vectors, ((0, 0), (0, 0), (0, width - share)))
        bias = jnp.pad(halves[:, -1].reshape(zero, 1, inner_share), ((0, 0), (0, 7), (0, width - inner_share)))
        late = jnp.concatenate([three, vectors, bias], axis=1)
        late = jnp.sum(lax.all_to_all(late, "zero", 0, 0, tiled=True).astype(F32), axis=0).astype(BF)
        grad_tokens = token_grads(0, images, rank, ())
        late = jnp.sum(exchange_dp(late, dp).astype(F32), axis=0)

    if direct:
        grad_out_own, grad_up_own, grad_down_own, *three = pl.pallas_call(
            finish_kernel,
            in_specs=[scalars()] + [pl.BlockSpec(memory_space=pltpu.VMEM)] * dp,
            out_shape=[stored((share, width), F32), stored((share, inner), F32), stored((inner_share, width), F32)]
            + [stored((share, width), F32)] * 3
            + [shaped((share,), F32)] * 8
            + [shaped((inner_share,), F32)],
            compiler_params=pltpu.CompilerParams(vmem_limit_bytes=16 << 20),
            name="finish",
        )(jnp.stack([lax.axis_index("dp"), me]).astype(jnp.int32), *tail)
        *cuts, up_bias_own = three[3:]
    else:
        lanes = inner // width
        total = jnp.sum(early.astype(F32), axis=0)
        grad_out_own = total[:share]
        grad_up_own = total[share : share * (lanes + 1)].reshape(lanes, share, width).transpose(1, 0, 2).reshape(share, inner)
        grad_down_own = total[share * (lanes + 1) :]
        three = late[: 3 * share].reshape(3, share, width)
        vectors = late[3 * share :]
        cuts = [vectors[k, :share] for k in range(8)]
        up_bias_own = vectors[8, :inner_share]
    return (
        layer_out.reshape(images, length, width),
        grad_tokens,
        three[0],
        three[1],
        three[2],
        grad_out_own,
        grad_up_own,
        grad_down_own,
        cuts[0],
        cuts[1],
        cuts[2],
        up_bias_own,
        cuts[3],
        cuts[4],
        cuts[5],
        cuts[6],
        cuts[7],
    )


def solution(mesh):
    batch = P(("dp", "zero"))
    wide = P(("dp", "zero"), None, None)
    flat = P(("dp", "zero"), None)
    matrix = P("zero", None)
    vector = P("zero")
    in_specs = (wide, batch, flat, batch, flat) + (matrix,) * 6 + (vector,) * 9 + (wide,)
    out_specs = (wide, wide) + (matrix,) * 6 + (vector,) * 9
    run = functools.partial(body, zero=mesh.shape["zero"], dp=mesh.shape["dp"])
    return jax.shard_map(run, mesh=mesh, in_specs=in_specs, out_specs=out_specs, check_vma=False)
```

```python
import functools
import math

import jax
import jax.numpy as jnp
import numpy as np
from jax import lax
from jax.experimental import pallas as pl
from jax.experimental.pallas import tpu as pltpu
from jax.sharding import PartitionSpec as P

HEADS = 8
GRID = 32
EPS = 1e-05
LOG2E = 1.4426950408889634
SAFE = 60.0

BF = jnp.bfloat16
F32 = jnp.float32
SMEM = pltpu.SMEM
VIRTUAL = 8
QUARTERS = 4


def nn(left, right):
    return lax.dot_general(left, right, (((1,), (0,)), ((), ())), preferred_element_type=F32)


def nt(left, right):
    return lax.dot_general(left, right, (((1,), (1,)), ((), ())), preferred_element_type=F32)


def position_table(grid, width):
    half = width // 2
    index = np.arange(half)
    freq = np.power(np.float32(10000.0), (2 * (index // 2)).astype(np.float32) / np.float32(half)).astype(np.float32)
    coord = np.arange(grid).astype(np.float32)
    angle = ((coord + np.float32(1.0)) / np.float32(grid + 1e-06) * np.float32(2.0 * math.pi)).astype(np.float32)
    angle = (angle[:, None] / freq).astype(np.float32)
    table = np.where(index % 2 == 0, np.sin(angle), np.cos(angle)).astype(np.float32)
    high = table.astype(BF)
    rest = (table - high.astype(np.float32)).astype(BF)
    whole = np.zeros((4 * grid, width), dtype=BF)
    for group, piece in enumerate((high, high, rest, rest)):
        start = (group % 2) * half
        whole[group * grid : (group + 1) * grid, start : start + half] = piece
    return np.ascontiguousarray(whole.T)


def pack_kernel(where, query, key, value, *refs):
    vectors, up_bias, near, stack = refs[:8], refs[8], refs[9], refs[10]
    share, width = query.shape
    for k, vector in enumerate(vectors):
        stack[k : k + 1, :] = vector[...].astype(F32).reshape(1, share)
    place = lax.broadcasted_iota(jnp.int32, (share, width), 1) - where[0] * share
    spread = jnp.where(place == lax.broadcasted_iota(jnp.int32, (share, width), 0), 1.0, 0.0).astype(BF)
    rows = nn(stack[...].astype(BF), spread)
    bias = jnp.broadcast_to(up_bias[...].astype(F32).reshape(1, width), (8, width))
    last = jnp.concatenate([rows, bias], axis=0).astype(BF)
    for d in range(near.shape[0]):
        near[d, 0:share, :] = query[...]
        near[d, share : 2 * share, :] = key[...]
        near[d, 2 * share : 3 * share, :] = value[...]
        near[d, 3 * share :, :] = last


def prep_kernel(
    counts, rotation, tokens, key_mask, token_order, table, out, down, up,
    lifted_t, lifted_ct, tokens_ct, rank_out, used, *far,
):
    image = pl.program_id(0)
    length = tokens.shape[1]
    slot = lax.broadcasted_iota(jnp.int32, (1, length), 1)
    mask = key_mask[pl.ds(image, 1), :]
    usable = (slot < counts[image]) & ((mask == 1) | (slot == 0))
    flag = jnp.where(usable, 1, 0)
    used[image] = jnp.sum(flag)
    total = flag
    step = 1
    while step < length:
        total = total + jnp.where(slot >= step, pltpu.roll(total, step, 1), 0)
        step *= 2
    rank = jnp.where(usable, total - 1, -1)
    rank_out[pl.ds(image, 1), :] = rank
    cell = token_order[pl.ds(image, 1), :]
    row = cell // GRID
    column = cell - row * GRID
    turn = rotation[image]
    last = GRID - 1
    ycoord = jnp.where(turn == 0, row, jnp.where(turn == 1, column, jnp.where(turn == 2, last - row, last - column)))
    xcoord = jnp.where(turn == 0, column, jnp.where(turn == 1, last - row, jnp.where(turn == 2, last - column, row)))
    place = lax.broadcasted_iota(jnp.int32, (4 * GRID, length), 0)
    group = place // GRID
    wanted = jnp.where(group % 2 == 0, ycoord, xcoord)
    hot = jnp.where(place - group * GRID == wanted, 1.0, 0.0).astype(BF)
    pos_t = nn(table[...], hot)
    tokens_t = tokens[0].T
    low_t = (tokens_t.astype(F32) + pos_t).astype(BF)
    lifted_t[0] = low_t
    both = jnp.concatenate([low_t, tokens_t], axis=0)
    width = low_t.shape[0]
    few = 256
    for block in range(length // few):
        own = slice(block * few, (block + 1) * few)

        @pl.when(block * few < used[image])
        def _(block=block, own=own):
            place = lax.broadcasted_iota(jnp.int32, (few, length), 0) + block * few
            taken = nt(both, jnp.where(place == rank, 1.0, 0.0).astype(BF)).astype(BF)
            lifted_ct[0, :, own] = taken[:width]
            tokens_ct[0, :, own] = taken[width:]

        @pl.when(block * few >= used[image])
        def _(own=own):
            lifted_ct[0, :, own] = jnp.zeros((width, few), BF)
            tokens_ct[0, :, own] = jnp.zeros((width, few), BF)

    if far:

        @pl.when(image == 0)
        def _():
            (bundle,) = far
            share, width = out.shape
            bundle[0 : down.shape[0], :] = down[...]
            bundle[down.shape[0] : down.shape[0] + share, :] = out[...]
            for lane in range(up.shape[1] // width):
                start = down.shape[0] + share * (lane + 1)
                bundle[start : start + share, :] = up[:, lane * width : (lane + 1) * width]


def near_weight(near, k):
    share = near.shape[2] // VIRTUAL
    return jnp.concatenate([near[d, k * share : (k + 1) * share, :] for d in range(VIRTUAL)], axis=0)


def near_vectors(near):
    share = near.shape[2] // VIRTUAL
    total = near[0, 3 * share : 3 * share + 16, :].astype(F32)
    for d in range(1, VIRTUAL):
        total = total + near[d, 3 * share : 3 * share + 16, :].astype(F32)
    return total[:8]


def forward_kernel(
    heads_per_step, used, lifted_t, lifted_ct, tokens_ct, near,
    kept, mixed_t, mixed_rest, inverse, query_t, key_t, value_rows, key_rows, value_ext, spare, calm,
):
    image = pl.program_id(0)
    step = pl.program_id(1)
    width, length = query_t.shape[1:]
    size = width // HEADS
    ext = size + 16
    scale = LOG2E * size ** (-0.5)
    count = used[image]

    @pl.when(step == 0)
    def _():
        weights = [near_weight(near, k) for k in range(3)]
        columns = near_vectors(near).T
        query = (nn(weights[0].T, lifted_t[0]) + columns[:, 0:1]).astype(BF)
        query_t[0] = query
        key = nn(weights[1].T, lifted_ct[0]).astype(BF)
        key_t[0] = key
        value = (nn(weights[2].T, tokens_ct[0]) + columns[:, 1:2]).astype(BF)
        key_turned = key.T
        value_turned = value.T
        for block in range(width // 128):
            part = slice(block * 128, (block + 1) * 128)
            key_rows[block] = key_turned[:, part]
            value_rows[0, block] = value_turned[:, part]
        valid = lax.broadcasted_iota(jnp.int32, (size, length), 1) < count
        first = lax.broadcasted_iota(jnp.int32, (16, length), 0) == 0
        ones = jnp.where(first & valid[:16], 1.0, 0.0).astype(BF)
        for head in range(HEADS):
            value_ext[head * ext : head * ext + size, :] = jnp.where(valid, value[head * size : (head + 1) * size], 0).astype(BF)
            value_ext[head * ext + size : (head + 1) * ext, :] = ones
        wide_query = query.astype(F32)
        wide_key = key.astype(F32)
        query_norm = jnp.max(jnp.sum((wide_query * wide_query).reshape(HEADS, size, length), axis=1), axis=1, keepdims=True)
        key_norm = jnp.max(jnp.sum((wide_key * wide_key).reshape(HEADS, size, length), axis=1), axis=1, keepdims=True)
        reach = jnp.max(query_norm * key_norm) * (scale * scale)
        calm[0] = jnp.where(reach <= SAFE * SAFE, 1, 0)

    group_rows = lax.broadcasted_iota(jnp.int32, (128, length), 0) // size

    def one_head(index, blocks, safe):
        head = step * heads_per_step + index
        block = head // (128 // size)
        inner = head - block * (128 // size)
        span = blocks * 128
        around = query_t[0, pl.ds(pl.multiple_of(block * 128, 128), 128), :]
        own = jnp.where(group_rows == inner, around, 0).astype(BF)
        keys = key_rows[block, :span, :]
        values = value_ext[pl.ds(pl.multiple_of(head * ext, 16), ext), :span]
        def some(cut):
            scores = nn(keys, own[:, cut] if safe else spare[:, cut]) * scale
            if not safe:
                place = lax.broadcasted_iota(jnp.int32, scores.shape, 0)
                scores = jnp.where(place < count, scores, -1e30)
                scores = scores - jnp.max(scores, axis=0, keepdims=True)
            weight = jnp.exp2(scores).astype(BF)
            kept[0, index, :span, cut] = weight
            summed = nn(values, weight)
            turned = 1.0 / summed[size : size + 1, :]
            mixed = summed[:size] * turned
            low = mixed.astype(BF)
            rows = pl.ds(pl.multiple_of(head * size, 32), size)
            mixed_t[0, rows, cut] = low
            mixed_rest[0, rows, cut] = (mixed - low.astype(F32)).astype(BF)
            inverse[0, pl.ds(head, 1), cut] = turned

        if safe:
            some(slice(0, length))
            if blocks % 2:
                kept[0, index, span : span + 128, :] = jnp.zeros((128, length), BF)
        else:
            spare[...] = own
            lax.fori_loop(0, length // 256, lambda part, carry: some(pl.ds(pl.multiple_of(part * 256, 256), 256)), None)

    blocks_used = (count + 127) // 128
    for blocks in range(1, length // 128 + 1):

        @pl.when((calm[0] == 1) & (blocks_used == blocks))
        def _(blocks=blocks):
            for index in range(heads_per_step):
                one_head(index, blocks, True)

    @pl.when(calm[0] == 0)
    def _():
        lax.fori_loop(0, heads_per_step, lambda index, carry: one_head(index, length // 128, False), None)


def norm_parts(field):
    middle = jnp.mean(field, axis=-1, keepdims=True)
    center = field - middle
    spread = jnp.mean(center * center, axis=-1, keepdims=True)
    pull = lax.rsqrt(spread + EPS)
    return center * pull, pull


def norm_back(grad, normal, pull):
    return (grad - jnp.mean(grad, axis=-1, keepdims=True) - normal * jnp.mean(grad * normal, axis=-1, keepdims=True)) * pull


def ffn_kernel(chunk, where, tokens, mixed_t, mixed_rest, inverse, cotangent, near, *refs):
    far, refs = refs[:VIRTUAL], refs[VIRTUAL:]
    layer_out, grad_first, mixed_grad_t, center, keep, send, grad_vectors, grad_up_bias = refs[:8]
    out_sum, up_sum, down_sum, vector_sum, hidden_all, slope_all, up_weight, down_weight, out_weight, up_bias = refs[8:]
    step = pl.program_id(0)
    rows, width = tokens.shape
    inner = hidden_all.shape[1]
    size = width // HEADS
    share = width // VIRTUAL
    part = inner // VIRTUAL

    @pl.when(step == 0)
    def _():
        out_sum[...] = jnp.zeros_like(out_sum)
        up_sum[...] = jnp.zeros_like(up_sum)
        down_sum[...] = jnp.zeros_like(down_sum)
        vector_sum[...] = jnp.zeros_like(vector_sum)
        for side in range(2):
            for slot in range(VIRTUAL // 2):
                ref = far[side * (VIRTUAL // 2) + slot]
                owner = where[0] ^ (2 * slot + side)
                strip = pl.ds(pl.multiple_of(owner * share, share), share)
                down_weight[pl.ds(pl.multiple_of(owner * part, part), part), :] = ref[:part, :]
                out_weight[strip, :] = ref[part : part + share, :]
                for lane in range(inner // width):
                    cut = slice(part + share * (lane + 1), part + share * (lane + 2))
                    up_weight[strip, lane * width : (lane + 1) * width] = ref[cut, :]
        for d in range(VIRTUAL):
            up_bias[:, d * part : (d + 1) * part] = near[d, 3 * share : 3 * share + 16, :].astype(F32)[8:9]

    vectors = near_vectors(near)
    out_bias, down_bias, first_gain, first_shift, second_gain, second_shift = [vectors[k : k + 1, :] for k in range(2, 8)]
    mixed = mixed_t[0].T
    first_sum = tokens[...].astype(F32) + nn(mixed, out_weight[...]) + out_bias
    first_normal, first_pull = norm_parts(first_sum)
    first_norm = first_normal * first_gain + first_shift
    first_low = first_norm.astype(BF)
    second_sum = first_norm + down_bias
    root = math.sqrt(2.0 / math.pi)
    for start in range(0, inner, chunk):
        cut = slice(start, start + chunk)
        pre = (nn(first_low, up_weight[:, cut]) + up_bias[:, cut]).astype(BF)
        square = pre * pre
        gate = jnp.bfloat16(0.5) + jnp.bfloat16(0.5) * jnp.tanh(pre * (jnp.bfloat16(root) + jnp.bfloat16(root * 0.044715) * square))
        hidden = pre * gate
        slope_all[:, cut] = gate + hidden * (jnp.bfloat16(1.0) - gate) * (jnp.bfloat16(2.0 * root) + jnp.bfloat16(6.0 * root * 0.044715) * square)
        hidden_all[:, cut] = hidden
        second_sum = second_sum + nn(hidden, down_weight[cut, :])
    second_normal, second_pull = norm_parts(second_sum)
    layer_out[...] = (second_normal * second_gain + second_shift).astype(BF)
    wide = cotangent[...].astype(F32)
    grad_second = norm_back(wide * second_gain, second_normal, second_pull)
    ffn_grad = grad_second.astype(BF)
    ffn_grad_t = ffn_grad.T
    first_low_t = first_low.T
    ones = jnp.where(lax.broadcasted_iota(jnp.int32, (16, rows), 0) == 0, 1.0, 0.0).astype(BF)
    first_ext = jnp.concatenate([first_low_t, ones], axis=0)
    back = grad_second
    for start in range(0, inner, chunk):
        cut = slice(start, start + chunk)
        hidden_grad = nt(ffn_grad, down_weight[cut, :]).astype(BF) * slope_all[:, cut]
        down_sum[:, cut] += nn(ffn_grad_t, hidden_all[:, cut])
        up_sum[:, cut] += nn(first_ext, hidden_grad)
        back = back + nt(hidden_grad, up_weight[:, cut])
    first = norm_back(back * first_gain, first_normal, first_pull)
    grad_first[...] = first
    branch_grad = first.astype(BF)
    out_sum[...] += nn(mixed_t[0], branch_grad)
    mixed_grad = nt(out_weight[...], branch_grad).reshape(HEADS, size, rows)
    turned = inverse[0]
    scaled = (mixed_grad * turned[:, None, :]).astype(BF)
    mixed_grad_t[0] = scaled.reshape(width, rows)
    mixed_whole = mixed_t[0].astype(F32) + mixed_rest[0].astype(F32)
    center[0] = jnp.sum(scaled.astype(F32) * mixed_whole.reshape(HEADS, size, rows), axis=1)
    sums = (
        branch_grad.astype(F32), ffn_grad.astype(F32), back * first_normal, back, wide * second_normal, wide,
    )
    vector_sum[...] += jnp.concatenate(
        [jnp.zeros((2, width), F32)] + [jnp.sum(piece, axis=0, keepdims=True) for piece in sums], axis=0
    )

    @pl.when(step == pl.num_programs(0) - 1)
    def _():
        lanes = inner // width // QUARTERS
        few = share // QUARTERS
        for slot in range(VIRTUAL // 2):
            for ref, side in ((keep, where[0] % 2), (send, 1 - where[0] % 2)):
                owner = 2 * slot + side
                start = pl.multiple_of(owner * share, share)
                turned_down = down_sum[:, pl.ds(pl.multiple_of(owner * part, part), part)].astype(BF).T
                for quarter in range(QUARTERS):
                    for lane in range(lanes):
                        place = (quarter * lanes + lane) * width
                        ref[quarter, slot, lane * share : (lane + 1) * share, :] = up_sum[pl.ds(start, share), place : place + width].astype(BF)
                    low = lanes * share
                    high = low + part // QUARTERS
                    ref[quarter, slot, low:high, :] = turned_down[quarter * (part // QUARTERS) : (quarter + 1) * (part // QUARTERS)]
                    out = out_sum[pl.ds(start + quarter * few, few), :]
                    ref[quarter, slot, high:, :] = jnp.concatenate([out] * (16 // few), axis=0).astype(BF)
        for d in range(VIRTUAL):
            grad_up_bias[d : d + 1, :] = up_sum[width : width + 1, d * part : (d + 1) * part]
        grad_vectors[...] = vector_sum[...]


def backward_kernel(heads_per_step, used, kept, value_rows, key_t, query_t, mixed_grad_t, center, *refs):
    (where, lifted_t, lifted_ct, tokens_ct, early_vectors, up_bias), refs = refs[:6], refs[6:]
    query_grad_t, key_grad_t, value_grad_t, keep, send, weight_turned, grad_turned, held, arrived = refs
    steps = HEADS // heads_per_step
    unit = pl.program_id(0)
    last_unit = query_grad_t.shape[0] - 1
    image = unit // steps
    step = unit - image * steps
    width, length = query_t.shape[1:]
    size = width // HEADS
    share = width // VIRTUAL
    scale = size ** (-0.5)
    count = used[image]
    blocks_used = (count + 127) // 128
    group_rows = lax.broadcasted_iota(jnp.int32, (128, length), 0) // size
    copies = [
        pltpu.make_async_copy(source, held.at[k], arrived.at[k]) for k, source in enumerate((lifted_t, lifted_ct, tokens_ct))
    ]

    @pl.when(unit == 1)
    def _():
        for copy in copies:
            copy.start()

    def one_head(index, blocks):
        head = step * heads_per_step + index
        block = head // (128 // size)
        inner = head - block * (128 // size)
        span = blocks * 128
        head_rows = pl.ds(pl.multiple_of(head * size, 32), size)
        own_rows = slice(index * size, (index + 1) * size)
        around = mixed_grad_t[0, pl.ds(pl.multiple_of(block * 128, 128), 128), :]
        own = jnp.where(group_rows == inner, around, 0).astype(BF)
        values = value_rows[0, block, :span, :]
        keys = key_t[0, head_rows, :span]
        weight = kept[0, index, :span, :]
        weight_turned[index, :, :span] = weight.T
        pulled = nn(values, own) - center[0, pl.ds(head, 1), :]
        score_grad = (weight.astype(F32) * pulled).astype(BF)
        grad_turned[index, :, :span] = score_grad.T
        query_grad_t[unit, own_rows, :] = (nn(keys, score_grad) * scale).astype(BF)
        value_sum = nn(mixed_grad_t[0, head_rows, :], weight_turned[index, :, :span])
        key_sum = nn(query_t[0, head_rows, :], grad_turned[index, :, :span])
        valid = lax.broadcasted_iota(jnp.int32, (size, span), 1) < count
        value_grad_t[unit, own_rows, :span] = jnp.where(valid, value_sum, 0.0).astype(BF)
        key_grad_t[unit, own_rows, :span] = jnp.where(valid, key_sum * scale, 0.0).astype(BF)
        if span < length:
            value_grad_t[unit, own_rows, span:] = jnp.zeros((size, length - span), BF)
            key_grad_t[unit, own_rows, span:] = jnp.zeros((size, length - span), BF)

    for blocks in range(2, length // 128 + 1, 2):

        @pl.when((blocks_used == blocks) | (blocks_used == blocks - 1))
        def _(blocks=blocks):
            for index in range(heads_per_step):
                one_head(index, blocks)

    @pl.when(unit == last_unit)
    def _():
        for copy in copies:
            copy.wait()
        ones = jnp.ones((16, length), BF)
        sums = [None] * 3
        for one in range(held.shape[1]):
            units = slice(one * steps, (one + 1) * steps)
            turned = [ref[units].reshape(width, length) for ref in (query_grad_t, key_grad_t, value_grad_t)]
            for k in range(3):
                left = held[k, one]
                added = nt(left if k == 1 else jnp.concatenate([left, ones], axis=0), turned[k])
                sums[k] = added if sums[k] is None else sums[k] + added
        vectors = jnp.concatenate([sums[0][width : width + 1], sums[2][width : width + 1], early_vectors[2:8, :]], axis=0)
        for k in range(3):
            low = sums[k][:width].astype(BF)
            for owner in range(VIRTUAL):
                mine = where[0] % 2 == owner % 2
                piece = low[owner * share : (owner + 1) * share]

                @pl.when(mine)
                def _(owner=owner, piece=piece, k=k):
                    keep[owner // 2, k * share : (k + 1) * share, :] = piece

                @pl.when(jnp.logical_not(mine))
                def _(owner=owner, piece=piece, k=k):
                    send[owner // 2, k * share : (k + 1) * share, :] = piece

        for slot in range(VIRTUAL // 2):
            for ref, side in ((keep, where[0] % 2), (send, 1 - where[0] % 2)):
                bias = jnp.broadcast_to(up_bias[pl.ds(2 * slot + side, 1), :], (8, width))
                ref[slot, 3 * share :, :] = jnp.concatenate([vectors, bias], axis=0).astype(BF)


def finish_kernel(place, *refs):
    pieces, others, (grad_out, grad_up, grad_down, *rest) = refs[:QUARTERS], refs[:QUARTERS], refs[QUARTERS:]
    share, width = grad_out.shape
    lanes = grad_up.shape[1] // width // QUARTERS
    part = grad_down.shape[0] // QUARTERS
    few = share // QUARTERS
    early_rows = lanes * share + part + 16
    for far, ref in enumerate(pieces):
        owner = place[0] ^ far
        piece = ref[:early_rows, :].astype(F32)
        for lane in range(lanes):
            at = pl.multiple_of((owner * lanes + lane) * width, width)
            grad_up[:, pl.ds(at, width)] = piece[lane * share : (lane + 1) * share]
        grad_down[pl.ds(pl.multiple_of(owner * part, part), part), :] = piece[lanes * share : lanes * share + part]
        grad_out[pl.ds(pl.multiple_of(owner * few, few), few), :] = piece[lanes * share + part : lanes * share + part + few]
    sums = [ref[early_rows:, :].astype(F32) for ref in others]
    while len(sums) > 1:
        sums = [sums[k] + sums[k + 1] for k in range(0, len(sums), 2)]
    for k in range(3):
        rest[k][...] = sums[0][k * share : (k + 1) * share]
    vectors = sums[0][3 * share :]
    rest[11][...] = vectors[8, :]
    turned = pltpu.roll(vectors, width - place[1] * share, 1)
    for k in range(8):
        rest[3 + k][...] = turned[k, :share]


def tokens_kernel(first, rank, grad_first, near, query_grad_t, key_grad_t, value_grad_t, *refs):
    grad_tokens = refs[-1]
    image = pl.program_id(0) + first
    length = query_grad_t.shape[2]
    width = query_grad_t.shape[1]
    compact = lax.broadcasted_iota(jnp.int32, (length, length), 0)
    chosen = jnp.where(compact == rank[pl.ds(image, 1), :], 1.0, 0.0).astype(BF)
    both = nn(jnp.concatenate([key_grad_t[0], value_grad_t[0]], axis=0), chosen).astype(BF)
    weights = [near_weight(near, k) for k in range(3)]
    total_t = nn(weights[0], query_grad_t[0]) + nn(weights[1], both[:width]) + nn(weights[2], both[width:])
    grad_tokens[0] = grad_first[0] + total_t.T


def params(mebibytes, *semantics):
    return pltpu.CompilerParams(dimension_semantics=semantics, vmem_limit_bytes=mebibytes << 20)


def cost(microseconds):
    return pl.CostEstimate(flops=int(microseconds * 1.0e9), bytes_accessed=1 << 20, transcendentals=0)


def whole(shape):
    return pl.BlockSpec(shape, lambda *_: (0,) * len(shape))


def per_image(shape):
    return pl.BlockSpec((1,) + shape, lambda i, *_: (i,) + (0,) * len(shape))


def scalars():
    return pl.BlockSpec(memory_space=SMEM)


def shaped(shape, dtype):
    return jax.ShapeDtypeStruct(shape, dtype)


def resident(shape, dtype):
    return pltpu.VMEM(shape, dtype)


def stored(shape, dtype):
    return pltpu.HBM(shape, dtype)


def near_by(*arrays):
    return [pltpu.with_memory_space_constraint(array, pltpu.VMEM) for array in arrays]


def far_off(*arrays):
    return [pltpu.with_memory_space_constraint(array, pltpu.HBM) for array in arrays]


def exchange_dp(field, dp):
    return lax.all_to_all(jnp.broadcast_to(field, (dp,) + field.shape), "dp", 0, 0, tiled=True)


def same_core(zero):
    return [[k for k in range(zero) if k % 2 == side] for side in range(2)]


def swap_cores(send, zero):
    return lax.ppermute(send, "zero", [(k, k ^ 1) for k in range(zero)])


def by_owner(keep, send):
    return jnp.stack([keep, send], axis=1).reshape((VIRTUAL,) + keep.shape[1:])


def body(
    tokens, counts, key_mask, rotation, token_order, query_weight, key_weight, value_weight, out_weight, up_weight,
    down_weight, query_bias, value_bias, out_bias, up_bias, down_bias, first_gain, first_shift, second_gain,
    second_shift, cotangent, *, zero, dp,
):
    images, length, width = tokens.shape
    rows = images * length
    inner = up_weight.shape[1]
    share = width // zero
    inner_share = inner // zero
    direct = zero == VIRTUAL and dp == QUARTERS
    heads_per_step = 2
    steps = HEADS // heads_per_step
    me = lax.axis_index("zero")
    spot = (me if direct else me * 0).astype(jnp.int32).reshape(1)

    small = [query_bias, value_bias, out_bias, down_bias, first_gain, first_shift, second_gain, second_shift]
    near_rows = 3 * (width // VIRTUAL) + 16
    far_rows = (2 * inner + width) // VIRTUAL
    if direct:
        near = pl.pallas_call(
            pack_kernel,
            in_specs=[scalars()] + [pl.BlockSpec(memory_space=pltpu.VMEM)] * 12,
            out_shape=shaped((zero, near_rows, width), BF),
            scratch_shapes=[pltpu.VMEM((8, share), F32)],
            name="pack",
        )(me.astype(jnp.int32).reshape(1), query_weight, key_weight, value_weight, *small, up_bias)
        near = lax.all_to_all(near, "zero", 0, 0, tiled=True)
    else:
        gather = functools.partial(lax.all_gather, axis_name="zero", axis=0, tiled=True)
        shards = [gather(w).reshape(VIRTUAL, -1, width) for w in (query_weight, key_weight, value_weight)]
        vectors = jnp.zeros((VIRTUAL, 8, width), BF).at[0].set(jnp.stack([gather(v) for v in small]))
        biases = jnp.broadcast_to(gather(up_bias).reshape(VIRTUAL, 1, inner // VIRTUAL), (VIRTUAL, 8, inner // VIRTUAL))
        near = jnp.concatenate(shards + [vectors, biases], axis=1)
        lanes = gather(up_weight).reshape(VIRTUAL, width // VIRTUAL, inner // width, width).transpose(0, 2, 1, 3)
        shards = [gather(w).reshape(VIRTUAL, -1, width) for w in (down_weight, out_weight)]
        far = jnp.concatenate(shards + [lanes.reshape(VIRTUAL, -1, width)], axis=1)
        far = [far[2 * slot + side] for side in range(2) for slot in range(VIRTUAL // 2)]

    table = jnp.asarray(position_table(GRID, width))
    turned = stored((images, width, length), BF)
    bundle = [shaped((far_rows, width), BF)] if direct else []
    lifted_t, lifted_ct, tokens_ct, rank, used, *mine = pl.pallas_call(
        prep_kernel,
        grid=(images,),
        in_specs=[
            scalars(), scalars(), per_image((length, width)), whole((images, length)), whole((images, length)),
            whole(table.shape), whole(out_weight.shape), whole(down_weight.shape), whole(up_weight.shape),
        ],
        out_specs=[per_image((width, length))] * 3 + [whole((images, length)), scalars()] + [whole(b.shape) for b in bundle],
        out_shape=[turned] * 3 + [stored((images, length), jnp.int32), shaped((images,), jnp.int32)] + bundle,
        compiler_params=params(40, "arbitrary"),
        name="prep",
    )(counts, rotation, *far_off(tokens, key_mask, token_order, table, out_weight, down_weight, up_weight))
    if direct:
        mine = mine + [lax.ppermute(mine[0], "zero", [(k, k ^ (2 * step)) for k in range(zero)]) for step in range(1, zero // 2)]

    head_block = pl.BlockSpec((1, heads_per_step, length, length), lambda i, s: (i, s, 0, 0))
    kept, mixed_t, mixed_rest, inverse, query_t, key_t, value_rows = pl.pallas_call(
        functools.partial(forward_kernel, heads_per_step),
        grid=(images, steps),
        in_specs=[scalars()] + [per_image((width, length))] * 3 + [whole(near.shape)],
        out_specs=[
            head_block, per_image((width, length)), per_image((width, length)), per_image((HEADS, length)), per_image((width, length)),
            per_image((width, length)), per_image((width // 128, length, 128)),
        ],
        out_shape=[
            stored((images, HEADS, length, length), BF), turned, turned, stored((images, HEADS, length), F32), turned, turned,
            stored((images, width // 128, length, 128), BF),
        ],
        scratch_shapes=[
            pltpu.VMEM((width // 128, length, 128), BF),
            pltpu.VMEM((width + 16 * HEADS, length), BF),
            pltpu.VMEM((128, length), BF),
            pltpu.SMEM((1,), jnp.int32),
        ],
        compiler_params=params(30, "arbitrary", "arbitrary"),
        cost_estimate=cost(22),
        name="attend_forward",
    )(used, *far_off(lifted_t, lifted_ct, tokens_ct), *near_by(near))

    if direct:
        mine, mixed_t = lax.optimization_barrier((mine, mixed_t))
        far = mine + [swap_cores(piece, zero) for piece in mine]
    block = length
    per = length // block
    row_block = pl.BlockSpec((block, width), lambda s: (s, 0))

    def turned_block(height):
        return pl.BlockSpec((1, height, block), lambda s: (s // per, 0, s % per))

    early_rows = 2 * inner // VIRTUAL // QUARTERS + 16
    half = resident((QUARTERS, VIRTUAL // 2, early_rows, width), BF)
    layer_out, grad_first, mixed_grad_t, center, keep, send, grad_vectors, grad_up_bias = pl.pallas_call(
        functools.partial(ffn_kernel, 256),
        grid=(rows // block,),
        in_specs=[
            scalars(), row_block, turned_block(width), turned_block(width), turned_block(HEADS), row_block, whole(near.shape),
        ]
        + [whole(piece.shape) for piece in far],
        out_specs=[
            row_block, row_block, turned_block(width), turned_block(HEADS), whole(half.shape), whole(half.shape),
            whole((8, width)), whole((VIRTUAL, inner // VIRTUAL)),
        ],
        out_shape=[
            stored((rows, width), BF), stored((rows, width), F32), turned, stored((images, HEADS, length), F32),
            half, half, shaped((8, width), F32), shaped((VIRTUAL, inner // VIRTUAL), F32),
        ],
        scratch_shapes=[
            pltpu.VMEM((width, width), F32), pltpu.VMEM((width + 16, inner), F32), pltpu.VMEM((width, inner), F32),
            pltpu.VMEM((8, width), F32), pltpu.VMEM((block, inner), BF), pltpu.VMEM((block, inner), BF),
            pltpu.VMEM((width, inner), BF), pltpu.VMEM((inner, width), BF), pltpu.VMEM((width, width), BF),
            pltpu.VMEM((1, inner), F32),
        ],
        compiler_params=params(50, "arbitrary"),
        cost_estimate=cost(27),
        name="feed_forward",
    )(
        spot, *far_off(tokens.reshape(rows, width)), *far_off(mixed_t, mixed_rest, inverse),
        *far_off(cotangent.reshape(rows, width), near), *near_by(*far),
    )

    units = images * steps
    unit_shape = (heads_per_step * (width // HEADS), length)

    def attend_backward(center):
        def unit_block(shape, index):
            return pl.BlockSpec((1,) + shape, index)

        image = lambda u: (u // steps, 0, 0)
        out = resident((units,) + unit_shape, BF)
        late_half = stored((VIRTUAL // 2, near_rows, width), BF)
        return pl.pallas_call(
            functools.partial(backward_kernel, heads_per_step),
            grid=(units,),
            in_specs=[
                scalars(),
                unit_block((heads_per_step, length, length), lambda u: (u // steps, u % steps, 0, 0)),
                unit_block((width // 128, length, 128), lambda u: (u // steps, 0, 0, 0)),
            ]
            + [unit_block((width, length), image)] * 3
            + [unit_block((HEADS, length), image), scalars()]
            + [pl.BlockSpec(memory_space=pl.ANY)] * 3
            + [whole((8, width)), whole((VIRTUAL, inner // VIRTUAL))],
            out_specs=[whole(out.shape)] * 3 + [whole(late_half.shape)] * 2,
            out_shape=[out] * 3 + [late_half] * 2,
            scratch_shapes=[pltpu.VMEM((heads_per_step, length, length), BF)] * 2
            + [pltpu.VMEM((3, images, width, length), BF), pltpu.SemaphoreType.DMA((3,))],
            compiler_params=params(40, "arbitrary"),
            cost_estimate=cost(1),
            name="attend_backward",
        )(
            used, *far_off(kept, value_rows, key_t, query_t, mixed_grad_t, center),
            spot, *far_off(lifted_t, lifted_ct, tokens_ct), grad_vectors, grad_up_bias,
        )

    if direct:
        came = swap_cores(send, zero)
        merged = (keep.astype(F32) + came.astype(F32)).astype(BF).reshape(zero // 2 * dp, early_rows, width)
        groups = [[d * zero + 2 * q + side for d in range(dp) for q in range(zero // 2)] for side in range(2)]
        merged, center = lax.optimization_barrier((merged, center))
        early = lax.all_to_all(merged, ("dp", "zero"), 0, 0, tiled=True, axis_index_groups=groups)
        *grads, keep, send = attend_backward(center)
        early, send = lax.optimization_barrier((early, send))
        early = jnp.sum(early.astype(F32), axis=0).astype(BF)
    else:
        lanes = inner // width
        strip = width // VIRTUAL
        cuts = (lanes // QUARTERS * strip, (lanes // QUARTERS * strip) + inner // VIRTUAL // QUARTERS)
        halves = jnp.stack([keep, send], axis=2).reshape((QUARTERS, VIRTUAL) + keep.shape[2:])
        grad_up = halves[:, :, : cuts[0]].reshape(QUARTERS, VIRTUAL, lanes // QUARTERS, strip, width)
        grad_up = grad_up.transpose(1, 3, 0, 2, 4).reshape(zero, share, lanes, width).transpose(0, 2, 1, 3)
        grad_down = halves[:, :, cuts[0] : cuts[1]].transpose(1, 0, 2, 3).reshape(zero, inner_share, width)
        grad_out = halves[:, :, cuts[1] : cuts[1] + strip // QUARTERS].transpose(1, 0, 2, 3).reshape(zero, share, width)
        early = jnp.concatenate([grad_out, grad_up.reshape(zero, share * lanes, width), grad_down], axis=1)
        early = jnp.sum(lax.all_to_all(early, "zero", 0, 0, tiled=True).astype(F32), axis=0).astype(BF)
        early = exchange_dp(early, dp)
        *grads, keep, send = attend_backward(center)
    query_grad_t, key_grad_t, value_grad_t = [g.reshape(images, width, length) for g in grads]

    def token_grads(first, last, rank, before):
        def own(shape):
            return pl.BlockSpec((1,) + shape, lambda i: (i + first, 0, 0))

        return pl.pallas_call(
            functools.partial(tokens_kernel, first),
            grid=(last - first,),
            in_specs=[whole((images, length)), own((length, width)), whole(near.shape)]
            + [own((width, length))] * 3
            + [pl.BlockSpec(memory_space=pl.ANY)] * len(before),
            out_specs=own((length, width)),
            out_shape=stored((images, length, width), F32),
            input_output_aliases={6: 0} if before else {},
            compiler_params=params(24, "arbitrary"),
            cost_estimate=cost(1),
            name="token_grads",
        )(
            *far_off(rank, grad_first.reshape(images, length, width), near),
            *near_by(query_grad_t, key_grad_t, value_grad_t),
            *far_off(*before),
        )

    if direct:
        came = swap_cores(send, zero)
        early, came = lax.optimization_barrier((early, came))
        merged = (keep.astype(F32) + came.astype(F32)).astype(BF)
        late = lax.all_to_all(merged, "zero", 0, 0, tiled=True, axis_index_groups=same_core(zero))
        grad_tokens = token_grads(0, images // 2, rank, ())
        late, grad_tokens = lax.optimization_barrier((late, grad_tokens))
        late = jnp.sum(late.astype(F32), axis=0).astype(BF)
        tail = jnp.concatenate([early, late], axis=0)
        tail, rank = lax.optimization_barrier((tail, rank))
        tail = [tail] + [lax.ppermute(tail, "dp", [(k, k ^ step) for k in range(dp)]) for step in range(1, dp)]
        grad_tokens = token_grads(images // 2, images, rank, (grad_tokens,))
    else:
        halves = by_owner(keep, send)
        strip = width // VIRTUAL
        three = halves[:, : 3 * strip].reshape(VIRTUAL, 3, strip, width).transpose(1, 0, 2, 3).reshape(3, zero, share, width)
        three = three.transpose(1, 0, 2, 3).reshape(zero, 3 * share, width)
        vectors = halves[:, 3 * strip : 3 * strip + 8].reshape(VIRTUAL, 8, width)[0]
        vectors = vectors.reshape(8, zero, share).transpose(1, 0, 2)
        vectors = jnp.pad(vectors, ((0, 0), (0, 0), (0, width - share)))
        bias = jnp.pad(halves[:, -1].reshape(zero, 1, inner_share), ((0, 0), (0, 7), (0, width - inner_share)))
        late = jnp.concatenate([three, vectors, bias], axis=1)
        late = jnp.sum(lax.all_to_all(late, "zero", 0, 0, tiled=True).astype(F32), axis=0).astype(BF)
        grad_tokens = token_grads(0, images, rank, ())
        late = jnp.sum(exchange_dp(late, dp).astype(F32), axis=0)

    if direct:
        grad_out_own, grad_up_own, grad_down_own, *three = pl.pallas_call(
            finish_kernel,
            in_specs=[scalars()] + [pl.BlockSpec(memory_space=pltpu.VMEM)] * dp,
            out_shape=[stored((share, width), F32), stored((share, inner), F32), stored((inner_share, width), F32)]
            + [stored((share, width), F32)] * 3
            + [shaped((share,), F32)] * 8
            + [shaped((inner_share,), F32)],
            compiler_params=pltpu.CompilerParams(vmem_limit_bytes=16 << 20),
            name="finish",
        )(jnp.stack([lax.axis_index("dp"), me]).astype(jnp.int32), *tail)
        *cuts, up_bias_own = three[3:]
    else:
        lanes = inner // width
        total = jnp.sum(early.astype(F32), axis=0)
        grad_out_own = total[:share]
        grad_up_own = total[share : share * (lanes + 1)].reshape(lanes, share, width).transpose(1, 0, 2).reshape(share, inner)
        grad_down_own = total[share * (lanes + 1) :]
        three = late[: 3 * share].reshape(3, share, width)
        vectors = late[3 * share :]
        cuts = [vectors[k, :share] for k in range(8)]
        up_bias_own = vectors[8, :inner_share]
    return (
        layer_out.reshape(images, length, width),
        grad_tokens,
        three[0],
        three[1],
        three[2],
        grad_out_own,
        grad_up_own,
        grad_down_own,
        cuts[0],
        cuts[1],
        cuts[2],
        up_bias_own,
        cuts[3],
        cuts[4],
        cuts[5],
        cuts[6],
        cuts[7],
    )


def solution(mesh):
    batch = P(("dp", "zero"))
    wide = P(("dp", "zero"), None, None)
    flat = P(("dp", "zero"), None)
    matrix = P("zero", None)
    vector = P("zero")
    in_specs = (wide, batch, flat, batch, flat) + (matrix,) * 6 + (vector,) * 9 + (wide,)
    out_specs = (wide, wide) + (matrix,) * 6 + (vector,) * 9
    run = functools.partial(body, zero=mesh.shape["zero"], dp=mesh.shape["dp"])
    return jax.shard_map(run, mesh=mesh, in_specs=in_specs, out_specs=out_specs, check_vma=False)
```
